32 devices in a mesh: batch: 4 (over y, x), seq: 8 (over z, core).
Axes of the slice: x: 2, y: 2, z: 4, core: 2. Of those that a mesh axis runs over, the one named last changes fastest.
Arguments:
- tokens: bfloat16 [4, 2048, 2048], P('batch', 'seq'), may hold values from -6 to 6
- segments: int32 [4, 2048], P('batch', 'seq'), may hold values from 0 to 10, as said below
- cotangent: bfloat16 [4, 2048, 2048], P('batch', 'seq'), may hold values from -6 to 6
- norm_gain: bfloat16 [2048], P(('batch', 'seq')), may hold values from 0.099609375 to 1.8984375
- gating_weight: bfloat16 [2048, 3072], P(('batch', 'seq')), may hold values from -0.125 to 0.125
- input_weight: bfloat16 [2048, 3072], P(('batch', 'seq')), may hold values from -0.125 to 0.125
- state_weight: bfloat16 [2048, 512], P(('batch', 'seq')), may hold values from -0.125 to 0.125
- step_weight: bfloat16 [2048, 48], P(('batch', 'seq')), may hold values from -0.125 to 0.125
- conv_weight: bfloat16 [4, 3584], P(None, ('batch', 'seq')), may hold values from -3 to 3
- conv_bias: bfloat16 [3584], P(('batch', 'seq')), may hold values from -3 to 3
- step_bias: bfloat16 [48], replicated, may hold values from -7 to -2.296875
- decay_log: bfloat16 [48], replicated, may hold values from 0 to 2.765625
- skip_gain: bfloat16 [48], replicated, may hold values from 0.5 to 1.5
- ssm_gain: bfloat16 [3072], P(('batch', 'seq')), may hold values from 0.099609375 to 1.8984375
- out_weight: bfloat16 [3072, 2048], P(('batch', 'seq')), may hold values from -0.109375 to 0.109375
- query_weight: bfloat16 [2048, 1024], P(('batch', 'seq')), may hold values from -0.125 to 0.125
- keyval_weight: bfloat16 [2048, 512], P(('batch', 'seq')), may hold values from -0.125 to 0.125
- context_weight: bfloat16 [1024, 2048], P(('batch', 'seq')), may hold values from -3 to 3
- mlp_gain: bfloat16 [2048], P(('batch', 'seq')), may hold values from 0.099609375 to 1.8984375
- gate_weight: bfloat16 [2048, 4096], P(('batch', 'seq')), may hold values from -0.125 to 0.125
- up_weight: bfloat16 [2048, 4096], P(('batch', 'seq')), may hold values from -0.125 to 0.125
- down_weight: bfloat16 [4096, 2048], P(('batch', 'seq')), may hold values from -0.09375 to 0.09375
Outputs:
- layer_out: bfloat16 [4, 2048, 2048], P('batch', 'seq')
- grad_tokens: bfloat16 [4, 2048, 2048], P('batch', 'seq')
- grad_norm_gain: float32 [2048], P(('batch', 'seq'))
- grad_gating_weight: float32 [2048, 3072], P(('batch', 'seq'))
- grad_input_weight: float32 [2048, 3072], P(('batch', 'seq'))
- grad_state_weight: float32 [2048, 512], P(('batch', 'seq'))
- grad_step_weight: float32 [2048, 48], P(('batch', 'seq'))
- grad_conv_weight: float32 [4, 3584], P(None, ('batch', 'seq'))
- grad_conv_bias: float32 [3584], P(('batch', 'seq'))
- grad_step_bias: float32 [48], replicated
- grad_decay_log: float32 [48], replicated
- grad_skip_gain: float32 [48], replicated
- grad_ssm_gain: float32 [3072], P(('batch', 'seq'))
- grad_out_weight: float32 [3072, 2048], P(('batch', 'seq'))
- grad_query_weight: float32 [2048, 1024], P(('batch', 'seq'))
- grad_keyval_weight: float32 [2048, 512], P(('batch', 'seq'))
- grad_context_weight: float32 [1024, 2048], P(('batch', 'seq'))
- grad_mlp_gain: float32 [2048], P(('batch', 'seq'))
- grad_gate_weight: float32 [2048, 4096], P(('batch', 'seq'))
- grad_up_weight: float32 [2048, 4096], P(('batch', 'seq'))
- grad_down_weight: float32 [4096, 2048], P(('batch', 'seq'))
The draws below stay inside these ranges and needn't reach their ends.
Inputs may be any that keep to these rules, and one draw needn't show every extreme that they name: `segments`: along each sequence the segment numbers start at 0 and rise by one where a new document begins; every document has at most 2000 tokens, and every one but the last of its sequence at least 200. In one sequence every document but the last has exactly 200 tokens.
All inputs are finite; a program needn't handle non-finite values.
Results may differ from the reference program's by a relative error of at most 0.03.
Values may be sent and summed in bfloat16 or wider, within the bound.
No kernel may reach another device: no remote copies, remote signals or barrier semaphores. Data moves between devices by JAX's collectives and lax.ppermute only.
A program may use at most 448 MiB of HBM per device.

```python
import math
import jax
import jax.numpy as jnp
from jax import lax

D = 2048
HEADS = 48
SSM_HEAD = 64
STATE = 256
CONV = 4
QHEADS = 8
KVHEADS = 2
ATT_HEAD = 128
FF = 4096
TOK_DEV = 256
DOC_MIN = 200
DOC_MAX = 2000
SSM_WIDTH = 3072
CHANNELS = 3584
SEQS = 4
LENGTH = 2048


def draw_segments(key, part):
    key = jax.random.fold_in(key, 7)
    doc_count = LENGTH // DOC_MIN + 1
    length_key = jax.random.fold_in(key, 1)
    pick_key = jax.random.fold_in(key, 2)
    lengths = jax.random.randint(length_key, (SEQS, doc_count), DOC_MIN, DOC_MAX + 1)
    chosen = jax.random.randint(pick_key, (), 0, SEQS)
    rows = jnp.arange(SEQS, dtype=jnp.int32)[:, None]
    lengths = jnp.where(rows == chosen, DOC_MIN, lengths)
    bounds = jnp.cumsum(lengths, axis=1)
    places = jnp.arange(LENGTH, dtype=jnp.int32)
    return jnp.sum((bounds[:, None, :] <= places[None, :, None]).astype(jnp.int32), axis=2)


def level_of(own_key, extent, cuts, low, top_value):
    def one(position, parts):
        heights = jax.random.uniform(jax.random.fold_in(jax.random.fold_in(own_key, 6), position), (parts,), jnp.float32, low / len(cuts), top_value / len(cuts))
        return jnp.repeat(jnp.exp(heights), extent[position] // parts).reshape((-1,) + (1,) * (len(extent) - position - 1))

    factor_of = one(*cuts[0])
    for cut in cuts[1:]:
        factor_of = factor_of * one(*cut)
    return factor_of


def noise(key, dims, deviation, most, shards=(), held_as=jnp.bfloat16):
    values = deviation * jax.random.normal(key, dims, jnp.float32)
    if shards:
        values = values * level_of(key, dims, shards, -0.22, 0.18)
    return jnp.clip(values, -most, most).astype(held_as)


def setup_inputs(seed: int = 0) -> dict:
    key_list = jax.random.split(jax.random.key(seed), 23)
    tokens = noise(key_list[0], (SEQS, LENGTH, D), 1.0, 6.0, ((0, 4), (1, 8)))
    segments = draw_segments(jax.random.fold_in(key_list[22], 71), 0)
    cotangent = noise(key_list[2], (SEQS, LENGTH, D), 1.0, 6.0, ((0, 4), (1, 8)))
    norm_gain = jnp.clip(1.0 + 0.18 * jax.random.normal(key_list[3], (D,), jnp.float32), 0.099609375, 1.8984375).astype(jnp.bfloat16)
    gating_weight = noise(key_list[4], (D, SSM_WIDTH), D ** -0.5, 0.125, ((0, 32),))
    input_weight = noise(key_list[5], (D, SSM_WIDTH), D ** -0.5, 0.125, ((0, 32),))
    state_weight = noise(key_list[6], (D, 2 * STATE), D ** -0.5, 0.125, ((0, 32),))
    step_weight = noise(key_list[7], (D, HEADS), D ** -0.5, 0.125, ((0, 32),))
    conv_weight = noise(key_list[8], (CONV, CHANNELS), CONV ** -0.5, 3.0, ((1, 32),))
    conv_bias = noise(key_list[9], (CHANNELS,), 0.5, 3.0, ((0, 32),))
    step_bias = jnp.clip(jax.random.uniform(key_list[10], (HEADS,), jnp.float32, -7.0, -2.296875), -7.0, -2.296875).astype(jnp.bfloat16)
    decay_log = jnp.clip(jax.random.uniform(key_list[11], (HEADS,), jnp.float32, 0.0, 2.765625), 0.0, 2.765625).astype(jnp.bfloat16)
    skip_gain = jnp.clip(jax.random.uniform(key_list[12], (HEADS,), jnp.float32, 0.5, 1.5), 0.5, 1.5).astype(jnp.bfloat16)
    ssm_gain = jnp.clip(1.0 + 0.18 * jax.random.normal(key_list[13], (SSM_WIDTH,), jnp.float32), 0.099609375, 1.8984375).astype(jnp.bfloat16)
    out_weight = noise(key_list[14], (SSM_WIDTH, D), SSM_WIDTH ** -0.5, 0.109375, ((0, 32),))
    query_weight = noise(key_list[15], (D, QHEADS * ATT_HEAD), D ** -0.5, 0.125, ((0, 32),))
    keyval_weight = noise(key_list[16], (D, 2 * KVHEADS * ATT_HEAD), D ** -0.5, 0.125, ((0, 32),))
    context_weight = noise(key_list[17], (QHEADS * ATT_HEAD, D), 4 ** -0.5, 3.0, ((0, 32),))
    mlp_gain = jnp.clip(1.0 + 0.18 * jax.random.normal(key_list[18], (D,), jnp.float32), 0.099609375, 1.8984375).astype(jnp.bfloat16)
    gate_weight = noise(key_list[19], (D, FF), D ** -0.5, 0.125, ((0, 32),))
    up_weight = noise(key_list[20], (D, FF), D ** -0.5, 0.125, ((0, 32),))
    down_weight = noise(key_list[21], (FF, D), FF ** -0.5, 0.09375, ((0, 32),))
    return dict(tokens=tokens, segments=segments, cotangent=cotangent, norm_gain=norm_gain, gating_weight=gating_weight, input_weight=input_weight, state_weight=state_weight, step_weight=step_weight, conv_weight=conv_weight, conv_bias=conv_bias, step_bias=step_bias, decay_log=decay_log, skip_gain=skip_gain, ssm_gain=ssm_gain, out_weight=out_weight, query_weight=query_weight, keyval_weight=keyval_weight, context_weight=context_weight, mlp_gain=mlp_gain, gate_weight=gate_weight, up_weight=up_weight, down_weight=down_weight)


HIGH = lax.Precision.HIGHEST
EPSILON = 1e-05
ROPE_BASE = 10000.0
NEG_BIG = -1e+30

@jax.custom_vjp
def low(v):
    return lax.optimization_barrier(v.astype(jnp.bfloat16)).astype(jnp.float32)

@jax.custom_vjp
def low_back(v):
    return v

def low_keep(v):
    return (low(v), None)

def low_pass(kept, grad):
    return (grad,)

def back_keep(v):
    return (v, None)

def back_low(kept, grad):
    return (low(grad),)
low.defvjp(low_keep, low_pass)
low_back.defvjp(back_keep, back_low)

def matmul(left, right):
    return jnp.dot(left, right, precision=HIGH, preferred_element_type=jnp.float32)

def rms_scale(values):
    return lax.rsqrt(lax.optimization_barrier(jnp.mean(values * values, axis=-1, keepdims=True)) + EPSILON)

def rotate(values, places, direction):
    full_width = values.shape[-1]
    half_width = full_width // 2
    frequency = jnp.exp(jnp.arange(half_width, dtype=jnp.float32) * (-2.0 * math.log(ROPE_BASE) / full_width))
    angles = places.astype(jnp.float32)[:, None] * frequency[None, :]
    cosine = jnp.cos(angles)[:, None, :]
    sine_part = direction * jnp.sin(angles)[:, None, :]
    first_half = values[..., :half_width]
    second_half = values[..., half_width:]
    return jnp.concatenate([first_half * cosine - second_half * sine_part, second_half * cosine + first_half * sine_part], axis=-1)

def conv_mix(mixed_in, seg_ids, conv_weight, conv_bias):
    length = mixed_in.shape[0]
    padded = jnp.concatenate([jnp.zeros((CONV - 1, mixed_in.shape[1]), jnp.float32), mixed_in], axis=0)
    seg_padded = jnp.concatenate([jnp.full((CONV - 1,), -1, jnp.int32), seg_ids])
    summed = conv_bias[None, :]
    for offset in range(CONV):
        matches = (seg_padded[offset:offset + length] == seg_ids).astype(jnp.float32)[:, None]
        summed = summed + conv_weight[offset][None, :] * padded[offset:offset + length] * matches
    return summed

def span_step(carried_in, pieces, decay_rate):
    ssm_state, prev_seg = carried_in
    ssm_part, b_part, c_part, step_part, seg_part = pieces
    length = seg_part.shape[0]
    cumulative = jnp.cumsum(step_part * decay_rate[None, :], axis=0)
    index_col = jnp.arange(length)
    allowed = (seg_part[:, None] == seg_part[None, :]) & (index_col[:, None] >= index_col[None, :])
    spread = jnp.where(allowed[None], cumulative.T[:, :, None] - cumulative.T[:, None, :], 0.0)
    decays = jnp.where(allowed[None], jnp.exp(spread), 0.0)
    inner_prod = low_back(matmul(c_part, b_part.T))
    mix_weights = low(inner_prod[None] * decays * step_part.T[:, None, :])
    within = jnp.einsum('hts,shp->thp', mix_weights, ssm_part, precision=HIGH)
    carried = (seg_part == prev_seg).astype(jnp.float32)
    entry_decay = jnp.exp(cumulative) * carried[:, None]
    across = jnp.einsum('tn,hpn->thp', c_part, low(ssm_state), precision=HIGH) * entry_decay[:, :, None]
    ending = (seg_part == seg_part[length - 1]).astype(jnp.float32)
    tail_weight = jnp.exp(cumulative[length - 1][None, :] - cumulative) * ending[:, None] * step_part
    weighted = low(ssm_part * tail_weight[:, :, None])
    local_state = jnp.einsum('shp,sn->hpn', weighted, b_part, precision=HIGH)
    passing = jnp.exp(cumulative[length - 1]) * carried[length - 1]
    new_state = passing[:, None, None] * ssm_state + local_state
    return ((new_state, seg_part[length - 1]), within + across)

def sequence_forward(inputs, seg_ids, params):
    norm_gain, gating_weight, input_weight, state_weight, step_weight, conv_weight, conv_bias, step_bias, decay_log, skip_gain, ssm_gain, out_weight, query_weight, keyval_weight, context_weight, mlp_gain, gate_weight, up_weight, down_weight = params
    length = inputs.shape[0]
    ssm_width = HEADS * SSM_HEAD
    kv_width = KVHEADS * ATT_HEAD
    groups = QHEADS // KVHEADS
    score_scale = 1.0 / math.sqrt(ATT_HEAD)
    normed = low(inputs * rms_scale(inputs) * norm_gain)
    gating = low_back(matmul(normed, gating_weight))
    mixed_in = low(low_back(jnp.concatenate([matmul(normed, input_weight), matmul(normed, state_weight)], axis=1)))
    step_raw = low_back(matmul(normed, step_weight))
    activated = low(jax.nn.silu(conv_mix(mixed_in, seg_ids, conv_weight, conv_bias)))
    ssm_in = activated[:, :ssm_width].reshape(length, HEADS, SSM_HEAD)
    b_mat = activated[:, ssm_width:ssm_width + STATE]
    c_mat = activated[:, ssm_width + STATE:]
    step_size = jax.nn.softplus(step_raw + step_bias[None, :])
    decay_rate = -jnp.exp(decay_log)
    blocks = length // TOK_DEV

    def scan_step(carried_in, pieces):
        return span_step(carried_in, pieces, decay_rate)
    initial = (jnp.zeros((HEADS, SSM_HEAD, STATE), jnp.float32), jnp.int32(-1))
    _, mixed_out = lax.scan(jax.checkpoint(scan_step), initial, (ssm_in.reshape(blocks, TOK_DEV, HEADS, SSM_HEAD), b_mat.reshape(blocks, TOK_DEV, STATE), c_mat.reshape(blocks, TOK_DEV, STATE), step_size.reshape(blocks, TOK_DEV, HEADS), seg_ids.reshape(blocks, TOK_DEV)))
    ssm_out = low_back(mixed_out.reshape(length, HEADS, SSM_HEAD) + skip_gain[None, :, None] * ssm_in)
    ssm_out = ssm_out.reshape(length, ssm_width)
    gated = ssm_out * jax.nn.silu(gating)
    mamba_in = low(gated * rms_scale(gated) * ssm_gain)
    mamba_out = matmul(mamba_in, out_weight)
    places = jnp.arange(length, dtype=jnp.int32)
    queries = low(rotate(low_back(matmul(normed, query_weight)).reshape(length, QHEADS, ATT_HEAD), places, 1.0))
    keyval = low_back(matmul(normed, keyval_weight))
    key_rot = low(rotate(keyval[:, :kv_width].reshape(length, KVHEADS, ATT_HEAD), places, 1.0))
    values = low(keyval[:, kv_width:].reshape(length, KVHEADS, ATT_HEAD))
    rows_block = min(512, length)
    query_blocks = queries.reshape(length // rows_block, rows_block, KVHEADS, groups, ATT_HEAD)

    def attend(pieces):
        query_part, place_part, seg_part = pieces
        scores = low_back(jnp.einsum('tkgd,skd->kgts', query_part, key_rot, precision=HIGH) * score_scale)
        allowed = (seg_part[:, None] == seg_ids[None, :]) & (place_part[:, None] >= places[None, :])
        masked = jnp.where(allowed, scores, NEG_BIG)
        highest = lax.optimization_barrier(jnp.max(masked, axis=-1, keepdims=True))
        exponent = jnp.where(allowed, jnp.exp(masked - highest), 0.0)
        probability = low(exponent / lax.optimization_barrier(jnp.sum(exponent, axis=-1, keepdims=True)))
        return jnp.einsum('kgts,skd->tkgd', probability, values, precision=HIGH)
    context = lax.map(jax.checkpoint(attend), (query_blocks, places.reshape(-1, rows_block), seg_ids.reshape(-1, rows_block)))
    context = low(low_back(context.reshape(length, QHEADS * ATT_HEAD)))
    attn_out = matmul(context, context_weight)
    hidden = inputs + low_back(mamba_out + attn_out)
    normed_two = low(hidden * rms_scale(hidden) * mlp_gain)
    gate_pre = low_back(matmul(normed_two, gate_weight))
    up_pre = low_back(matmul(normed_two, up_weight))
    activation = low(jax.nn.silu(gate_pre) * up_pre)
    return hidden + low_back(matmul(activation, down_weight))

def reference(tokens, segments, cotangent, norm_gain, gating_weight, input_weight, state_weight, step_weight, conv_weight, conv_bias, step_bias, decay_log, skip_gain, ssm_gain, out_weight, query_weight, keyval_weight, context_weight, mlp_gain, gate_weight, up_weight, down_weight):
    params = tuple((weight_arg.astype(jnp.float32) for weight_arg in (norm_gain, gating_weight, input_weight, state_weight, step_weight, conv_weight, conv_bias, step_bias, decay_log, skip_gain, ssm_gain, out_weight, query_weight, keyval_weight, context_weight, mlp_gain, gate_weight, up_weight, down_weight)))

    def forward(inputs, *weights):

        def one_sequence(seq_pair):
            return sequence_forward(seq_pair[0], seq_pair[1], weights)
        return lax.map(jax.checkpoint(one_sequence), (inputs, segments))
    result, pullback = jax.vjp(forward, tokens.astype(jnp.float32), *params)
    gradients = pullback(cotangent.astype(jnp.float32))
    return (result.astype(jnp.bfloat16), gradients[0].astype(jnp.bfloat16), gradients[1], gradients[2], gradients[3], gradients[4], gradients[5], gradients[6], gradients[7], gradients[8], gradients[9], gradients[10], gradients[11], gradients[12], gradients[13], gradients[14], gradients[15], gradients[16], gradients[17], gradients[18], gradients[19])
```

```python
import math

import jax
import jax.numpy as jnp
from jax import lax
from jax.sharding import Mesh
from jax.sharding import PartitionSpec as P

HEADS = 48
SSM_HEAD = 64
STATE = 256
CONV = 4
QHEADS = 8
KVHEADS = 2
ATT_HEAD = 128
EPSILON = 1e-05
ROPE_BASE = 10000.0
NEG_BIG = -1e30
HIGH = lax.Precision.HIGHEST

RANKS = 8
ROWS = 4
OWN_HEADS = HEADS // RANKS
OWN_SSM = OWN_HEADS * SSM_HEAD
OWN_STATE = 2 * STATE // RANKS
OWN_CONV = OWN_SSM + OWN_STATE

bf16 = jnp.bfloat16
f32 = jnp.float32


def dot(left, right, dims=((1,), (0,))):
    return lax.dot_general(left, right, (dims, ((), ())), preferred_element_type=f32)


def dot_rows(left, right):
    return dot(left, right, ((0,), (0,)))


def dot_cols(left, right):
    return dot(left, right, ((1,), (1,)))


def bdot(left, right, lc, rc):
    return lax.dot_general(
        left, right, (((lc,), (rc,)), ((0,), (0,))), preferred_element_type=f32
    )


def hop(values, flip):
    return lax.ppermute(values, "b", [(i, i ^ flip) for i in range(ROWS)])


def twin(values):
    return lax.ppermute(values, "c", [(0, 1), (1, 0)])


def zhop(values, flip):
    return lax.ppermute(values, "z", [(i, i ^ flip) for i in range(lax.axis_size("z"))])


def zshift(values, step):
    size = lax.axis_size("z")
    return lax.ppermute(
        values, "z", [(i, i + step) for i in range(size) if 0 <= i + step < size]
    )


def gather_group(own):
    half = own.shape[0] // 2
    by_x = hop(own, 1)
    by_y = hop(own, 2)
    far = jnp.concatenate([hop(by_x[:half], 2), hop(by_y[half:], 1)], axis=0)
    mine = [own, by_x, by_y, far]
    return jnp.stack(mine + [twin(part) for part in mine]).reshape((2, ROWS) + own.shape)


def scatter_group(terms):
    half = terms.shape[2] // 2
    other = [twin(terms[1, k]) for k in range(ROWS)]
    sums = [terms[0, k].astype(f32) + other[k].astype(f32) for k in range(ROWS)]
    far = sums[3].astype(bf16)
    to_x = hop(far[:half], 2).astype(f32)
    to_y = hop(far[half:], 1).astype(f32)
    by_x = jnp.concatenate([sums[1][:half] + to_x, sums[1][half:]], axis=0).astype(bf16)
    by_y = jnp.concatenate([sums[2][:half], sums[2][half:] + to_y], axis=0).astype(bf16)
    return sums[0] + hop(by_x, 1).astype(f32) + hop(by_y, 2).astype(f32)


def reslot(values, flip, axis):
    order = [k ^ flip for k in range(ROWS)]
    return jnp.concatenate(
        [lax.slice_in_dim(values, k, k + 1, axis=axis) for k in order], axis=axis
    )


def sum_group(values):
    values = values + twin(values)
    values = values + reslot(hop(values, 1), 1, 1)
    return values + reslot(hop(values, 2), 2, 1)


def gather_all(own):
    rows = own[None]
    rows = jnp.concatenate([rows, twin(rows)], axis=0)
    for flip in (1, 2):
        rows = jnp.concatenate([rows, hop(rows, flip)], axis=0)
    flip = 1
    while flip < lax.axis_size("z"):
        rows = jnp.concatenate([rows, zhop(rows, flip)], axis=0)
        flip *= 2
    return rows


def silu_slope(values):
    sigmoid = jax.nn.sigmoid(values)
    return sigmoid * (1.0 + values * (1.0 - sigmoid))


def rms_scale(values):
    return lax.rsqrt(jnp.mean(values * values, axis=-1, keepdims=True) + EPSILON)


def rotate(values, cosine, sine):
    half = values.shape[-1] // 2
    first = values[..., :half]
    second = values[..., half:]
    return jnp.concatenate([first * cosine - second * sine, second * cosine + first * sine], axis=-1)


def per_device(
    tokens,
    segments,
    cotangent,
    norm_gain,
    gating_weight,
    input_weight,
    state_weight,
    step_weight,
    conv_weight,
    conv_bias,
    step_bias,
    decay_log,
    skip_gain,
    ssm_gain,
    out_weight,
    query_weight,
    keyval_weight,
    context_weight,
    mlp_gain,
    gate_weight,
    up_weight,
    down_weight,
):
    zs = lax.axis_size("z")
    b = lax.axis_index("b")
    z = lax.axis_index("z")
    c = lax.axis_index("c")
    rank = 2 * b + c
    rows = tokens.shape[1]
    width = tokens.shape[2]
    share = norm_gain.shape[0]
    ssm_width = HEADS * SSM_HEAD
    score_scale = 1.0 / math.sqrt(ATT_HEAD)

    def to_z(values):
        return (
            values.reshape(rows, ROWS, zs, 2 * share).transpose(0, 2, 1, 3).reshape(rows, width)
        )

    def from_z(values):
        return (
            values.reshape(rows, zs, ROWS, 2 * share).transpose(0, 2, 1, 3).reshape(rows, width)
        )

    def swap(values):
        return jnp.where(c == 0, values, values[::-1])

    def to_ranks(values):
        return lax.all_to_all(values, ("b", "c"), split_axis=0, concat_axis=0, tiled=True)

    def along_z(values):
        return lax.all_gather(values, "z", axis=0, tiled=True)

    def owner_z(values):
        return lax.psum_scatter(values, "z", scatter_dimension=0, tiled=True)

    x = tokens[0].astype(f32)
    cot = cotangent[0]
    gain_col = norm_gain.astype(f32)[:, None]
    gain2_col = mlp_gain.astype(f32)[:, None]
    ssm_gain_col = ssm_gain.astype(f32)[:, None]

    scale_one = rms_scale(x)
    unit_one = x * scale_one
    n1 = gather_group(to_z(unit_one.astype(bf16))).reshape(-1, width)
    g_all = gather_group(cot).reshape(-1, width)

    scaled = lambda w, gain: (w.astype(f32) * gain).astype(bf16)
    by_rank = lambda w: w.reshape(w.shape[0], RANKS, -1).transpose(1, 0, 2)
    group_kv = KVHEADS * ATT_HEAD
    kv_heads = keyval_weight.reshape(share, 2, KVHEADS, ATT_HEAD).transpose(2, 0, 1, 3)
    kv_rank = jnp.repeat(kv_heads.reshape(KVHEADS, share, 2 * ATT_HEAD), RANKS // KVHEADS, axis=0)
    pad_cols = 128 - OWN_STATE - OWN_HEADS
    w_a = jnp.concatenate(
        [
            by_rank(input_weight),
            by_rank(state_weight),
            by_rank(step_weight),
            jnp.zeros((RANKS, share, pad_cols), bf16),
        ],
        axis=2,
    )
    w_b = jnp.concatenate([by_rank(query_weight), kv_rank], axis=2)
    w_c = by_rank(gating_weight)
    cols_a, cols_b, cols_c = w_a.shape[2], w_b.shape[2], w_c.shape[2]
    w_abc = to_ranks(scaled(jnp.concatenate([w_a, w_b, w_c], axis=2), gain_col[None]))
    cut_b, cut_c = cols_a, cols_a + cols_b
    wa = along_z(w_abc[:, :, :cut_b]).reshape(width, cols_a)
    wb = along_z(w_abc[:, :, cut_b:cut_c]).reshape(width, cols_b)
    wc = along_z(w_abc[:, :, cut_c:]).reshape(width, cols_c)

    def ff_ranks(w):
        return (
            w.reshape(w.shape[0], ROWS, zs, 2, -1)
            .transpose(1, 3, 0, 2, 4)
            .reshape(RANKS, w.shape[0], -1)
        )

    w_gu = to_ranks(
        scaled(jnp.concatenate([ff_ranks(gate_weight), ff_ranks(up_weight)], axis=2), gain2_col[None])
    )
    own_ff = w_gu.shape[2] // 2

    row_out = out_weight.shape[0]
    row_ctx = context_weight.shape[0]
    w_oc = along_z(jnp.concatenate([scaled(out_weight, ssm_gain_col), context_weight], axis=0)[None])
    halves = w_oc.reshape(2, zs // 2, row_out + row_ctx, width)
    kept = lax.dynamic_index_in_dim(halves, c, 0, keepdims=False)
    sent = lax.dynamic_index_in_dim(halves, 1 - c, 0, keepdims=False)
    got = twin(sent)
    both = jnp.where(c == 0, jnp.stack([kept, got], 1), jnp.stack([got, kept], 1))
    w_out = both[:, :, :row_out].reshape(-1, width)
    w_ctx = both[:, :, row_out:].reshape(-1, width)

    w_gu_full = along_z(w_gu).reshape(width, 2 * own_ff)
    w_down = along_z(down_weight)

    chan = conv_bias.shape[0]
    small = gather_all(
        jnp.concatenate(
            [segments[0].astype(bf16), conv_weight.reshape(-1), conv_bias.reshape(-1)]
        )
    )
    count = small.shape[0]
    place = jnp.arange(count)
    me = c + 2 * b + 8 * z

    def pick(wanted, table):
        chosen = (wanted[:, None] == place[None, :]).astype(bf16)
        return dot(chosen, table)

    slot_rows = (place // (2 * zs)) * 2 + ((place // 2) % zs ^ z) * 8 + (place % 2 ^ c)
    segs_all = pick(slot_rows, small[:, :rows]).reshape(ROWS, zs * 2 * rows)
    plain_rows = ((place // (2 * zs)) * 2 + ((place // 2) % zs) * 8 + place % 2) ^ me
    conv_all = pick(plain_rows, small[:, rows:]).reshape(count, CONV + 1, chan)
    conv_all = conv_all.transpose(1, 0, 2).reshape(CONV + 1, count * chan)
    conv_own = jnp.concatenate(
        [
            lax.dynamic_slice_in_dim(conv_all, rank * OWN_SSM, OWN_SSM, 1),
            lax.dynamic_slice_in_dim(conv_all, ssm_width + rank * OWN_STATE, OWN_STATE, 1),
        ],
        axis=1,
    )
    conv_w, conv_b = conv_own[:CONV], conv_own[CONV]
    seg_pad = jnp.concatenate([jnp.zeros((ROWS, rows), f32), segs_all], axis=1)
    seg_near = lax.dynamic_slice_in_dim(seg_pad, z * 2 * rows, 3 * rows, 1)
    seg = seg_near[:, rows:].reshape(ROWS, 2, rows).transpose(1, 0, 2)
    seg_before = seg_near[:, : 2 * rows].reshape(ROWS, 2, rows).transpose(1, 0, 2)

    proj_a = swap(dot(n1, wa).reshape(2, ROWS, rows, cols_a))
    proj_b = swap(dot(n1, wb).reshape(2, ROWS, rows, cols_b))
    gating = swap(dot(n1, wc).reshape(2, ROWS, rows, cols_c))

    mixed = proj_a[..., :OWN_CONV].astype(bf16)
    step_raw = proj_a[..., OWN_CONV : OWN_CONV + OWN_HEADS]
    tails = mixed[:, :, rows - CONV + 1 :]
    before = jnp.stack([zshift(tails[1], 1), tails[0]])
    extended = jnp.concatenate([before, mixed], axis=2).astype(f32)
    seg_ext = jnp.concatenate([seg_before[:, :, rows - CONV + 1 :], seg], axis=2)
    tap_masks = [
        (seg_ext[:, :, o : o + rows] == seg).astype(f32)[..., None] for o in range(CONV)
    ]
    conv_pre = conv_b
    for o in range(CONV):
        conv_pre = conv_pre + conv_w[o] * extended[:, :, o : o + rows] * tap_masks[o]
    activated = jax.nn.silu(conv_pre).astype(bf16)
    chunks = 2 * ROWS
    xs = activated[..., :OWN_SSM].reshape(chunks, rows, OWN_SSM)
    bc = gather_group(activated[..., OWN_SSM:].reshape(2 * ROWS * rows, OWN_STATE))
    bc = bc.reshape(2, ROWS, 2, ROWS, rows, OWN_STATE)

    def joined(slots):
        parts = [reslot(bc[r, m], m, 1) for m in slots for r in range(2)]
        return jnp.concatenate(parts, axis=-1).reshape(chunks, rows, STATE)

    low_half, high_half = joined((0, 1)), joined((2, 3))
    b_mat = jnp.where(b < 2, low_half, high_half)
    c_mat = jnp.where(b < 2, high_half, low_half)

    own_slice = lambda v: lax.dynamic_slice_in_dim(v.astype(f32), rank * OWN_HEADS, OWN_HEADS, 0)
    step_b = own_slice(step_bias)
    rate = -jnp.exp(own_slice(decay_log))
    skip = own_slice(skip_gain)
    skip_wide = jnp.repeat(skip, SSM_HEAD)
    step_in = (step_raw + step_b).reshape(chunks, rows, OWN_HEADS)
    step = jax.nn.softplus(step_in)
    index = jnp.arange(rows)
    lower = (index[:, None] >= index[None, :])
    lower_f = lower.astype(f32)
    cumulative = jnp.einsum("ts,qsh->qth", lower_f, step * rate, precision=HIGH)
    seg_q = seg.reshape(chunks, rows)
    allowed = (seg_q[:, :, None] == seg_q[:, None, :]) & lower[None]
    cum_h = cumulative.transpose(0, 2, 1)
    decays = jnp.where(
        allowed[:, None],
        jnp.exp(jnp.where(allowed[:, None], cum_h[..., None] - cum_h[:, :, None, :], 0.0)),
        0.0,
    )
    inner = bdot(c_mat, b_mat, 2, 2)
    step_h = step.transpose(0, 2, 1)[:, :, None, :]
    mix = (inner[:, None] * decays * step_h).astype(bf16)
    xs_h = xs.reshape(chunks, rows, OWN_HEADS, SSM_HEAD)
    within = jnp.einsum("qhts,qshp->qthp", mix, xs_h, preferred_element_type=f32)
    within = within.reshape(chunks, rows, OWN_SSM)
    wide = lambda v: jnp.repeat(v, SSM_HEAD, axis=-1)
    per_head = lambda v: v.reshape(v.shape[:-1] + (OWN_HEADS, SSM_HEAD)).sum(-1)
    last_before = seg_before[:, :, rows - 1].reshape(chunks, 1)
    carried = (seg_q == last_before).astype(f32)
    entry = jnp.exp(cumulative) * carried[..., None]
    ending = (seg_q == seg_q[:, rows - 1 :]).astype(f32)
    cum_last = cumulative[:, rows - 1 :]
    tail_decay = jnp.exp(cum_last - cumulative) * ending[..., None]
    tail = tail_decay * step
    xs_f = xs.astype(f32)
    weighted = (xs_f * wide(tail)).astype(bf16)
    local = bdot(weighted, b_mat, 1, 1).reshape(2, ROWS, OWN_SSM, STATE)
    passing = (jnp.exp(cum_last[:, 0]) * carried[:, rows - 1 :]).reshape(2, ROWS, OWN_HEADS)
    pass_wide = wide(passing)[..., None]
    pass_both = pass_wide[0] * pass_wide[1]
    local_both = pass_wide[1] * local[0] + local[1]
    state = jnp.zeros_like(local[0])
    for s in range(zs - 1):
        message = (pass_both * state + local_both).astype(bf16)
        state = state + lax.ppermute(message, "z", [(s, s + 1)]).astype(f32)
    state_in = jnp.stack([state, pass_wide[0] * state + local[0]]).reshape(chunks, OWN_SSM, STATE)
    state_low = state_in.astype(bf16)
    inter = bdot(c_mat, state_low, 2, 2)
    entry_wide = wide(entry)
    ssm_out = within + inter * entry_wide + skip_wide * xs_f
    gating_q = gating.reshape(chunks, rows, OWN_SSM)
    gate_act = jax.nn.silu(gating_q)
    gated = ssm_out * gate_act

    squares = sum_group(jnp.sum(gated * gated, axis=-1).reshape(2, ROWS, rows))
    scale_ssm = lax.rsqrt(squares * (1.0 / ssm_width) + EPSILON).reshape(chunks, rows, 1)
    unit_ssm = gated * scale_ssm
    unit_low = unit_ssm.astype(bf16)

    places = (z * 2 * rows + jnp.arange(2 * rows, dtype=jnp.int32)).astype(f32)
    half_head = ATT_HEAD // 2
    frequency = jnp.exp(jnp.arange(half_head, dtype=f32) * (-2.0 * math.log(ROPE_BASE) / ATT_HEAD))
    angles = (places[:, None] * frequency[None, :]).reshape(2, 1, rows, half_head)
    cosine, sine = jnp.cos(angles), jnp.sin(angles)
    by_seq = lambda v: v.transpose(1, 0, 2, 3).reshape(ROWS, 2 * rows, v.shape[-1])
    from_seq = lambda v: v.reshape(ROWS, 2, rows, v.shape[-1]).transpose(1, 0, 2, 3)
    query = by_seq(rotate(proj_b[..., :ATT_HEAD], cosine, sine).astype(bf16))
    key = rotate(proj_b[..., ATT_HEAD : 2 * ATT_HEAD], cosine, sine).astype(bf16)
    keyval = by_seq(jnp.concatenate([key, proj_b[..., 2 * ATT_HEAD :].astype(bf16)], axis=-1))
    own_kv = lax.dynamic_slice_in_dim(keyval, 2 * c, 2, 0)
    kv_parts = [own_kv] + [zhop(own_kv, m) for m in range(1, zs)]
    kv_own = jnp.stack(kv_parts, axis=1)
    kv_other = twin(kv_own)
    kv_all = jnp.where(
        c == 0,
        jnp.concatenate([kv_own, kv_other], axis=0),
        jnp.concatenate([kv_other, kv_own], axis=0),
    ).reshape(ROWS, zs * 2 * rows, 2 * ATT_HEAD)
    key_all, val_all = kv_all[..., :ATT_HEAD], kv_all[..., ATT_HEAD:]
    key_place = ((jnp.arange(zs) ^ z)[:, None] * 2 * rows + jnp.arange(2 * rows)[None, :]).reshape(-1)
    seg_keys = jnp.concatenate(
        [lax.dynamic_slice_in_dim(segs_all, (m ^ z) * 2 * rows, 2 * rows, 1) for m in range(zs)],
        axis=1,
    )
    seg_query = seg_near[:, rows:]
    seen = (seg_query[:, :, None] == seg_keys[:, None, :]) & (
        places.astype(jnp.int32)[None, :, None] >= key_place[None, None, :]
    )
    scores = jnp.where(seen, bdot(query, key_all, 2, 2) * score_scale, NEG_BIG)
    highest = jnp.max(scores, axis=-1, keepdims=True)
    exponent = jnp.where(seen, jnp.exp(scores - highest), 0.0)
    total = jnp.sum(exponent, axis=-1, keepdims=True)
    context = bdot(exponent.astype(bf16), val_all, 2, 1) / total
    logsum = highest + jnp.log(total)
    context_low = context.astype(bf16)

    mixer_in = jnp.concatenate(
        [unit_low.reshape(2, ROWS, rows, OWN_SSM), from_seq(context_low)], axis=-1
    )
    mixer_in = swap(mixer_in).reshape(-1, OWN_SSM + ATT_HEAD)
    w_mix = jnp.concatenate([w_out, w_ctx], axis=0)
    terms = dot(mixer_in, w_mix).astype(bf16)
    hidden = x + scatter_group(terms.reshape(2, ROWS, rows, width))

    scale_two = rms_scale(hidden)
    unit_two = hidden * scale_two
    n2 = gather_group(to_z(unit_two.astype(bf16))).reshape(-1, width)
    gate_up = dot(n2, w_gu_full)
    gate_pre, up_pre = gate_up[:, :own_ff], gate_up[:, own_ff:]
    gate_silu = jax.nn.silu(gate_pre)
    activation = (gate_silu * up_pre).astype(bf16)
    down_terms = dot(activation, w_down).astype(bf16)
    result = (hidden + scatter_group(down_terms.reshape(2, ROWS, rows, width))).astype(bf16)

    grad_down = owner_z(dot_rows(activation, g_all).astype(bf16))
    grad_act = dot_cols(g_all, w_down)
    grad_gate = (grad_act * up_pre * silu_slope(gate_pre)).astype(bf16)
    grad_up = (grad_act * gate_silu).astype(bf16)
    grad_gu = jnp.concatenate([grad_gate, grad_up], axis=1)
    grad_gu_w = owner_z(dot_rows(n2, grad_gu).astype(bf16)).reshape(RANKS, share, 2 * own_ff)
    e2_terms = dot_cols(grad_gu, w_gu_full).astype(bf16)
    e2 = from_z(scatter_group(e2_terms.reshape(2, ROWS, rows, width)))
    grad_hidden = cot.astype(f32) + scale_two * (
        e2 - unit_two * jnp.mean(e2 * unit_two, axis=-1, keepdims=True)
    )
    grad_mix = gather_group(grad_hidden.astype(bf16)).reshape(-1, width)

    grad_oc_w = dot_rows(mixer_in, grad_mix).astype(bf16)
    grad_out_rows = grad_oc_w[:OWN_SSM].reshape(zs // 2, 2, row_out, width)
    grad_ctx_rows = grad_oc_w[OWN_SSM:].reshape(zs // 2, 2, row_ctx, width)
    grad_oc = jnp.concatenate([grad_out_rows, grad_ctx_rows], axis=2)
    oc_kept = lax.dynamic_index_in_dim(grad_oc, c, 1, keepdims=False)
    oc_got = twin(lax.dynamic_index_in_dim(grad_oc, 1 - c, 1, keepdims=False))
    oc_all = jnp.where(
        c == 0,
        jnp.concatenate([oc_kept, oc_got], axis=0),
        jnp.concatenate([oc_got, oc_kept], axis=0),
    )
    grad_oc_own = owner_z(oc_all)[0].astype(f32)
    grad_mixer = swap(dot_cols(grad_mix, w_mix).reshape(2, ROWS, rows, OWN_SSM + ATT_HEAD))
    es = grad_mixer[..., :OWN_SSM].reshape(chunks, rows, OWN_SSM)
    grad_context = by_seq(grad_mixer[..., OWN_SSM:].astype(bf16))

    es_sum = sum_group(jnp.sum(es * unit_ssm, axis=-1).reshape(2, ROWS, rows))
    es_mean = (es_sum * (1.0 / ssm_width)).reshape(chunks, rows, 1)
    grad_gated = scale_ssm * (es - unit_ssm * es_mean)
    gy = (grad_gated * gate_act).astype(bf16)
    grad_gating = (grad_gated * ssm_out * silu_slope(gating_q)).astype(bf16)
    to_rel = lambda v: swap(v.reshape(2, ROWS, rows, v.shape[-1])).reshape(-1, v.shape[-1])
    grad_c_low = to_rel(grad_gating)
    grad_wc = owner_z(dot_rows(n1, grad_c_low).astype(bf16)).reshape(RANKS, share, cols_c)

    delta = jnp.sum(grad_context.astype(f32) * context, axis=-1, keepdims=True)
    prob = jnp.where(seen, jnp.exp(jnp.where(seen, scores - logsum, NEG_BIG)), 0.0)
    grad_prob = bdot(grad_context, val_all, 2, 2)
    grad_scores = (prob * (grad_prob - delta)).astype(bf16)
    grad_query = bdot(grad_scores, key_all, 2, 1) * score_scale
    grad_key = bdot(grad_scores, query, 1, 1) * score_scale
    grad_val = bdot(prob.astype(bf16), grad_context, 1, 1)
    grad_kv = jnp.concatenate([grad_key, grad_val], axis=-1).astype(bf16)
    grad_kv = grad_kv.reshape(2, 2, zs, 2 * rows, 2 * ATT_HEAD)
    kv_kept = lax.dynamic_index_in_dim(grad_kv, c, 0, keepdims=False).astype(f32)
    kv_got = twin(lax.dynamic_index_in_dim(grad_kv, 1 - c, 0, keepdims=False)).astype(f32)
    kv_sum = kv_kept + kv_got
    kv_low = kv_sum.astype(bf16)
    kv_grad = kv_sum[:, 0]
    for m in range(1, zs):
        kv_grad = kv_grad + zhop(kv_low[:, m], m).astype(f32)
    zero_kv = jnp.zeros_like(kv_grad)
    kv_grad = jnp.where(
        c == 0,
        jnp.concatenate([kv_grad, zero_kv], axis=0),
        jnp.concatenate([zero_kv, kv_grad], axis=0),
    )
    kv_grad = from_seq(kv_grad)
    grad_b_low = jnp.concatenate(
        [
            rotate(from_seq(grad_query), cosine, -sine),
            rotate(kv_grad[..., :ATT_HEAD], cosine, -sine),
            kv_grad[..., ATT_HEAD:],
        ],
        axis=-1,
    ).astype(bf16)
    grad_b_low = to_rel(grad_b_low)
    grad_wb = owner_z(dot_rows(n1, grad_b_low).astype(bf16)).reshape(RANKS, share, cols_b)

    gy_f = gy.astype(f32)
    gy_h = gy.reshape(chunks, rows, OWN_HEADS, SSM_HEAD)
    grad_skip = per_head(jnp.sum(gy_f * xs_f, axis=(0, 1)))
    grad_mixw = jnp.einsum("qthp,qshp->qhts", gy_h, xs_h, preferred_element_type=f32)
    grad_xs = skip_wide * gy_f + jnp.einsum(
        "qhts,qthp->qshp", mix, gy_h, preferred_element_type=f32
    ).reshape(chunks, rows, OWN_SSM)
    product = grad_mixw * decays
    grad_inner = jnp.sum(product * step_h, axis=1).astype(bf16)
    flow = product * inner[:, None]
    step_grad = jnp.sum(flow, axis=2).transpose(0, 2, 1)
    flow = flow * step_h
    grad_cum = (jnp.sum(flow, axis=3) - jnp.sum(flow, axis=2)).transpose(0, 2, 1)
    grad_c = bdot(grad_inner, b_mat, 2, 1)
    grad_b = bdot(grad_inner, c_mat, 1, 1)
    across = (gy_f * entry_wide).astype(bf16)
    grad_c = grad_c + bdot(across, state_low, 2, 1)
    grad_local = bdot(across, c_mat, 1, 1).reshape(2, ROWS, OWN_SSM, STATE)
    grad_cum = grad_cum + per_head(gy_f * inter) * entry
    back_both = pass_wide[0] * grad_local[1] + grad_local[0]
    flowing = jnp.zeros_like(back_both)
    for s in range(zs - 1, 0, -1):
        message = (pass_both * flowing + back_both).astype(bf16)
        flowing = flowing + lax.ppermute(message, "z", [(s, s - 1)]).astype(f32)
    outgoing = jnp.stack([pass_wide[1] * flowing + grad_local[1], flowing])
    outgoing = outgoing.reshape(chunks, OWN_SSM, STATE)
    out_low = outgoing.astype(bf16)
    grad_pass = jnp.sum((outgoing * state_in).reshape(chunks, OWN_HEADS, -1), axis=-1)
    grad_weighted = bdot(b_mat, out_low, 2, 2)
    grad_b = grad_b + bdot(weighted, out_low, 2, 1)
    grad_xs = grad_xs + grad_weighted * wide(tail)
    grad_tail = per_head(grad_weighted * xs_f)
    tail_flow = grad_tail * tail
    step_grad = step_grad + grad_tail * tail_decay
    is_last = (index == rows - 1).astype(f32)[None, :, None]
    end_term = grad_pass * passing.reshape(chunks, OWN_HEADS) + jnp.sum(tail_flow, axis=1)
    grad_cum = grad_cum - tail_flow + is_last * end_term[:, None]
    grad_rate = jnp.einsum("st,qsh->qth", lower_f, grad_cum, precision=HIGH)
    step_grad = step_grad + grad_rate * rate
    grad_decay = jnp.sum(grad_rate * step, axis=(0, 1)) * rate
    grad_step_raw = step_grad * jax.nn.sigmoid(step_in)
    grad_step_bias = jnp.sum(grad_step_raw, axis=(0, 1))

    low_grad = jnp.where(b < 2, grad_b, grad_c).reshape(2, ROWS, rows, 4, OWN_STATE)
    high_grad = jnp.where(b < 2, grad_c, grad_b).reshape(2, ROWS, rows, 4, OWN_STATE)
    bc_terms = [[None] * ROWS, [None] * ROWS]
    for m in range(ROWS):
        source = low_grad if m < 2 else high_grad
        for r in range(2):
            piece = reslot(source[..., 2 * (m % 2) + r, :], m, 1)
            bc_terms[r][m] = piece.reshape(-1, OWN_STATE).astype(bf16)
    grad_bc = scatter_group(jnp.stack([jnp.stack(bc_terms[0]), jnp.stack(bc_terms[1])]))
    grad_act_in = jnp.concatenate(
        [grad_xs.reshape(2, ROWS, rows, OWN_SSM), grad_bc.reshape(2, ROWS, rows, OWN_STATE)],
        axis=-1,
    )

    grad_pre = grad_act_in * silu_slope(conv_pre)
    conv_sums = []
    grad_ext = jnp.zeros((2, ROWS, rows + CONV - 1, OWN_CONV), f32)
    for o in range(CONV):
        masked = grad_pre * tap_masks[o]
        conv_sums.append(jnp.sum(masked * extended[:, :, o : o + rows], axis=(0, 1, 2)))
        grad_ext = grad_ext + jnp.pad(
            masked * conv_w[o], ((0, 0), (0, 0), (o, CONV - 1 - o), (0, 0))
        )
    conv_sums.append(jnp.sum(grad_pre, axis=(0, 1, 2)))
    head_sums = jnp.concatenate([grad_step_bias, grad_decay, grad_skip])
    conv_sums.append(jnp.pad(head_sums, (0, OWN_CONV - head_sums.shape[0])))
    first = grad_ext[:, :, : CONV - 1]
    returned = jnp.stack([first[1], zshift(first[0].astype(bf16), -1).astype(f32)])
    grad_mixed = grad_ext[:, :, CONV - 1 :] + jnp.pad(
        returned, ((0, 0), (0, 0), (rows - CONV + 1, 0), (0, 0))
    )
    grad_a_low = jnp.concatenate(
        [
            grad_mixed.astype(bf16),
            grad_step_raw.reshape(2, ROWS, rows, OWN_HEADS).astype(bf16),
            jnp.zeros((2, ROWS, rows, pad_cols), bf16),
        ],
        axis=-1,
    )
    grad_a_low = to_rel(grad_a_low)
    grad_wa = owner_z(dot_rows(n1, grad_a_low).astype(bf16)).reshape(RANKS, share, cols_a)

    e1_terms = (
        dot_cols(grad_c_low, wc) + dot_cols(grad_b_low, wb) + dot_cols(grad_a_low, wa)
    ).astype(bf16)
    e1 = from_z(scatter_group(e1_terms.reshape(2, ROWS, rows, width)))
    grad_x = grad_hidden + scale_one * (
        e1 - unit_one * jnp.mean(e1 * unit_one, axis=-1, keepdims=True)
    )

    def from_ranks(values):
        return to_ranks(values).astype(f32)

    def unrank(values):
        return values.transpose(1, 0, 2).reshape(share, -1)

    got_a = from_ranks(grad_wa)
    got_b = from_ranks(grad_wb)
    got_c = from_ranks(grad_wc)
    got_gu = from_ranks(grad_gu_w)
    d_input = unrank(got_a[..., :OWN_SSM])
    d_state = unrank(got_a[..., OWN_SSM:OWN_CONV])
    d_step = unrank(got_a[..., OWN_CONV : OWN_CONV + OWN_HEADS])
    d_query = unrank(got_b[..., :ATT_HEAD])
    d_kv = got_b[..., ATT_HEAD:].reshape(KVHEADS, RANKS // KVHEADS, share, 2, ATT_HEAD).sum(1)
    d_kv = d_kv.transpose(1, 2, 0, 3).reshape(share, 2 * group_kv)
    d_gating = unrank(got_c)

    def ff_unrank(values):
        return (
            values.reshape(ROWS, 2, share, zs, own_ff // zs)
            .transpose(2, 0, 3, 1, 4)
            .reshape(share, -1)
        )

    d_gate, d_up = ff_unrank(got_gu[..., :own_ff]), ff_unrank(got_gu[..., own_ff:])

    def gain_grad(pairs):
        return sum(jnp.sum(w.astype(f32) * d, axis=1) for w, d in pairs)

    d_norm_gain = gain_grad(
        (
            (gating_weight, d_gating),
            (input_weight, d_input),
            (state_weight, d_state),
            (step_weight, d_step),
            (query_weight, d_query),
            (keyval_weight, d_kv),
        )
    )
    d_mlp_gain = gain_grad(((gate_weight, d_gate), (up_weight, d_up)))
    d_out = grad_oc_own[:row_out]
    d_ctx = grad_oc_own[row_out:]
    d_ssm_gain = gain_grad(((out_weight, d_out),))

    sums = jnp.stack(conv_sums)
    flip = 1
    while flip < zs:
        sums = sums + zhop(sums, flip)
        flip *= 2
    table = sums[None]
    table = jnp.concatenate([table, twin(table)], axis=0)
    for flip in (1, 2):
        table = jnp.concatenate([table, hop(table, flip)], axis=0)
    place = jnp.arange(RANKS)
    chosen = ((place ^ rank)[:, None] == place[None, :]).astype(f32)
    table = jnp.einsum("rs,sof->rof", chosen, table, precision=HIGH)
    conv_ssm = table[:, : CONV + 1, :OWN_SSM].transpose(1, 0, 2).reshape(CONV + 1, -1)
    conv_state = table[:, : CONV + 1, OWN_SSM:].transpose(1, 0, 2).reshape(CONV + 1, -1)
    conv_full = jnp.concatenate([conv_ssm, conv_state], axis=1)
    conv_mine = lax.dynamic_slice_in_dim(conv_full, (rank // 2 * zs * 2 + z * 2 + c) * chan, chan, 1)
    heads = table[:, CONV + 1, : 3 * OWN_HEADS].reshape(RANKS, 3, OWN_HEADS)
    heads = heads.transpose(1, 0, 2).reshape(3, HEADS)

    return (
        result[None],
        grad_x.astype(bf16)[None],
        d_norm_gain,
        d_gating * gain_col,
        d_input * gain_col,
        d_state * gain_col,
        d_step * gain_col,
        conv_mine[:CONV],
        conv_mine[CONV],
        heads[0],
        heads[1],
        heads[2],
        d_ssm_gain,
        d_out * ssm_gain_col,
        d_query * gain_col,
        d_kv * gain_col,
        d_ctx,
        d_mlp_gain,
        d_gate * gain2_col,
        d_up * gain2_col,
        grad_down.astype(f32),
    )


def solution(mesh):
    places = mesh.devices.reshape(ROWS, mesh.shape["seq"] // 2, 2)
    split = Mesh(places, ("b", "z", "c"))
    everywhere = ("b", "z", "c")
    row = P(everywhere, None)
    vector = P(everywhere)
    token = P("b", ("z", "c"), None)
    return jax.shard_map(
        per_device,
        mesh=split,
        in_specs=(
            token,
            P("b", ("z", "c")),
            token,
            vector,
            row,
            row,
            row,
            row,
            P(None, everywhere),
            vector,
            P(),
            P(),
            P(),
            vector,
            row,
            row,
            row,
            row,
            vector,
            row,
            row,
            row,
        ),
        out_specs=(
            token,
            token,
            vector,
            row,
            row,
            row,
            row,
            P(None, everywhere),
            vector,
            P(),
            P(),
            P(),
            vector,
            row,
            row,
            row,
            row,
            vector,
            row,
            row,
            row,
        ),
        check_vma=False,
    )
```

```python
import math

import jax
import jax.numpy as jnp
from jax import lax
from jax.experimental import pallas as pl
from jax.experimental.pallas import tpu as pltpu
from jax.sharding import Mesh
from jax.sharding import PartitionSpec as P

HEADS = 48
SSM_HEAD = 64
STATE = 256
CONV = 4
QHEADS = 8
KVHEADS = 2
ATT_HEAD = 128
EPSILON = 1e-05
ROPE_BASE = 10000.0
NEG_BIG = -1e30
HIGH = lax.Precision.HIGHEST

RANKS = 8
ROWS = 4
OWN_HEADS = HEADS // RANKS
OWN_SSM = OWN_HEADS * SSM_HEAD
OWN_STATE = 2 * STATE // RANKS
OWN_CONV = OWN_SSM + OWN_STATE

bf16 = jnp.bfloat16
f32 = jnp.float32


ANY = pl.BlockSpec(memory_space=pl.ANY)
IN_VMEM = pl.BlockSpec(memory_space=pltpu.VMEM)
CHUNK = 256
LANES_A = 512
STEP_AT = OWN_CONV
PIECE = OWN_STATE
HALF = 2 * CHUNK


def dot(left, right, dims=((1,), (0,))):
    return lax.dot_general(left, right, (dims, ((), ())), preferred_element_type=f32)


def dot_rows(left, right):
    return dot(left, right, ((0,), (0,)))


def dot_cols(left, right):
    return dot(left, right, ((1,), (1,)))


def bdot(left, right, lc, rc):
    return lax.dot_general(
        left, right, (((lc,), (rc,)), ((0,), (0,))), preferred_element_type=f32
    )


def hop(values, flip):
    return lax.ppermute(values, "b", [(i, i ^ flip) for i in range(ROWS)])


def twin(values):
    return lax.ppermute(values, "c", [(0, 1), (1, 0)])


def zhop(values, flip):
    return lax.ppermute(values, "z", [(i, i ^ flip) for i in range(lax.axis_size("z"))])


def zshift(values, step):
    size = lax.axis_size("z")
    return lax.ppermute(
        values, "z", [(i, i + step) for i in range(size) if 0 <= i + step < size]
    )


def after(values, *earlier):
    return lax.optimization_barrier((values,) + earlier)[0]


def gather_group(own, meanwhile=None):
    half = own.shape[0] // 2
    by_x = hop(own, 1)
    by_y = hop(own, 2)
    if meanwhile is not None:
        by_x, by_y, meanwhile = lax.optimization_barrier((by_x, by_y, meanwhile))
    mine = [own, by_x, by_y, hop(by_x[:half], 2), hop(by_y[half:], 1)]
    pieces = mine + [twin(part) for part in mine]
    return pieces if meanwhile is None else (pieces, meanwhile)


def starts_of(pieces):
    starts = [0]
    for piece in pieces:
        starts.append(starts[-1] + piece.shape[0])
    return starts


def reslot(values, flip, axis):
    order = [k ^ flip for k in range(ROWS)]
    return jnp.concatenate(
        [lax.slice_in_dim(values, k, k + 1, axis=axis) for k in order], axis=axis
    )


def sum_group(values):
    values = values + twin(values)[::-1]
    total = values
    for flip in range(1, ROWS):
        total = total + reslot(hop(values, flip), flip, 1)
    return total


def silu_slope(values):
    sigmoid = jax.nn.sigmoid(values)
    return sigmoid * (1.0 + values * (1.0 - sigmoid))


def rms_scale(values):
    return lax.rsqrt(jnp.mean(values * values, axis=-1, keepdims=True) + EPSILON)


def rotate(values, cosine, sine):
    half = values.shape[-1] // 2
    first = values[..., :half]
    second = values[..., half:]
    return jnp.concatenate([first * cosine - second * sine, second * cosine + first * sine], axis=-1)


def split(values, count):
    terms = []
    for _ in range(count):
        low = values.astype(bf16)
        terms.append(low)
        values = values - low.astype(f32)
    return terms


def exact(ones, values, dims=((1,), (0,)), count=3):
    return sum(dot(ones.astype(bf16), term, dims) for term in split(values, count))


def head_map(rows, cols, along):
    channel = lax.broadcasted_iota(jnp.int32, (rows, cols), along)
    head = lax.broadcasted_iota(jnp.int32, (rows, cols), 1 - along)
    return (channel // SSM_HEAD == head).astype(bf16)


def widen(values):
    rows = values.shape[0]
    first = lax.broadcasted_iota(jnp.int32, (rows, 2 * SSM_HEAD), 1) < SSM_HEAD
    parts = []
    for h in range(0, OWN_HEADS, 2):
        left = jnp.broadcast_to(values[:, h : h + 1], first.shape)
        right = jnp.broadcast_to(values[:, h + 1 : h + 2], first.shape)
        parts.append(jnp.where(first, left, right))
    return jnp.concatenate(parts, axis=1)


def narrow(values):
    ones = head_map(OWN_SSM, 8, 0)
    return sum(dot(term, ones) for term in split(values, 2))


def row_sums(values):
    ones = jnp.ones((8, values.shape[1]), bf16)
    return exact(ones, values, ((1,), (1,)), 2)


def sigmoid_of(values):
    return 1.0 / (1.0 + jnp.exp(-values))


def tri(lower):
    t = lax.broadcasted_iota(jnp.int32, (CHUNK, CHUNK), 0)
    s = lax.broadcasted_iota(jnp.int32, (CHUNK, CHUNK), 1)
    return (t >= s) if lower else (t <= s)


def conv_kernel(proj, halo, marks, conv, head, xs_out, bc_out, slope_out, meta_out, row_out, ext):
    ext[0:8, :] = halo[0]
    ext[8:, :] = proj[0].astype(bf16).astype(f32)
    pre = conv[4:5, :] + conv[3:4, :] * ext[8 : 8 + CHUNK, :]
    for o in range(CONV - 1):
        pre = pre + conv[o : o + 1, :] * ext[5 + o : 5 + o + CHUNK, :] * marks[0, :, 3 + o : 4 + o]
    sig = sigmoid_of(pre)
    act = (pre * sig).astype(bf16)
    xs_out[0] = act[:, :OWN_SSM]
    for r in range(2):

        @pl.when(pl.program_id(1) == r)
        def _():
            bc_out[0, :, r * PIECE : (r + 1) * PIECE] = act[:, OWN_SSM:OWN_CONV]

    slope_out[0] = sig * (1.0 + pre * (1.0 - sig))
    raw = proj[0][:, STEP_AT : STEP_AT + 8] + head[0:1, 0:8]
    real = lax.broadcasted_iota(jnp.int32, (CHUNK, 8), 1) < OWN_HEADS
    step = jnp.maximum(raw, 0.0) + jnp.log(1.0 + jnp.exp(-jnp.abs(raw)))
    step = jnp.where(real, step, 0.0)
    cum = exact(tri(True), step * head[1:2, 0:8])
    meta = jnp.concatenate(
        [step, cum, sigmoid_of(raw), jnp.zeros((CHUNK, 104), f32)], axis=1
    )
    meta_out[0] = meta[:, :32]
    row_out[0] = meta.T[:16]


def marks_kernel(own, before, out):
    lane = lax.broadcasted_iota(jnp.int32, (1, CHUNK), 1)
    for q in range(own.shape[0]):
        seg, prev = own[q : q + 1, :], before[q : q + 1, :]
        rows = [seg, (seg == prev[:, CHUNK - 1 :]).astype(f32), (seg == seg[:, CHUNK - 1 :]).astype(f32)]
        for o in range(CONV - 1):
            by = CONV - 1 - o
            moved = jnp.where(lane < by, pltpu.roll(prev, by, 1), pltpu.roll(seg, by, 1))
            rows.append((moved == seg).astype(f32))
        rows.append(jnp.zeros((128 - len(rows), CHUNK), f32))
        out[q] = jnp.concatenate(rows, axis=0).T[:, :8]


def marks_of(own, before):
    chunks = own.shape[0]
    return pl.pallas_call(
        marks_kernel,
        in_specs=[IN_VMEM] * 2,
        out_specs=IN_VMEM,
        out_shape=jax.ShapeDtypeStruct((chunks, CHUNK, 8), f32),
        compiler_params=pltpu.CompilerParams(vmem_limit_bytes=VMEM),
        cost_estimate=lasting(3),
        name="marks",
    )(own, before)


def conv_forward(proj, halo, marks, conv, head):
    block = lambda *shape: pl.BlockSpec((1,) + shape, lambda k, r: (r * ROWS + k, 0, 0))
    whole = pl.BlockSpec((8, LANES_A), lambda k, r: (0, 0))
    chunks = proj.shape[0]
    return pl.pallas_call(
        conv_kernel,
        grid=(ROWS, 2),
        in_specs=[
            block(CHUNK, LANES_A),
            block(8, LANES_A),
            block(CHUNK, 8),
            whole,
            pl.BlockSpec((8, 128), lambda k, r: (0, 0)),
        ],
        out_specs=[
            block(CHUNK, OWN_SSM),
            pl.BlockSpec((1, CHUNK, 2 * PIECE), lambda k, r: (k, 0, 0)),
            block(CHUNK, LANES_A),
            block(CHUNK, 32),
            block(16, CHUNK),
        ],
        out_shape=[
            jax.ShapeDtypeStruct((chunks, CHUNK, OWN_SSM), bf16),
            jax.ShapeDtypeStruct((ROWS, CHUNK, 2 * PIECE), bf16),
            jax.ShapeDtypeStruct((chunks, CHUNK, LANES_A), f32),
            jax.ShapeDtypeStruct((chunks, CHUNK, 32), f32),
            jax.ShapeDtypeStruct((chunks, 16, CHUNK), f32),
        ],
        scratch_shapes=[pltpu.VMEM((8 + CHUNK, LANES_A), f32)],
        compiler_params=pltpu.CompilerParams(vmem_limit_bytes=VMEM),
        cost_estimate=lasting(8),
        name="conv_forward",
    )(proj, halo, marks, conv, head)


VMEM = 60 * 1024 * 1024


def lasting(microseconds):
    return pl.CostEstimate(
        flops=0, bytes_accessed=int(microseconds * 1.1e6), transcendentals=0
    )


def time_spec(shape, backward=False):
    def at(k, t, where):
        core = (1 - t if backward else t) ^ where[2]
        return (core * ROWS + k,) + (0,) * len(shape)

    return pl.BlockSpec((1,) + tuple(shape), at)


def slot_spec(shape):
    return pl.BlockSpec((1,) + tuple(shape), lambda k, t, where: (k,) + (0,) * len(shape))


def piece_specs(kind):
    def spec(i):
        def at(k, t, where):
            slot = (i // 2 + 2 * kind) ^ (2 * (where[0] // 2))
            return (i % 2 * ROWS + slot, k ^ slot, 0, 0)

        return pl.BlockSpec((1, 1, CHUNK, 2 * PIECE), at)

    return [spec(i) for i in range(4)]


def core_of(where, backward=False):
    t = pl.program_id(1)
    return (1 - t if backward else t) ^ where[2]


def joined(pieces, core):
    parts = []
    for i, piece in enumerate(pieces):
        both = piece[0, 0]
        parts.append(jnp.where(core ^ (i % 2) == 0, both[:, :PIECE], both[:, PIECE:]))
    return jnp.concatenate(parts, axis=1)


def tails_of(meta, marks):
    step, cum = meta[0, :, 0:8], meta[0, :, 8:16]
    last = cum[CHUNK - 1 : CHUNK]
    decay = jnp.exp(last - cum) * marks[0, :, 2:3]
    return step, cum, decay, decay * step


def local_kernel(where, xs, b0, b1, b2, b3, meta, marks, p1, first_out, both_out):
    _, _, _, tail = tails_of(meta, marks)
    weighted = (xs[0].astype(f32) * widen(tail)).astype(bf16)
    local = dot_rows(weighted, joined((b0, b1, b2, b3), core_of(where)))

    @pl.when(pl.program_id(1) == 0)
    def _():
        first_out[0] = local

    @pl.when(pl.program_id(1) == 1)
    def _():
        both_out[0] = p1[0] * first_out[0] + local


def local_states(where, xs, bc, meta, marks, p1):
    state = jax.ShapeDtypeStruct((ROWS, OWN_SSM, STATE), f32)
    return pl.pallas_call(
        local_kernel,
        grid_spec=pltpu.PrefetchScalarGridSpec(
            num_scalar_prefetch=1,
            grid=(ROWS, 2),
            in_specs=[time_spec((CHUNK, OWN_SSM))]
            + piece_specs(0)
            + [time_spec((CHUNK, 32)), time_spec((CHUNK, 8)), slot_spec((OWN_SSM, 1))],
            out_specs=[slot_spec((OWN_SSM, STATE))] * 2,
        ),
        out_shape=[state, state],
        compiler_params=pltpu.CompilerParams(vmem_limit_bytes=VMEM),
        cost_estimate=lasting(8),
        name="local_states",
    )(where, xs, bc, bc, bc, bc, meta, marks, p1)


def decay_of(meta, row, allowed, h):
    spread = meta[0, :, 8 + h : 9 + h] - row[0, 8 + h : 9 + h, :]
    return jnp.exp(jnp.where(allowed, spread, NEG_BIG))


def ssm_kernel(
    where, xs, b0, b1, b2, b3, c0, c1, c2, c3, meta, row, marks, segs, state, first, p0, gating, skip,
    out, gated_out, square_out, work,
):
    later = pl.program_id(1) == 1
    core = core_of(where)
    b_mat, c_mat = joined((b0, b1, b2, b3), core), joined((c0, c1, c2, c3), core)
    inner = dot_cols(c_mat, b_mat)
    allowed = (marks[0, :, 0:1] == segs[0, 0:1, :]) & tri(True)
    xs_f = xs[0].astype(f32)
    step, cum = meta[0, :, 0:8], meta[0, :, 8:16]
    stepped = (xs_f * widen(step)).astype(bf16)
    entering = jnp.where(later, p0[0] * state[0] + first[0], state[0]).astype(bf16)
    entry = widen(jnp.exp(cum) * marks[0, :, 1:2])
    for h in range(OWN_HEADS):
        at = slice(h * SSM_HEAD, (h + 1) * SSM_HEAD)
        mix = (inner * decay_of(meta, row, allowed, h)).astype(bf16)
        work[:, at] = dot(mix, stepped[:, at])
    total = work[...] + dot_cols(c_mat, entering) * entry + skip[0:1, :] * xs_f
    out[0] = total
    gate = gating[0]
    gated = total * gate * sigmoid_of(gate)
    gated_out[0] = gated.astype(bf16)
    square_out[0] = row_sums(gated * gated)


def ssm_forward(where, xs, bc, meta, row, marks, segs, state, first, p0, gating, skip):
    chunks = xs.shape[0]
    return pl.pallas_call(
        ssm_kernel,
        grid_spec=pltpu.PrefetchScalarGridSpec(
            num_scalar_prefetch=1,
            grid=(ROWS, 2),
            in_specs=[time_spec((CHUNK, OWN_SSM))]
            + piece_specs(0)
            + piece_specs(1)
            + [
                time_spec((CHUNK, 32)),
                time_spec((16, CHUNK)),
                time_spec((CHUNK, 8)),
                time_spec((8, CHUNK)),
                slot_spec((OWN_SSM, STATE)),
                slot_spec((OWN_SSM, STATE)),
                slot_spec((OWN_SSM, 1)),
                time_spec((CHUNK, OWN_SSM)),
                pl.BlockSpec((8, OWN_SSM), lambda k, t, where: (0, 0)),
            ],
            out_specs=[
                time_spec((CHUNK, OWN_SSM)),
                time_spec((CHUNK, OWN_SSM)),
                time_spec((8, CHUNK)),
            ],
            scratch_shapes=[pltpu.VMEM((CHUNK, OWN_SSM), f32)],
        ),
        out_shape=[
            jax.ShapeDtypeStruct((chunks, CHUNK, OWN_SSM), f32),
            jax.ShapeDtypeStruct((chunks, CHUNK, OWN_SSM), bf16),
            jax.ShapeDtypeStruct((chunks, 8, CHUNK), f32),
        ],
        compiler_params=pltpu.CompilerParams(vmem_limit_bytes=VMEM),
        cost_estimate=lasting(16),
        name="ssm_forward",
    )(where, xs, bc, bc, bc, bc, bc, bc, bc, bc, meta, row, marks, segs, state, first, p0, gating, skip)


def attention_mask(where, seg_q, seg_k):
    m = pl.program_id(1)
    same = seg_q[...].reshape(HALF, 8)[:, 0:1] == seg_k[0, 0:1, :]
    row = lax.broadcasted_iota(jnp.int32, (HALF, HALF), 0)
    place = lax.rem(row + where[2] * CHUNK, HALF)
    key = lax.broadcasted_iota(jnp.int32, (HALF, HALF), 1)
    return same & ((place >= key) | (m < where[1]))


def slot_keyval(where, own, other):
    mine = pl.program_id(0) // 2 == where[2]
    return jnp.where(mine, own[0, 0], other[0, 0])


def attend_kernel(where, query, kv_own, kv_other, seg_q, seg_k, out, low_out, sum_out, best, total, acc):
    m = pl.program_id(1)
    scale = 1.0 / math.sqrt(ATT_HEAD)

    @pl.when(m == 0)
    def _():
        best[...] = jnp.full_like(best, NEG_BIG)
        total[...] = jnp.zeros_like(total)
        acc[...] = jnp.zeros_like(acc)

    @pl.when(m <= where[1])
    def _():
        q = query[...].reshape(HALF, ATT_HEAD)
        keyval = slot_keyval(where, kv_own, kv_other)
        keys, vals = keyval[:, :ATT_HEAD], keyval[:, ATT_HEAD:]
        scores = jnp.where(attention_mask(where, seg_q, seg_k), dot_cols(q, keys) * scale, NEG_BIG)
        before = best[:, 0:1]
        now = jnp.maximum(before, jnp.max(scores, axis=1, keepdims=True))
        shrink = jnp.exp(before - now)
        weights = jnp.where(scores > 0.5 * NEG_BIG, jnp.exp(scores - now), 0.0)
        total[...] = total[...] * shrink + jnp.sum(weights, axis=1, keepdims=True)
        acc[...] = acc[...] * shrink + dot(weights.astype(bf16), vals)
        best[...] = jnp.broadcast_to(now, best.shape)

    @pl.when(m == pl.num_programs(1) - 1)
    def _():
        context = (acc[...] / total[...]).reshape(2, 1, CHUNK, ATT_HEAD)
        out[...] = context
        low_out[...] = context.astype(bf16)
        sum_out[0] = (best[...] + jnp.log(total[...]))[:, 0:8]


def pair_spec(width):
    return pl.BlockSpec((2, 1, CHUNK, width), lambda k, m, where: (0, k, 0, 0))


def attend(where, query, kv_own, kv_other, seg_q, seg_k):
    slots = kv_own.shape[0]
    keyval_spec = pl.BlockSpec((1, 1, HALF, 2 * ATT_HEAD), lambda k, m, where: (m, k % 2, 0, 0))
    return pl.pallas_call(
        attend_kernel,
        grid_spec=pltpu.PrefetchScalarGridSpec(
            num_scalar_prefetch=1,
            grid=(ROWS, slots),
            in_specs=[
                pair_spec(ATT_HEAD),
                keyval_spec,
                keyval_spec,
                pair_spec(8),
                pl.BlockSpec((1, 8, HALF), lambda k, m, where: (k * slots + m, 0, 0)),
            ],
            out_specs=[
                pair_spec(ATT_HEAD),
                pair_spec(ATT_HEAD),
                pl.BlockSpec((1, HALF, 8), lambda k, m, where: (k, 0, 0)),
            ],
            scratch_shapes=[pltpu.VMEM((HALF, ATT_HEAD), f32)] * 3,
        ),
        out_shape=[
            jax.ShapeDtypeStruct(query.shape, f32),
            jax.ShapeDtypeStruct(query.shape, bf16),
            jax.ShapeDtypeStruct((ROWS, HALF, 8), f32),
        ],
        compiler_params=pltpu.CompilerParams(vmem_limit_bytes=VMEM),
        cost_estimate=lasting(10),
        name="attend",
    )(where, query, kv_own, kv_other, seg_q, seg_k)


def attend_back_kernel(where, query, kv_own, kv_other, seg_q, seg_k, grad, context, sums, query_out, keyval_out):
    m = pl.program_id(1)
    scale = 1.0 / math.sqrt(ATT_HEAD)
    used = m <= where[1]

    @pl.when(m == 0)
    def _():
        query_out[...] = jnp.zeros_like(query_out)

    @pl.when(jnp.logical_not(used))
    def _():
        keyval_out[...] = jnp.zeros_like(keyval_out)

    @pl.when(used)
    def _():
        q = query[...].reshape(HALF, ATT_HEAD)
        g = grad[...].reshape(HALF, ATT_HEAD)
        keyval = slot_keyval(where, kv_own, kv_other)
        keys, vals = keyval[:, :ATT_HEAD], keyval[:, ATT_HEAD:]
        delta = jnp.sum(
            g.astype(f32) * context[...].reshape(HALF, ATT_HEAD), axis=1, keepdims=True
        )
        spread = dot_cols(q, keys) * scale - sums[0, :, 0:1]
        prob = jnp.exp(jnp.where(attention_mask(where, seg_q, seg_k), spread, NEG_BIG))
        slope = (prob * (dot_cols(g, vals) - delta)).astype(bf16)
        part = (dot(slope, keys) * scale).reshape(2, 1, CHUNK, ATT_HEAD)
        query_out[...] = query_out[...] + part
        keyval_out[0, 0, :, :ATT_HEAD] = (dot_rows(slope, q) * scale).astype(bf16)
        keyval_out[0, 0, :, ATT_HEAD:] = dot_rows(prob.astype(bf16), g).astype(bf16)


def attend_back(where, query, kv_own, kv_other, seg_q, seg_k, grad, context, sums):
    slots = kv_own.shape[0]
    keyval_spec = pl.BlockSpec((1, 1, HALF, 2 * ATT_HEAD), lambda k, m, where: (m, k % 2, 0, 0))
    grad_spec = pl.BlockSpec((1, 1, HALF, 2 * ATT_HEAD), lambda k, m, where: (m, k, 0, 0))
    return pl.pallas_call(
        attend_back_kernel,
        grid_spec=pltpu.PrefetchScalarGridSpec(
            num_scalar_prefetch=1,
            grid=(ROWS, slots),
            in_specs=[
                pair_spec(ATT_HEAD),
                keyval_spec,
                keyval_spec,
                pair_spec(8),
                pl.BlockSpec((1, 8, HALF), lambda k, m, where: (k * slots + m, 0, 0)),
                pair_spec(ATT_HEAD),
                pair_spec(ATT_HEAD),
                pl.BlockSpec((1, HALF, 8), lambda k, m, where: (k, 0, 0)),
            ],
            out_specs=[pair_spec(ATT_HEAD), grad_spec],
        ),
        out_shape=[
            jax.ShapeDtypeStruct(query.shape, f32),
            jax.ShapeDtypeStruct((slots, ROWS, HALF, 2 * ATT_HEAD), bf16),
        ],
        compiler_params=pltpu.CompilerParams(vmem_limit_bytes=VMEM),
        cost_estimate=lasting(14),
        name="attend_back",
    )(where, query, kv_own, kv_other, seg_q, seg_k, grad, context, sums)


def gate_back_kernel(
    where, es, scale, gating, ssm_out, c0, c1, c2, c3, meta, marks, p0,
    gy_out, gating_out, unit_out, later_out, both_out,
):
    gate = gating[0]
    sig = sigmoid_of(gate)
    act = gate * sig
    out = ssm_out[0]
    norm = scale[0, :, 0:1]
    unit = out * act * norm
    unit_out[0] = unit.astype(bf16)
    grad = norm * (es[0] - unit * scale[0, :, 1:2])
    gy = (grad * act).astype(bf16)
    gy_out[0] = gy
    gating_out[0] = (grad * out * (sig * (1.0 + gate * (1.0 - sig)))).astype(bf16)
    entry = widen(jnp.exp(meta[0, :, 8:16]) * marks[0, :, 1:2])
    across = (gy.astype(f32) * entry).astype(bf16)
    local = dot_rows(across, joined((c0, c1, c2, c3), core_of(where, True)))

    @pl.when(pl.program_id(1) == 0)
    def _():
        later_out[0] = local

    @pl.when(pl.program_id(1) == 1)
    def _():
        both_out[0] = p0[0] * later_out[0] + local


def gate_back(where, es, scale, gating, ssm_out, bc, meta, marks, p0):
    chunks = gating.shape[0]
    wide = time_spec((CHUNK, OWN_SSM), True)
    state = jax.ShapeDtypeStruct((ROWS, OWN_SSM, STATE), f32)
    token = jax.ShapeDtypeStruct((chunks, CHUNK, OWN_SSM), bf16)
    return pl.pallas_call(
        gate_back_kernel,
        grid_spec=pltpu.PrefetchScalarGridSpec(
            num_scalar_prefetch=1,
            grid=(ROWS, 2),
            in_specs=[wide, time_spec((CHUNK, 8), True), wide, wide]
            + piece_specs(1)
            + [
                time_spec((CHUNK, 32), True),
                time_spec((CHUNK, 8), True),
                slot_spec((OWN_SSM, 1)),
            ],
            out_specs=[wide, wide, wide, slot_spec((OWN_SSM, STATE)), slot_spec((OWN_SSM, STATE))],
        ),
        out_shape=[token, token, token, state, state],
        compiler_params=pltpu.CompilerParams(vmem_limit_bytes=VMEM),
        cost_estimate=lasting(11),
        name="gate_back",
    )(where, es, scale, gating, ssm_out, bc, bc, bc, bc, meta, marks, p0)


def ssm_back_kernel(
    where, xs, gy, b0, b1, b2, b3, c0, c1, c2, c3, meta, row, marks, segs, state, first, flow, later,
    p0, p1, skip, head,
    xs_out, o00, o01, o02, o03, o10, o11, o12, o13, step_out, sums_out, work,
):
    early = pl.program_id(1) == 1
    core = core_of(where, True)
    b_mat, c_mat = joined((b0, b1, b2, b3), core), joined((c0, c1, c2, c3), core)
    inner = dot_cols(b_mat, c_mat)
    allowed = (marks[0, :, 0:1] == segs[0, 0:1, :]) & tri(False)
    xs_f = xs[0].astype(f32)
    gy_low = gy[0]
    gy_f = gy_low.astype(f32)
    step, cum, tail_decay, tail = tails_of(meta, marks)
    step_wide, tail_wide = widen(step), widen(tail)
    entry = widen(jnp.exp(cum) * marks[0, :, 1:2])
    stepped = (xs_f * step_wide).astype(bf16)
    grad_inner = jnp.zeros((CHUNK, CHUNK), f32)
    read = jnp.zeros((CHUNK, 8), f32)
    reads = jnp.zeros((8, CHUNK), f32)
    lane = lax.broadcasted_iota(jnp.int32, (CHUNK, 8), 1)
    sublane = lax.broadcasted_iota(jnp.int32, (8, CHUNK), 0)
    for h in range(OWN_HEADS):
        at = slice(h * SSM_HEAD, (h + 1) * SSM_HEAD)
        spread = row[0, 8 + h : 9 + h, :] - meta[0, :, 8 + h : 9 + h]
        decay = jnp.exp(jnp.where(allowed, spread, NEG_BIG))
        slope = decay * dot_cols(stepped[:, at], gy_low[:, at])
        grad_inner = grad_inner + slope
        flow_low = (slope * inner).astype(bf16)
        read = read + dot(flow_low, (lane == h).astype(bf16))
        reads = reads + dot((sublane == h).astype(bf16), flow_low)
        work[:, at] = dot((inner * decay).astype(bf16), gy_low[:, at])
    reads = jnp.concatenate([reads, jnp.zeros((120, CHUNK), f32)], axis=0).T
    flows = reads[:, :8] - read
    from_mix = work[...]
    entering = jnp.where(early, state[0], p0[0] * state[0] + first[0])
    leaving = jnp.where(early, p1[0] * flow[0] + later[0], flow[0])
    leaving_low = leaving.astype(bf16)
    inner_low = grad_inner.astype(bf16)
    across = (gy_f * entry).astype(bf16)
    weighted = (xs_f * tail_wide).astype(bf16)
    grad_b = dot(inner_low, c_mat) + dot(weighted, leaving_low)
    grad_c = dot_rows(inner_low, b_mat) + dot(across, entering.astype(bf16))
    from_state = dot_cols(b_mat, leaving_low)
    skip_row = skip[0:1, :]
    xs_out[0] = skip_row * gy_f + step_wide * from_mix + tail_wide * from_state
    low_first = where[0] < 2
    lower = jnp.where(low_first, grad_b, grad_c).astype(bf16)
    upper = jnp.where(low_first, grad_c, grad_b).astype(bf16)
    for ref, value, i in (
        (o00, lower, 0), (o10, lower, 1), (o01, lower, 2), (o11, lower, 3),
        (o02, upper, 0), (o12, upper, 1), (o03, upper, 2), (o13, upper, 3),
    ):
        for half in range(2):

            @pl.when(core ^ (i % 2) == half)
            def _():
                ref[0, :, half * PIECE : (half + 1) * PIECE] = value[:, i * PIECE : (i + 1) * PIECE]

    entering_low = entering.astype(bf16)
    entry_sum = narrow(gy_f * (dot_cols(c_mat, entering_low) * entry))
    step_sum = narrow(xs_f * from_mix)
    tail_sum = narrow(xs_f * from_state)
    skip_sum = narrow(gy_f * xs_f)
    tail_flow = tail_sum * tail
    passed = jnp.sum(leaving * entering, axis=1, keepdims=True)
    passed = jnp.broadcast_to(passed, (OWN_SSM, 8))
    own_head = head_map(OWN_SSM, 8, 0).astype(f32)
    grad_pass = jnp.sum(passed * own_head, axis=0, keepdims=True)
    passing = jnp.exp(cum[CHUNK - 1 : CHUNK]) * marks[0, CHUNK - 1 : CHUNK, 1:2]
    end = grad_pass * passing + jnp.sum(tail_flow, axis=0, keepdims=True)
    last = lax.broadcasted_iota(jnp.int32, (CHUNK, 8), 0) == CHUNK - 1
    grad_cum = flows + entry_sum - tail_flow + jnp.where(last, end, 0.0)
    grad_rate = exact(tri(False), grad_cum)
    grad_step = step_sum + tail_sum * tail_decay + grad_rate * head[1:2, 0:8]
    raw = grad_step * meta[0, :, 16:24]
    step_out[0] = raw
    sums = [raw, grad_rate * step, skip_sum]
    sums_out[0] = jnp.concatenate(
        [jnp.sum(v, axis=0, keepdims=True) for v in sums] + [jnp.zeros((5, 8), f32)], axis=0
    )


def ssm_back(where, xs, gy, bc, meta, row, marks, segs, state, first, flow, later, p0, p1, skip, head):
    chunks = xs.shape[0]
    wide = time_spec((CHUNK, OWN_SSM), True)
    kept = slot_spec((OWN_SSM, STATE))
    column = slot_spec((OWN_SSM, 1))

    def owner(slot):
        return pl.BlockSpec((1, CHUNK, 2 * PIECE), lambda k, t, where: (k ^ slot, 0, 0))

    piece = jax.ShapeDtypeStruct((ROWS, CHUNK, 2 * PIECE), bf16)
    return pl.pallas_call(
        ssm_back_kernel,
        grid_spec=pltpu.PrefetchScalarGridSpec(
            num_scalar_prefetch=1,
            grid=(ROWS, 2),
            in_specs=[wide, wide]
            + piece_specs(0)
            + piece_specs(1)
            + [
                time_spec((CHUNK, 32), True),
                time_spec((16, CHUNK), True),
                time_spec((CHUNK, 8), True),
                time_spec((8, CHUNK), True),
                kept,
                kept,
                kept,
                kept,
                column,
                column,
                pl.BlockSpec((8, OWN_SSM), lambda k, t, where: (0, 0)),
                pl.BlockSpec((8, 128), lambda k, t, where: (0, 0)),
            ],
            out_specs=[wide]
            + [owner(m) for r in range(2) for m in range(ROWS)]
            + [time_spec((CHUNK, 8), True), time_spec((8, 8), True)],
            scratch_shapes=[pltpu.VMEM((CHUNK, OWN_SSM), f32)],
        ),
        out_shape=[jax.ShapeDtypeStruct((chunks, CHUNK, OWN_SSM), f32)]
        + [piece] * 8
        + [
            jax.ShapeDtypeStruct((chunks, CHUNK, 8), f32),
            jax.ShapeDtypeStruct((chunks, 8, 8), f32),
        ],
        compiler_params=pltpu.CompilerParams(vmem_limit_bytes=VMEM),
        cost_estimate=lasting(30),
        name="ssm_back",
    )(
        where, xs, gy, bc, bc, bc, bc, bc, bc, bc, bc, meta, row, marks, segs, state, first, flow,
        later, p0, p1, skip, head,
    )


def conv_back_kernel(grad_xs, grad_bc, step, slope, proj, halo, marks, returned, conv, out, sums_out, ext, back):
    ext[0:8, :] = halo[0]
    ext[8:, :] = proj[0].astype(bf16).astype(f32)
    rest = jnp.zeros((CHUNK, LANES_A - OWN_CONV), f32)
    both = grad_bc[0]
    own_bc = jnp.where(pl.program_id(0) < ROWS, both[:, :PIECE], both[:, PIECE:])
    grad = jnp.concatenate([grad_xs[0], own_bc, rest], axis=1) * slope[0]
    sums = []
    back[...] = jnp.zeros_like(back)
    back[CHUNK : CHUNK + 8, :] = returned[0]
    for o in range(CONV):
        masked = grad if o == CONV - 1 else grad * marks[0, :, 3 + o : 4 + o]
        sums.append(jnp.sum(masked * ext[5 + o : 5 + o + CHUNK, :], axis=0, keepdims=True))
        back[5 + o : 5 + o + CHUNK, :] = (
            back[5 + o : 5 + o + CHUNK, :] + masked * conv[o : o + 1, :]
        )
    sums.append(jnp.sum(grad, axis=0, keepdims=True))
    sums_out[0] = jnp.concatenate(sums + [jnp.zeros((3, LANES_A), f32)], axis=0)
    mixed = back[8 : 8 + CHUNK, :]
    out[0] = mixed.astype(bf16)
    out[0, :, STEP_AT : STEP_AT + 8] = step[0].astype(bf16)


def conv_backward(grad_xs, grad_bc, step, slope, proj, halo, marks, returned, conv):
    chunks = proj.shape[0]
    block = lambda *shape: pl.BlockSpec((1,) + shape, lambda q: (q, 0, 0))
    return pl.pallas_call(
        conv_back_kernel,
        grid=(chunks,),
        in_specs=[
            block(CHUNK, OWN_SSM),
            pl.BlockSpec((1, CHUNK, 2 * PIECE), lambda q: (lax.rem(q, ROWS), 0, 0)),
            block(CHUNK, 8),
            block(CHUNK, LANES_A),
            block(CHUNK, LANES_A),
            block(8, LANES_A),
            block(CHUNK, 8),
            block(8, LANES_A),
            pl.BlockSpec((8, LANES_A), lambda q: (0, 0)),
        ],
        out_specs=[block(CHUNK, LANES_A), block(8, LANES_A)],
        out_shape=[
            jax.ShapeDtypeStruct((chunks, CHUNK, LANES_A), bf16),
            jax.ShapeDtypeStruct((chunks, 8, LANES_A), f32),
        ],
        scratch_shapes=[pltpu.VMEM((8 + CHUNK, LANES_A), f32)] * 2,
        compiler_params=pltpu.CompilerParams(vmem_limit_bytes=VMEM),
        cost_estimate=lasting(6),
        name="conv_backward",
    )(grad_xs, grad_bc, step, slope, proj, halo, marks, returned, conv)


LARGE = VMEM


def fetch(pieces, held, arrived):
    starts = starts_of(pieces)
    copies = []
    for i, piece in enumerate(pieces):
        at = pl.ds(starts[i], piece.shape[0])
        copies.append(pltpu.make_async_copy(piece, held.at[at], arrived.at[i]))
        copies[-1].start()
    return copies, starts


def by_chunk(copies, starts):
    for i in range(8):
        for j, copy in enumerate(copies):
            if i * CHUNK < starts[j + 1] <= (i + 1) * CHUNK:
                copy.wait()
        yield i, slice(i * CHUNK, (i + 1) * CHUNK)


def times_kernel(count, *refs):
    pieces, (weight, out, held, arrived) = refs[:count], refs[count:]
    for i, at in by_chunk(*fetch(pieces, held, arrived)):
        out[i] = dot(held[at, :], weight[...])


def times(pieces, weight):
    width, cols = weight.shape
    count = len(pieces)
    return pl.pallas_call(
        lambda *refs: times_kernel(count, *refs),
        in_specs=[ANY] * count + [IN_VMEM],
        out_specs=IN_VMEM,
        out_shape=jax.ShapeDtypeStruct((8, CHUNK, cols), f32),
        scratch_shapes=[pltpu.VMEM((8 * CHUNK, width), bf16), pltpu.SemaphoreType.DMA((count,))],
        compiler_params=pltpu.CompilerParams(vmem_limit_bytes=LARGE),
        cost_estimate=lasting(5 + cols / 80),
        name="times",
    )(*pieces, weight)


def mixer_back_kernel(count, *refs):
    pieces = refs[:count]
    w_out, w_ctx, ssm_out, gating, es_out, context_out, sum_out, held, arrived = refs[count:]
    for i, at in by_chunk(*fetch(pieces, held, arrived)):
        es = dot_cols(held[at, :], w_out[...])
        es_out[i] = es
        context_out[i] = dot_cols(held[at, :], w_ctx[...]).astype(bf16)
        gate = gating[i]
        sum_out[i] = row_sums(es * ssm_out[i] * gate * sigmoid_of(gate))


def mixer_back(pieces, w_out, w_ctx, ssm_out, gating):
    count, width = len(pieces), w_out.shape[1]
    return pl.pallas_call(
        lambda *refs: mixer_back_kernel(count, *refs),
        in_specs=[ANY] * count + [IN_VMEM] * 4,
        out_specs=[IN_VMEM] * 3,
        out_shape=[
            jax.ShapeDtypeStruct((8, CHUNK, OWN_SSM), f32),
            jax.ShapeDtypeStruct((8, CHUNK, ATT_HEAD), bf16),
            jax.ShapeDtypeStruct((8, 8, CHUNK), f32),
        ],
        scratch_shapes=[pltpu.VMEM((8 * CHUNK, width), bf16), pltpu.SemaphoreType.DMA((count,))],
        compiler_params=pltpu.CompilerParams(vmem_limit_bytes=LARGE),
        cost_estimate=lasting(13),
        name="mixer_back",
    )(*pieces, w_out, w_ctx, ssm_out, gating)


def weight_grad_kernel(*refs):
    left, pieces, out = refs[0], refs[1:-1], refs[-1]
    starts = starts_of(pieces)
    total = dot(left[:, : starts[1]], pieces[0][...])
    for i in range(1, len(pieces)):
        total = total + dot(left[:, starts[i] : starts[i + 1]], pieces[i][...])
    out[...] = total.astype(bf16).reshape(out.shape)


def weight_grad(left, pieces, by_part=0):
    cols, rows = left.shape
    width = pieces[0].shape[1]
    parts = by_part or 4
    part = width // parts
    if by_part:
        out_spec = pl.BlockSpec((1, cols, part), lambda i: (i, 0, 0))
        out_shape = jax.ShapeDtypeStruct((parts, cols, part), bf16)
    else:
        out_spec = pl.BlockSpec((cols, part), lambda i: (0, i))
        out_shape = jax.ShapeDtypeStruct((cols, width), bf16)
    return pl.pallas_call(
        weight_grad_kernel,
        grid=(parts,),
        in_specs=[pl.BlockSpec((cols, rows), lambda i: (0, 0))]
        + [pl.BlockSpec((piece.shape[0], part), lambda i: (0, i)) for piece in pieces],
        out_specs=out_spec,
        out_shape=out_shape,
        compiler_params=pltpu.CompilerParams(vmem_limit_bytes=LARGE),
        cost_estimate=lasting(4 + cols / 100),
        name="weight_grad",
    )(left, *pieces)


def terms_kernel(count, turned, adds, scaled_by, *refs):
    lefts, weights = refs[:count], refs[count : 2 * count]
    rest = refs[2 * count :]
    norm = rest[0] if scaled_by else None
    got = rest[int(scaled_by) : int(scaled_by) + adds]
    outs = rest[int(scaled_by) + adds :]
    rows = outs[0].shape[0]
    half = rows // 2
    for k in range(ROWS):
        at = slice(k * rows, (k + 1) * rows)
        total = None
        for i in range(count):
            product = (dot_cols if turned else dot)(lefts[i][at, :], weights[i][...])
            if i == 0 and scaled_by:
                product = product * norm[at, 0:1]
            total = product if total is None else total + product
        if adds:
            total = total + got[k][...].astype(f32)
        if adds and k == 3:
            outs[3][...] = total[:half].astype(bf16)
            outs[4][...] = total[half:].astype(bf16)
        else:
            outs[k][...] = total.astype(outs[k].dtype)


def group_terms(lefts, weights, turned, core, got=(), norm=None):
    width = weights[0].shape[0 if turned else 1]
    rows = lefts[0].shape[0] // 8
    block = min(width, 512)
    in_specs = [
        pl.BlockSpec((ROWS * rows, left.shape[1]), lambda i, core=core: (core, 0)) for left in lefts
    ]
    for weight in weights:
        if turned:
            in_specs.append(pl.BlockSpec((block, weight.shape[1]), lambda i: (i, 0)))
        else:
            in_specs.append(pl.BlockSpec((weight.shape[0], block), lambda i: (0, i)))
    operands = list(lefts) + list(weights)
    if norm is not None:
        in_specs.append(pl.BlockSpec((ROWS * rows, 8), lambda i, core=core: (core, 0)))
        operands.append(norm)
    piece = pl.BlockSpec((rows, block), lambda i: (0, i))
    in_specs += [piece] * len(got)
    kinds = [(rows, f32)] * 3 + [(rows // 2, bf16)] * 2 if got else [(rows, bf16)] * 4
    depth = sum(left.shape[1] for left in lefts)
    return pl.pallas_call(
        lambda *refs: terms_kernel(len(lefts), turned, len(got), norm is not None, *refs),
        grid=(width // block,),
        in_specs=in_specs,
        out_specs=[pl.BlockSpec((n, block), lambda i: (0, i)) for n, _ in kinds],
        out_shape=[jax.ShapeDtypeStruct((n, width), kind) for n, kind in kinds],
        compiler_params=pltpu.CompilerParams(vmem_limit_bytes=LARGE),
        cost_estimate=lasting(4 + depth / 180),
        name="group_terms",
    )(*operands, *got)


def scatter_product(lefts, weights, turned=False, norm=None, give=False, meanwhile=None):
    other = group_terms(lefts, weights, turned, 1, norm=norm)
    got = [twin(part) for part in other]
    own, for_x, for_y, far_a, far_b = group_terms(lefts, weights, turned, 0, got=got, norm=norm)
    to_x, to_y = hop(far_a, 2), hop(far_b, 1)
    done = None
    if meanwhile is not None:
        done = meanwhile(own)
        to_x, to_y, done = lax.optimization_barrier((to_x, to_y, done))
    by_x, by_y = fold(for_x, for_y, to_x, to_y)
    sums = own, hop(by_x, 1), hop(by_y, 2)
    return (sums, done, own, by_x) if give else sums


def fold_kernel(for_x, for_y, to_x, to_y, by_x, by_y):
    half = to_x.shape[0]
    by_x[:half, :] = (for_x[:half, :] + to_x[...].astype(f32)).astype(bf16)
    by_x[half:, :] = for_x[half:, :].astype(bf16)
    by_y[:half, :] = for_y[:half, :].astype(bf16)
    by_y[half:, :] = (for_y[half:, :] + to_y[...].astype(f32)).astype(bf16)


def fold(for_x, for_y, to_x, to_y):
    rows, width = for_x.shape
    block = min(width, 512)
    spec = lambda n: pl.BlockSpec((n, block), lambda i: (0, i))
    return pl.pallas_call(
        fold_kernel,
        grid=(width // block,),
        in_specs=[spec(rows), spec(rows), spec(rows // 2), spec(rows // 2)],
        out_specs=[spec(rows), spec(rows)],
        out_shape=[jax.ShapeDtypeStruct((rows, width), bf16)] * 2,
        compiler_params=pltpu.CompilerParams(vmem_limit_bytes=VMEM),
        cost_estimate=lasting(2),
        name="fold",
    )(for_x, for_y, to_x, to_y)


def regroup(values, outer, part):
    count = values.shape[1] // part
    if count == 1:
        return values
    inner = count // outer
    order = [o * inner + i for i in range(inner) for o in range(outer)]
    return jnp.concatenate([values[:, k * part : (k + 1) * part] for k in order], axis=1)


def scaled_unit(values):
    scale = lax.rsqrt(jnp.mean(values * values, axis=1, keepdims=True) + EPSILON)
    return values * scale, scale


def norm_in_kernel(part, x, out):
    unit, _ = scaled_unit(x[...].astype(f32))
    out[...] = regroup(unit, ROWS, part).astype(bf16)


def norm_two_kernel(part, x, own, by_x, by_y, hidden_out, out):
    hidden = x[...].astype(f32) + own[...] + by_x[...].astype(f32) + by_y[...].astype(f32)
    hidden_out[...] = hidden
    unit, _ = scaled_unit(hidden)
    out[...] = regroup(unit, ROWS, part).astype(bf16)


def norm_back_kernel(part, values, own, by_x, by_y, base, *outs):
    unit, scale = scaled_unit(values[...].astype(f32))
    grad = own[...] + by_x[...].astype(f32) + by_y[...].astype(f32)
    grad = regroup(grad, grad.shape[1] // part // ROWS, part)
    mean = jnp.mean(grad * unit, axis=1, keepdims=True)
    total = base[...].astype(f32) + scale * (grad - unit * mean)
    for out in outs:
        out[...] = total.astype(out.dtype)


def on_rows(kernel, part, operands, kinds, name):
    rows, width = operands[0].shape
    step = rows // 4
    spec = pl.BlockSpec((step, width), lambda i: (i, 0))
    return pl.pallas_call(
        lambda *refs: kernel(part, *refs),
        grid=(4,),
        in_specs=[spec] * len(operands),
        out_specs=[spec] * len(kinds),
        out_shape=[jax.ShapeDtypeStruct((rows, width), kind) for kind in kinds],
        compiler_params=pltpu.CompilerParams(vmem_limit_bytes=VMEM),
        cost_estimate=lasting(4),
        name=name,
    )(*operands)


def turn(values, cosine, sine):
    return values * cosine + pltpu.roll(values, ATT_HEAD // 2, 1) * sine


def rope_kernel(where, query, key, value, cosine, sine, query_out, keyval_out):
    query_out[0, 0] = turn(query[0], cosine[0], sine[0]).astype(bf16)
    keyval_out[0, 0, :, :ATT_HEAD] = turn(key[0], cosine[0], sine[0]).astype(bf16)
    keyval_out[0, 0, :, ATT_HEAD:] = value[0].astype(bf16)


def rope_forward(where, proj, cosine, sine):
    def part(i):
        return pl.BlockSpec(
            (1, CHUNK, ATT_HEAD), lambda k, t, where: ((t ^ where[2]) * ROWS + k, 0, 4 + i)
        )

    angle = pl.BlockSpec((1, CHUNK, ATT_HEAD), lambda k, t, where: (t ^ where[2], 0, 0))
    return pl.pallas_call(
        rope_kernel,
        grid_spec=pltpu.PrefetchScalarGridSpec(
            num_scalar_prefetch=1,
            grid=(ROWS, 2),
            in_specs=[part(0), part(1), part(2), angle, angle],
            out_specs=[
                pl.BlockSpec((1, 1, CHUNK, ATT_HEAD), lambda k, t, where: (t ^ where[2], k, 0, 0)),
                pl.BlockSpec((1, 1, CHUNK, 2 * ATT_HEAD), lambda k, t, where: (k, t, 0, 0)),
            ],
        ),
        out_shape=[
            jax.ShapeDtypeStruct((2, ROWS, CHUNK, ATT_HEAD), bf16),
            jax.ShapeDtypeStruct((ROWS, 2, CHUNK, 2 * ATT_HEAD), bf16),
        ],
        compiler_params=pltpu.CompilerParams(vmem_limit_bytes=VMEM),
        cost_estimate=lasting(3),
        name="rope_forward",
    )(where, proj, proj, proj, cosine, sine)


def rope_back_kernel(where, query, keyval, cosine, sine, out):
    core, turned = cosine[0], -sine[0]
    out[0, :, :ATT_HEAD] = turn(query[0, 0], core, turned).astype(bf16)
    mine = pl.program_id(0) // 2 == where[2]
    both = jnp.where(mine, keyval[0, 0], 0.0)
    out[0, :, ATT_HEAD : 2 * ATT_HEAD] = turn(both[:, :ATT_HEAD], core, turned).astype(bf16)
    out[0, :, 2 * ATT_HEAD :] = both[:, ATT_HEAD:].astype(bf16)


def rope_back(where, query, keyval, cosine, sine):
    angle = pl.BlockSpec((1, CHUNK, ATT_HEAD), lambda k, t, where: (t ^ where[2], 0, 0))
    return pl.pallas_call(
        rope_back_kernel,
        grid_spec=pltpu.PrefetchScalarGridSpec(
            num_scalar_prefetch=1,
            grid=(ROWS, 2),
            in_specs=[
                pl.BlockSpec((1, 1, CHUNK, ATT_HEAD), lambda k, t, where: (t ^ where[2], k, 0, 0)),
                pl.BlockSpec((1, 1, CHUNK, 2 * ATT_HEAD), lambda k, t, where: (k % 2, t, 0, 0)),
                angle,
                angle,
            ],
            out_specs=pl.BlockSpec(
                (1, CHUNK, 3 * ATT_HEAD), lambda k, t, where: ((t ^ where[2]) * ROWS + k, 0, 0)
            ),
        ),
        out_shape=jax.ShapeDtypeStruct((2 * ROWS, CHUNK, 3 * ATT_HEAD), bf16),
        compiler_params=pltpu.CompilerParams(vmem_limit_bytes=VMEM),
        cost_estimate=lasting(3),
        name="rope_back",
    )(where, query, keyval, cosine, sine)


def feed_kernel(count, *refs):
    n2, g = refs[:count], refs[count : 2 * count]
    w_gu, w_down, act_out, grad_out, held_n, held_g, arrived_n, arrived_g = refs[2 * count :]
    copies_n, starts = fetch(n2, held_n, arrived_n)
    copies_g, _ = fetch(g, held_g, arrived_g)
    own = w_down.shape[0]
    for (i, at), _ in zip(by_chunk(copies_n, starts), by_chunk(copies_g, starts)):
        both = dot(held_n[at, :], w_gu[...])
        gate, up = both[:, :own], both[:, own:]
        sig = sigmoid_of(gate)
        silu = gate * sig
        act_out[at, :] = (silu * up).astype(bf16)
        grad = dot_cols(held_g[at, :], w_down[...])
        grad_out[at, :own] = (grad * up * (sig * (1.0 + gate * (1.0 - sig)))).astype(bf16)
        grad_out[at, own:] = (grad * silu).astype(bf16)


def feed(n2, g, w_gu, w_down):
    own, width = w_down.shape
    count, rows = len(n2), 8 * CHUNK
    return pl.pallas_call(
        lambda *refs: feed_kernel(count, *refs),
        in_specs=[ANY] * (2 * count) + [IN_VMEM] * 2,
        out_specs=[IN_VMEM] * 2,
        out_shape=[
            jax.ShapeDtypeStruct((rows, own), bf16),
            jax.ShapeDtypeStruct((rows, 2 * own), bf16),
        ],
        scratch_shapes=[
            pltpu.VMEM((rows, width), bf16),
            pltpu.VMEM((rows, width), bf16),
            pltpu.SemaphoreType.DMA((count,)),
            pltpu.SemaphoreType.DMA((count,)),
        ],
        compiler_params=pltpu.CompilerParams(vmem_limit_bytes=LARGE),
        cost_estimate=lasting(23),
        name="feed",
    )(*n2, *g, w_gu, w_down)


def per_device(
    tokens,
    segments,
    cotangent,
    norm_gain,
    gating_weight,
    input_weight,
    state_weight,
    step_weight,
    conv_weight,
    conv_bias,
    step_bias,
    decay_log,
    skip_gain,
    ssm_gain,
    out_weight,
    query_weight,
    keyval_weight,
    context_weight,
    mlp_gain,
    gate_weight,
    up_weight,
    down_weight,
):
    zs = lax.axis_size("z")
    b = lax.axis_index("b")
    z = lax.axis_index("z")
    c = lax.axis_index("c")
    rank = 2 * b + c
    rows = tokens.shape[1]
    width = tokens.shape[2]
    share = norm_gain.shape[0]
    ssm_width = HEADS * SSM_HEAD
    score_scale = 1.0 / math.sqrt(ATT_HEAD)

    def to_z(values):
        return (
            values.reshape(rows, ROWS, zs, 2 * share).transpose(0, 2, 1, 3).reshape(rows, width)
        )

    def from_z(values):
        return (
            values.reshape(rows, zs, ROWS, 2 * share).transpose(0, 2, 1, 3).reshape(rows, width)
        )

    def swap(values):
        return jnp.where(c == 0, values, values[::-1])

    def to_ranks(values):
        return lax.all_to_all(values, ("b", "c"), split_axis=0, concat_axis=0, tiled=True)

    def to_owner(values):
        mine = lax.psum_scatter(values, "z", scatter_dimension=0, tiled=True)[0]
        return mine.T.reshape(RANKS, share, -1)

    def along_z(values):
        return lax.all_gather(values, "z", axis=0, tiled=True)

    def owner_z(values):
        return lax.psum_scatter(values, "z", scatter_dimension=0, tiled=True)

    x = tokens[0]
    cot = cotangent[0]
    aligned = 2 * share % 128 == 0
    block = 2 * share if aligned else width
    lined = (lambda v: v) if aligned else to_z
    unlined = (lambda v: v) if aligned else from_z
    gain_col = norm_gain.astype(f32)[:, None]
    gain2_col = mlp_gain.astype(f32)[:, None]
    ssm_gain_col = ssm_gain.astype(f32)[:, None]

    (n1_own,) = on_rows(norm_in_kernel, block, [x], [bf16], "norm_in")
    scaled = lambda w, gain: (w.astype(f32) * gain).astype(bf16)
    by_rank = lambda w: w.reshape(w.shape[0], RANKS, -1).transpose(1, 0, 2)
    group_kv = KVHEADS * ATT_HEAD
    kv_heads = keyval_weight.reshape(share, 2, KVHEADS, ATT_HEAD).transpose(2, 0, 1, 3)
    kv_rank = jnp.repeat(kv_heads.reshape(KVHEADS, share, 2 * ATT_HEAD), RANKS // KVHEADS, axis=0)
    pad_cols = 128 - OWN_STATE - 8
    chan = conv_bias.shape[0]
    small = jnp.concatenate(
        [segments[0].astype(bf16), conv_weight.reshape(-1), conv_bias.reshape(-1)]
    )
    small_count = small.shape[0]
    small = jnp.pad(small, (0, share * pad_cols - small_count)).reshape(share, pad_cols)
    w_a = jnp.concatenate(
        [
            by_rank(input_weight),
            by_rank(state_weight),
            by_rank(step_weight),
            jnp.zeros((RANKS, share, 8 - OWN_HEADS), bf16),
        ],
        axis=2,
    )
    riders = jnp.broadcast_to(small[None], (RANKS, share, pad_cols))
    w_b = jnp.concatenate([by_rank(query_weight), kv_rank], axis=2)
    w_c = by_rank(gating_weight)
    cols_a, cols_b, cols_c = w_a.shape[2] + pad_cols, w_b.shape[2], w_c.shape[2]
    own_ab = to_ranks(
        jnp.concatenate([scaled(w_a, gain_col[None]), riders, scaled(w_b, gain_col[None])], axis=2)
    )
    w_ab = along_z(own_ab)
    small = w_ab[..., cols_a - pad_cols : cols_a].reshape(zs, ROWS, 2, -1)[..., :small_count]
    w_ab = w_ab.reshape(width, cols_a + cols_b)
    wa, wb = w_ab[:, :cols_a], w_ab[:, cols_a:]
    def ff_ranks(w):
        return (
            w.reshape(w.shape[0], ROWS, zs, 2, -1)
            .transpose(1, 3, 0, 2, 4)
            .reshape(RANKS, w.shape[0], -1)
        )

    w_cgu = jnp.concatenate(
        [
            scaled(w_c, gain_col[None]),
            scaled(
                jnp.concatenate([ff_ranks(gate_weight), ff_ranks(up_weight)], axis=2),
                gain2_col[None],
            ),
        ],
        axis=2,
    )
    n1, w_cgu = gather_group(lined(n1_own), w_cgu)
    own_cgu = to_ranks(w_cgu)
    own_c, w_gu = own_cgu[..., :cols_c], own_cgu[..., cols_c:]
    own_ff = w_gu.shape[2] // 2

    row_out = out_weight.shape[0]
    row_ctx = context_weight.shape[0]
    w_oc = jnp.concatenate([scaled(out_weight, ssm_gain_col), context_weight], axis=0)[None]
    segs = small[..., :rows].transpose(1, 0, 2, 3).reshape(ROWS, zs * 2 * rows).astype(f32)
    segs_all = jnp.concatenate(
        [lax.dynamic_slice_in_dim(segs, k ^ b, 1, 0) for k in range(ROWS)], axis=0
    )
    conv_all = small[..., rows:].transpose(1, 0, 2, 3).reshape(-1, CONV + 1, chan).astype(f32)
    conv_all = conv_all.transpose(1, 0, 2).reshape(CONV + 1, -1)
    conv_own = jnp.concatenate(
        [
            lax.dynamic_slice_in_dim(conv_all, rank * OWN_SSM, OWN_SSM, 1),
            lax.dynamic_slice_in_dim(conv_all, ssm_width + rank * OWN_STATE, OWN_STATE, 1),
        ],
        axis=1,
    )
    seg_pad = jnp.concatenate([jnp.zeros((ROWS, rows), f32), segs_all], axis=1)
    seg_near = lax.dynamic_slice_in_dim(seg_pad, z * 2 * rows, 3 * rows, 1)
    seg_time = seg_near[:, rows:].reshape(ROWS, 2, rows).transpose(1, 0, 2)
    seg = swap(seg_time).reshape(2 * ROWS, rows)
    seg_before = seg_near[:, : 2 * rows].reshape(ROWS, 2, rows).transpose(1, 0, 2)
    seg_before = swap(seg_before).reshape(2 * ROWS, rows)
    marks = marks_of(seg, seg_before)
    seg_rows = jnp.broadcast_to(seg[:, None, :], (2 * ROWS, 8, rows))
    seg_query = marks.reshape(2, ROWS, rows, 8)
    seg_keys = segs_all.reshape(ROWS * zs, 1, 2 * rows)
    seg_keys = jnp.broadcast_to(seg_keys, (ROWS * zs, 8, 2 * rows))
    where = jnp.stack([b, z, c]).astype(jnp.int32)
    conv_own = jnp.pad(conv_own, ((0, 3), (0, LANES_A - OWN_CONV)))
    own_slice = lambda v: lax.dynamic_slice_in_dim(v.astype(f32), rank * OWN_HEADS, OWN_HEADS, 0)
    rate = -jnp.exp(own_slice(decay_log))
    head = jnp.pad(jnp.stack([own_slice(step_bias), rate]), ((0, 6), (0, 128 - OWN_HEADS)))
    skip_wide = jnp.broadcast_to(jnp.repeat(own_slice(skip_gain), SSM_HEAD)[None], (8, OWN_SSM))

    half_head = ATT_HEAD // 2
    frequency = jnp.exp(jnp.arange(half_head, dtype=f32) * (-2.0 * math.log(ROPE_BASE) / ATT_HEAD))
    core_place = (z * 2 + (jnp.arange(2) ^ c)) * rows
    places = (core_place[:, None] + jnp.arange(rows)[None, :]).astype(f32)
    angles = (places[:, :, None] * frequency).reshape(2, rows, half_head)
    cosine, sine = jnp.cos(angles), jnp.sin(angles)
    cosine = jnp.concatenate([cosine, cosine], axis=-1)
    sine = jnp.concatenate([-sine, sine], axis=-1)

    chunks = 2 * ROWS
    proj = times(n1, after(w_ab, own_cgu))
    g_all, proj = gather_group(after(cot, own_cgu), proj)
    query, keyval = rope_forward(where, proj, cosine, sine)
    own_kv = lax.dynamic_slice_in_dim(keyval, 2 * c, 2, 0).reshape(1, 2, 2 * rows, 2 * ATT_HEAD)
    kv_own = along_z(own_kv)

    def before_chunk(own_last, moved):
        return jnp.stack(
            [jnp.where(c == 0, moved, own_last[1]), jnp.where(c == 0, own_last[0], moved)]
        )

    tails = after(proj[:, rows - 8 :, :cols_a], where)
    tails = tails.reshape(2, ROWS, 8, cols_a).astype(bf16)
    last_core = jnp.where(c == 0, tails[1], tails[0])
    moved = zshift(last_core[:, 8 - CONV + 1 :], 1)
    moved = jnp.pad(moved, ((0, 0), (8 - CONV + 1, 0), (0, 0)))
    halo = before_chunk(tails, moved).reshape(chunks, 8, cols_a).astype(f32)
    xs, bc_own, slope, meta, meta_rows = conv_forward(proj, halo, marks, conv_own, head)
    bc_own = after(bc_own, *g_all)
    mine = [bc_own] + [hop(bc_own, m) for m in range(1, ROWS)]
    mine = jnp.stack(mine)
    bc = jnp.concatenate([mine, twin(mine)], axis=0)
    wc = along_z(after(own_c, own_kv)).reshape(width, cols_c)

    passing = jnp.exp(meta[:, rows - 1, 8 : 8 + OWN_HEADS]) * marks[:, rows - 1, 1:2]
    pass_wide = swap(jnp.repeat(passing, SSM_HEAD, axis=1).reshape(2, ROWS, OWN_SSM, 1))
    p0, p1 = pass_wide[0], pass_wide[1]
    pass_both = p0 * p1
    first_local, both_local = local_states(where, xs, bc, meta, marks, p1)
    kv_other = twin(kv_own)
    state = jnp.zeros_like(both_local)
    for s in range(zs - 1):
        message = (pass_both * state + both_local).astype(bf16)
        if s == 1:
            query = after(query, message)
            context, context_low, logsum = attend(
                where, query, kv_own, kv_other, seg_query, seg_keys
            )
            gating = times(n1, after(wc, message))
        moved = lax.ppermute(message, "z", [(s, s + 1)])
        if s == 1:
            moved, context_low, gating = lax.optimization_barrier((moved, context_low, gating))
        state = state + moved.astype(f32)

    w_oc = along_z(after(w_oc, state))
    halves = w_oc.reshape(2, zs // 2, row_out + row_ctx, width)
    kept = lax.dynamic_index_in_dim(halves, c, 0, keepdims=False)
    sent = lax.dynamic_index_in_dim(halves, 1 - c, 0, keepdims=False)
    got = twin(sent)
    both = jnp.where(c == 0, jnp.stack([kept, got], 1), jnp.stack([got, kept], 1))
    w_out = both[:, :, :row_out].reshape(-1, width)
    w_ctx = both[:, :, row_out:].reshape(-1, width)
    w_gu_full = along_z(after(w_gu, state)).reshape(width, 2 * own_ff)
    w_down = along_z(after(down_weight, w_gu, state))

    ssm_out, gated_low, squares = ssm_forward(
        where, xs, bc, meta, meta_rows, marks, seg_rows, state, first_local, p0, gating, skip_wide
    )
    squares = sum_group(squares[:, 0].reshape(2, ROWS, rows))
    scale_ssm = lax.rsqrt(squares * (1.0 / ssm_width) + EPSILON).reshape(chunks, rows, 1)

    flat = lambda v: v.reshape(-1, v.shape[-1])
    norms = jnp.broadcast_to(scale_ssm.reshape(-1, 1), (chunks * rows, 8))
    mixed = scatter_product([flat(gated_low), flat(context_low)], [w_out, w_ctx], norm=norms)
    hidden, n2_own = on_rows(norm_two_kernel, block, [x, *mixed], [f32, bf16], "norm_two")

    n2 = gather_group(lined(n2_own))
    activation, grad_gu = feed(n2, g_all, w_gu_full, w_down)

    e2, grad_down_terms, _, folded = scatter_product(
        [grad_gu],
        [w_gu_full],
        turned=True,
        give=True,
        meanwhile=lambda own: weight_grad(after(activation, own).T, g_all),
    )
    grad_down = owner_z(grad_down_terms)
    grad_gu_terms = weight_grad(after(grad_gu, folded).T, n2, zs)
    e2 = (after(e2[0], grad_gu_terms),) + e2[1:]
    grad_gu_w = to_owner(grad_gu_terms)
    grad_hidden, grad_mix_own = on_rows(
        norm_back_kernel, block, [hidden, *map(unlined, e2), cot], [f32, bf16], "norm_back"
    )
    grad_mix = gather_group(grad_mix_own)
    (late_own, late_x, late_y), _, _, late_folded = scatter_product(
        [after(activation, grad_mix_own)], [w_down], give=True
    )
    es, grad_context, es_sum = mixer_back(
        grad_mix, after(w_out, late_own), w_ctx, ssm_out, gating
    )
    es_sum = es_sum[:, 0] * scale_ssm[..., 0]
    es_mean = sum_group(es_sum.reshape(2, ROWS, rows)) * (1.0 / ssm_width)
    scales = jnp.pad(
        jnp.stack([scale_ssm[..., 0], es_mean.reshape(chunks, rows)], axis=-1),
        ((0, 0), (0, 0), (0, 6)),
    )
    gy, grad_gating, unit_low, later_grad, both_grad = gate_back(
        where, es, scales, gating, ssm_out, bc, meta, marks, p0
    )

    def out_grads(unit_low):
        mixer_in = jnp.concatenate([flat(unit_low), flat(context_low)], axis=-1)
        grad_oc_w = weight_grad(mixer_in.T, grad_mix)
        grad_out_rows = grad_oc_w[:OWN_SSM].reshape(zs // 2, 2, row_out, width)
        grad_ctx_rows = grad_oc_w[OWN_SSM:].reshape(zs // 2, 2, row_ctx, width)
        grad_oc = jnp.concatenate([grad_out_rows, grad_ctx_rows], axis=2)
        oc_kept = lax.dynamic_index_in_dim(grad_oc, c, 1, keepdims=False)
        oc_got = twin(lax.dynamic_index_in_dim(grad_oc, 1 - c, 1, keepdims=False))
        return jnp.where(
            c == 0,
            jnp.concatenate([oc_kept, oc_got], axis=0),
            jnp.concatenate([oc_got, oc_kept], axis=0),
        )

    flowing = jnp.zeros_like(both_grad)
    grad_c_low = flat(grad_gating)
    for s in range(zs - 1, 0, -1):
        message = (pass_both * flowing + both_grad).astype(bf16)
        if s == 1:
            grad_context = after(grad_context, message).reshape(2, ROWS, rows, ATT_HEAD)
            grad_query, grad_kv = attend_back(
                where, query, kv_own, kv_other, seg_query, seg_keys, grad_context, context, logsum
            )
            grad_wc_terms = weight_grad(after(grad_c_low, message).T, n1, zs)
            kv_kept = lax.dynamic_slice_in_dim(grad_kv, 2 * c, 2, 1).astype(f32)
            kv_got = twin(lax.dynamic_slice_in_dim(grad_kv, 2 - 2 * c, 2, 1)).astype(f32)
            kv_terms = (kv_kept + kv_got).astype(bf16)
        moved = lax.ppermute(message, "z", [(s, s - 1)])
        if s == zs - 1:
            oc_all = out_grads(after(unit_low, message))
            moved, oc_all, late_folded = lax.optimization_barrier((moved, oc_all, late_folded))
        if s == zs - 2:
            got_gu = to_ranks(after(grad_gu_w, message, grad_down))
            moved, got_gu, late_x, late_y = lax.optimization_barrier(
                (moved, got_gu, late_x, late_y)
            )
            grad_oc_own = owner_z(after(oc_all, got_gu))
        if s == 1:
            moved, grad_query, kv_terms, grad_wc_terms, grad_oc_own = lax.optimization_barrier(
                (moved, grad_query, kv_terms, grad_wc_terms, grad_oc_own)
            )
        flowing = flowing + moved.astype(f32)
    grad_wc = to_owner(grad_wc_terms)

    kv_grad = owner_z(kv_terms)
    kv_grad = kv_grad[0].astype(f32)
    grad_b_low = rope_back(
        where, grad_query, kv_grad.reshape(2, 2, rows, 2 * ATT_HEAD), cosine, sine
    )
    grad_b_low = flat(grad_b_low)
    grad_wb_terms = weight_grad(grad_b_low.T, n1, zs)
    grad_wb = to_owner(grad_wb_terms)

    got_gu = got_gu.astype(f32)
    grad_xs, *bc_terms, grad_step, head_sums = ssm_back(
        where, xs, gy, bc, meta, meta_rows, marks, seg_rows, state, first_local, flowing, later_grad,
        p0, p1, skip_wide, head,
    )
    got = twin(jnp.stack(bc_terms[ROWS:])).astype(f32)
    bc_sums = [bc_terms[k].astype(f32) + got[k] for k in range(ROWS)]
    grad_bc = bc_sums[0]
    for k in range(1, ROWS):
        grad_bc = grad_bc + hop(bc_sums[k].astype(bf16), k).astype(f32)

    near = CONV - 1
    bc_near = grad_bc[:, :near].reshape(ROWS, near, 2, PIECE).transpose(2, 0, 1, 3)
    grad_near = jnp.concatenate(
        [grad_xs[:, :near], bc_near.reshape(chunks, near, PIECE)], axis=-1
    )
    grad_near = grad_near * slope[:, :near, :OWN_CONV]
    give = jnp.zeros((chunks, near, OWN_CONV), f32)
    for o in range(near):
        masked = grad_near[:, : near - o] * marks[:, : near - o, 3 + o : 4 + o]
        give = give + jnp.pad(masked * conv_own[o, :OWN_CONV], ((0, 0), (o, 0), (0, 0)))
    give = give.reshape(2, ROWS, near, OWN_CONV)
    moved = zshift(jnp.where(c == 0, give[0], give[1]).astype(bf16), -1).astype(f32)
    given = jnp.stack(
        [jnp.where(c == 0, give[1], moved), jnp.where(c == 0, moved, give[0])]
    ).reshape(chunks, near, OWN_CONV)
    given = after(given, grad_wb_terms)
    given = jnp.pad(given, ((0, 0), (8 - near, 0), (0, LANES_A - OWN_CONV)))
    grad_a_low, conv_sums = conv_backward(
        grad_xs, grad_bc, grad_step, slope, proj, halo, marks, given, conv_own
    )
    grad_a_low = flat(grad_a_low)
    conv_sums = jnp.sum(conv_sums, axis=0)[: CONV + 1, :OWN_CONV]
    head_sums = jnp.sum(head_sums, axis=0)[:3, :OWN_HEADS] * jnp.stack(
        [jnp.ones_like(rate), rate, jnp.ones_like(rate)]
    )
    head_sums = jnp.pad(head_sums.reshape(1, -1), ((0, 0), (0, OWN_CONV - 3 * OWN_HEADS)))

    def all_sums(sums):
        total = sums
        for flip in range(1, zs):
            total = total + zhop(sums, flip)
        table = jnp.stack([total, twin(total)])
        return jnp.concatenate([table] + [hop(table, flip) for flip in range(1, ROWS)], axis=0)

    grad_wa_terms = weight_grad(grad_a_low.T, n1, zs)
    grad_a_low = after(grad_a_low, grad_wa_terms)
    e1, _, _, e1_folded = scatter_product(
        [grad_c_low, grad_b_low, grad_a_low], [wc, wb, wa], turned=True, give=True
    )
    grad_wa = to_owner(grad_wa_terms)
    late_own = after(late_own, e1_folded)
    result = (hidden + late_own + late_x.astype(f32) + late_y.astype(f32)).astype(bf16)
    grad_oc_own = grad_oc_own[0].astype(f32)
    sums = jnp.concatenate([conv_sums, head_sums], axis=0)
    got_bc = to_ranks(after(jnp.concatenate([grad_wb, grad_wc], axis=2), e1_folded))
    got_a = to_ranks(grad_wa)
    table = all_sums(sums)
    e1 = (after(e1[0], got_bc, table),) + e1[1:]
    (grad_x,) = on_rows(
        norm_back_kernel, block, [x, *map(unlined, e1), grad_hidden], [bf16], "norm_back_in"
    )

    def unrank(values):
        return values.transpose(1, 0, 2).reshape(share, -1)

    got_a, got_bc = got_a.astype(f32), got_bc.astype(f32)
    got_b, got_c = got_bc[..., :cols_b], got_bc[..., cols_b:]
    d_input = unrank(got_a[..., :OWN_SSM])
    d_state = unrank(got_a[..., OWN_SSM:OWN_CONV])
    d_step = unrank(got_a[..., OWN_CONV : OWN_CONV + OWN_HEADS])
    d_query = unrank(got_b[..., :ATT_HEAD])
    d_kv = got_b[..., ATT_HEAD:].reshape(KVHEADS, RANKS // KVHEADS, share, 2, ATT_HEAD).sum(1)
    d_kv = d_kv.transpose(1, 2, 0, 3).reshape(share, 2 * group_kv)
    d_gating = unrank(got_c)

    def ff_unrank(values):
        return (
            values.reshape(ROWS, 2, share, zs, own_ff // zs)
            .transpose(2, 0, 3, 1, 4)
            .reshape(share, -1)
        )

    d_gate, d_up = ff_unrank(got_gu[..., :own_ff]), ff_unrank(got_gu[..., own_ff:])

    def gain_grad(pairs):
        return sum(jnp.sum(w.astype(f32) * d, axis=1) for w, d in pairs)

    d_norm_gain = gain_grad(
        (
            (gating_weight, d_gating),
            (input_weight, d_input),
            (state_weight, d_state),
            (step_weight, d_step),
            (query_weight, d_query),
            (keyval_weight, d_kv),
        )
    )
    d_mlp_gain = gain_grad(((gate_weight, d_gate), (up_weight, d_up)))
    d_out = grad_oc_own[:row_out]
    d_ctx = grad_oc_own[row_out:]
    d_ssm_gain = gain_grad(((out_weight, d_out),))

    place = jnp.arange(RANKS)
    chosen = ((place ^ rank)[:, None] == place[None, :]).astype(f32)
    table = jnp.einsum("rs,sof->rof", chosen, table, precision=HIGH)
    conv_ssm = table[:, : CONV + 1, :OWN_SSM].transpose(1, 0, 2).reshape(CONV + 1, -1)
    conv_state = table[:, : CONV + 1, OWN_SSM:].transpose(1, 0, 2).reshape(CONV + 1, -1)
    conv_full = jnp.concatenate([conv_ssm, conv_state], axis=1)
    conv_mine = lax.dynamic_slice_in_dim(conv_full, (rank // 2 * zs * 2 + z * 2 + c) * chan, chan, 1)
    heads = table[:, CONV + 1, : 3 * OWN_HEADS].reshape(RANKS, 3, OWN_HEADS)
    heads = heads.transpose(1, 0, 2).reshape(3, HEADS)

    return (
        result[None],
        grad_x[None],
        d_norm_gain,
        d_gating * gain_col,
        d_input * gain_col,
        d_state * gain_col,
        d_step * gain_col,
        conv_mine[:CONV],
        conv_mine[CONV],
        heads[0],
        heads[1],
        heads[2],
        d_ssm_gain,
        d_out * ssm_gain_col,
        d_query * gain_col,
        d_kv * gain_col,
        d_ctx,
        d_mlp_gain,
        d_gate * gain2_col,
        d_up * gain2_col,
        grad_down.astype(f32),
    )


def solution(mesh):
    places = mesh.devices.reshape(ROWS, mesh.shape["seq"] // 2, 2)
    split = Mesh(places, ("b", "z", "c"))
    everywhere = ("b", "z", "c")
    row = P(everywhere, None)
    vector = P(everywhere)
    token = P("b", ("z", "c"), None)
    return jax.shard_map(
        per_device,
        mesh=split,
        in_specs=(
            token,
            P("b", ("z", "c")),
            token,
            vector,
            row,
            row,
            row,
            row,
            P(None, everywhere),
            vector,
            P(),
            P(),
            P(),
            vector,
            row,
            row,
            row,
            row,
            vector,
            row,
            row,
            row,
        ),
        out_specs=(
            token,
            token,
            vector,
            row,
            row,
            row,
            row,
            P(None, everywhere),
            vector,
            P(),
            P(),
            P(),
            vector,
            row,
            row,
            row,
            row,
            vector,
            row,
            row,
            row,
        ),
        check_vma=False,
    )
```

```python
import math

import jax
import jax.numpy as jnp
from jax import lax
from jax.experimental import pallas as pl
from jax.experimental.pallas import tpu as pltpu
from jax.sharding import Mesh
from jax.sharding import PartitionSpec as P

HEADS = 48
SSM_HEAD = 64
STATE = 256
CONV = 4
QHEADS = 8
KVHEADS = 2
ATT_HEAD = 128
EPSILON = 1e-05
ROPE_BASE = 10000.0
NEG_BIG = -1e30
HIGH = lax.Precision.HIGHEST

RANKS = 8
ROWS = 4
OWN_HEADS = HEADS // RANKS
OWN_SSM = OWN_HEADS * SSM_HEAD
OWN_STATE = 2 * STATE // RANKS
OWN_CONV = OWN_SSM + OWN_STATE

bf16 = jnp.bfloat16
f32 = jnp.float32


ANY = pl.BlockSpec(memory_space=pl.ANY)
IN_VMEM = pl.BlockSpec(memory_space=pltpu.VMEM)
CHUNK = 256
LANES_A = 512
STEP_AT = OWN_CONV
PIECE = OWN_STATE
HALF = 2 * CHUNK


def dot(left, right, dims=((1,), (0,))):
    return lax.dot_general(left, right, (dims, ((), ())), preferred_element_type=f32)


def dot_rows(left, right):
    return dot(left, right, ((0,), (0,)))


def dot_cols(left, right):
    return dot(left, right, ((1,), (1,)))


def bdot(left, right, lc, rc):
    return lax.dot_general(
        left, right, (((lc,), (rc,)), ((0,), (0,))), preferred_element_type=f32
    )


def hop(values, flip):
    return lax.ppermute(values, "b", [(i, i ^ flip) for i in range(ROWS)])


def twin(values):
    return lax.ppermute(values, "c", [(0, 1), (1, 0)])


def zhop(values, flip):
    return lax.ppermute(values, "z", [(i, i ^ flip) for i in range(lax.axis_size("z"))])


def zshift(values, step):
    size = lax.axis_size("z")
    return lax.ppermute(
        values, "z", [(i, i + step) for i in range(size) if 0 <= i + step < size]
    )


def after(values, *earlier):
    return lax.optimization_barrier((values,) + earlier)[0]


def gather_group(own, meanwhile=None, then=None):
    half = own.shape[0] // 2
    by_x = hop(own, 1)
    by_y = hop(own, 2)
    if meanwhile is not None:
        by_x, by_y, meanwhile = lax.optimization_barrier((by_x, by_y, meanwhile))
    far = hop(by_x[:half], 2), hop(by_y[half:], 1)
    if then is not None:
        *far, meanwhile = lax.optimization_barrier((*far, then(meanwhile)))
    mine = [own, by_x, by_y, *far]
    pieces = mine + [twin(part) for part in mine]
    return pieces if meanwhile is None else (pieces, meanwhile)


def starts_of(pieces):
    starts = [0]
    for piece in pieces:
        starts.append(starts[-1] + piece.shape[0])
    return starts


def reslot(values, flip, axis):
    order = [k ^ flip for k in range(ROWS)]
    return jnp.concatenate(
        [lax.slice_in_dim(values, k, k + 1, axis=axis) for k in order], axis=axis
    )


def sum_group(values):
    values = values + twin(values)[::-1]
    total = values
    for flip in range(1, ROWS):
        total = total + reslot(hop(values, flip), flip, 1)
    return total


def silu_slope(values):
    sigmoid = jax.nn.sigmoid(values)
    return sigmoid * (1.0 + values * (1.0 - sigmoid))


def rms_scale(values):
    return lax.rsqrt(jnp.mean(values * values, axis=-1, keepdims=True) + EPSILON)


def rotate(values, cosine, sine):
    half = values.shape[-1] // 2
    first = values[..., :half]
    second = values[..., half:]
    return jnp.concatenate([first * cosine - second * sine, second * cosine + first * sine], axis=-1)


def split(values, count):
    terms = []
    for _ in range(count):
        low = values.astype(bf16)
        terms.append(low)
        values = values - low.astype(f32)
    return terms


def exact(ones, values, dims=((1,), (0,)), count=3):
    return sum(dot(ones.astype(bf16), term, dims) for term in split(values, count))


def head_map(rows, cols, along):
    channel = lax.broadcasted_iota(jnp.int32, (rows, cols), along)
    head = lax.broadcasted_iota(jnp.int32, (rows, cols), 1 - along)
    return (channel // SSM_HEAD == head).astype(bf16)


def widen(values):
    rows = values.shape[0]
    first = lax.broadcasted_iota(jnp.int32, (rows, 2 * SSM_HEAD), 1) < SSM_HEAD
    parts = []
    for h in range(0, OWN_HEADS, 2):
        left = jnp.broadcast_to(values[:, h : h + 1], first.shape)
        right = jnp.broadcast_to(values[:, h + 1 : h + 2], first.shape)
        parts.append(jnp.where(first, left, right))
    return jnp.concatenate(parts, axis=1)


def narrow(values):
    ones = head_map(OWN_SSM, 8, 0)
    return sum(dot(term, ones) for term in split(values, 2))


def row_sums(values):
    ones = jnp.ones((8, values.shape[1]), bf16)
    return exact(ones, values, ((1,), (1,)), 2)


def sigmoid_of(values):
    return 1.0 / (1.0 + jnp.exp(-values))


def tri(lower):
    t = lax.broadcasted_iota(jnp.int32, (CHUNK, CHUNK), 0)
    s = lax.broadcasted_iota(jnp.int32, (CHUNK, CHUNK), 1)
    return (t >= s) if lower else (t <= s)


def conv_kernel(proj, halo, marks, conv, head, xs_out, bc_out, slope_out, meta_out, row_out, ext):
    ext[0:8, :] = halo[0]
    ext[8:, :] = proj[0].astype(bf16).astype(f32)
    pre = conv[4:5, :] + conv[3:4, :] * ext[8 : 8 + CHUNK, :]
    for o in range(CONV - 1):
        pre = pre + conv[o : o + 1, :] * ext[5 + o : 5 + o + CHUNK, :] * marks[0, :, 3 + o : 4 + o]
    sig = sigmoid_of(pre)
    act = (pre * sig).astype(bf16)
    xs_out[0] = act[:, :OWN_SSM]
    for r in range(2):

        @pl.when(pl.program_id(1) == r)
        def _():
            bc_out[0, :, r * PIECE : (r + 1) * PIECE] = act[:, OWN_SSM:OWN_CONV]

    slope_out[0] = sig * (1.0 + pre * (1.0 - sig))
    raw = proj[0][:, STEP_AT : STEP_AT + 8] + head[0:1, 0:8]
    real = lax.broadcasted_iota(jnp.int32, (CHUNK, 8), 1) < OWN_HEADS
    step = jnp.maximum(raw, 0.0) + jnp.log(1.0 + jnp.exp(-jnp.abs(raw)))
    step = jnp.where(real, step, 0.0)
    cum = exact(tri(True), step * head[1:2, 0:8])
    meta = jnp.concatenate(
        [step, cum, sigmoid_of(raw), jnp.zeros((CHUNK, 104), f32)], axis=1
    )
    meta_out[0] = meta[:, :32]
    row_out[0] = meta.T[:16]


def marks_kernel(own, before, out):
    lane = lax.broadcasted_iota(jnp.int32, (1, CHUNK), 1)
    for q in range(own.shape[0]):
        seg, prev = own[q : q + 1, :], before[q : q + 1, :]
        rows = [seg, (seg == prev[:, CHUNK - 1 :]).astype(f32), (seg == seg[:, CHUNK - 1 :]).astype(f32)]
        for o in range(CONV - 1):
            by = CONV - 1 - o
            moved = jnp.where(lane < by, pltpu.roll(prev, by, 1), pltpu.roll(seg, by, 1))
            rows.append((moved == seg).astype(f32))
        rows.append(jnp.zeros((128 - len(rows), CHUNK), f32))
        out[q] = jnp.concatenate(rows, axis=0).T[:, :8]


def marks_of(own, before):
    chunks = own.shape[0]
    return pl.pallas_call(
        marks_kernel,
        in_specs=[IN_VMEM] * 2,
        out_specs=IN_VMEM,
        out_shape=jax.ShapeDtypeStruct((chunks, CHUNK, 8), f32),
        compiler_params=pltpu.CompilerParams(vmem_limit_bytes=VMEM),
        cost_estimate=lasting(3),
        name="marks",
    )(own, before)


def conv_forward(proj, halo, marks, conv, head):
    block = lambda *shape: pl.BlockSpec((1,) + shape, lambda k, r: (r * ROWS + k, 0, 0))
    whole = pl.BlockSpec((8, LANES_A), lambda k, r: (0, 0))
    chunks = proj.shape[0]
    return pl.pallas_call(
        conv_kernel,
        grid=(ROWS, 2),
        in_specs=[
            block(CHUNK, LANES_A),
            block(8, LANES_A),
            block(CHUNK, 8),
            whole,
            pl.BlockSpec((8, 128), lambda k, r: (0, 0)),
        ],
        out_specs=[
            block(CHUNK, OWN_SSM),
            pl.BlockSpec((1, CHUNK, 2 * PIECE), lambda k, r: (k, 0, 0)),
            block(CHUNK, LANES_A),
            block(CHUNK, 32),
            block(16, CHUNK),
        ],
        out_shape=[
            jax.ShapeDtypeStruct((chunks, CHUNK, OWN_SSM), bf16),
            jax.ShapeDtypeStruct((ROWS, CHUNK, 2 * PIECE), bf16),
            jax.ShapeDtypeStruct((chunks, CHUNK, LANES_A), f32),
            jax.ShapeDtypeStruct((chunks, CHUNK, 32), f32),
            jax.ShapeDtypeStruct((chunks, 16, CHUNK), f32),
        ],
        scratch_shapes=[pltpu.VMEM((8 + CHUNK, LANES_A), f32)],
        compiler_params=pltpu.CompilerParams(vmem_limit_bytes=VMEM),
        cost_estimate=lasting(8),
        name="conv_forward",
    )(proj, halo, marks, conv, head)


VMEM = 60 * 1024 * 1024


def lasting(microseconds):
    return pl.CostEstimate(
        flops=0, bytes_accessed=int(microseconds * 1.1e6), transcendentals=0
    )


def time_spec(shape, backward=False):
    def at(k, t, where):
        core = (1 - t if backward else t) ^ where[2]
        return (core * ROWS + k,) + (0,) * len(shape)

    return pl.BlockSpec((1,) + tuple(shape), at)


def slot_spec(shape):
    return pl.BlockSpec((1,) + tuple(shape), lambda k, t, where: (k,) + (0,) * len(shape))


def piece_specs(kind):
    def spec(i):
        def at(k, t, where):
            slot = (i // 2 + 2 * kind) ^ (2 * (where[0] // 2))
            return (i % 2 * ROWS + slot, k ^ slot, 0, 0)

        return pl.BlockSpec((1, 1, CHUNK, 2 * PIECE), at)

    return [spec(i) for i in range(4)]


def core_of(where, backward=False):
    t = pl.program_id(1)
    return (1 - t if backward else t) ^ where[2]


def joined(pieces, core):
    parts = []
    for i, piece in enumerate(pieces):
        both = piece[0, 0]
        parts.append(jnp.where(core ^ (i % 2) == 0, both[:, :PIECE], both[:, PIECE:]))
    return jnp.concatenate(parts, axis=1)


def tails_of(meta, marks):
    step, cum = meta[0, :, 0:8], meta[0, :, 8:16]
    last = cum[CHUNK - 1 : CHUNK]
    decay = jnp.exp(last - cum) * marks[0, :, 2:3]
    return step, cum, decay, decay * step


def local_kernel(where, xs, b0, b1, b2, b3, meta, marks, p1, first_out, both_out):
    _, _, _, tail = tails_of(meta, marks)
    weighted = (xs[0].astype(f32) * widen(tail)).astype(bf16)
    local = dot_rows(weighted, joined((b0, b1, b2, b3), core_of(where)))

    @pl.when(pl.program_id(1) == 0)
    def _():
        first_out[0] = local

    @pl.when(pl.program_id(1) == 1)
    def _():
        both_out[0] = p1[0] * first_out[0] + local


def local_states(where, xs, bc, meta, marks, p1):
    state = jax.ShapeDtypeStruct((ROWS, OWN_SSM, STATE), f32)
    return pl.pallas_call(
        local_kernel,
        grid_spec=pltpu.PrefetchScalarGridSpec(
            num_scalar_prefetch=1,
            grid=(ROWS, 2),
            in_specs=[time_spec((CHUNK, OWN_SSM))]
            + piece_specs(0)
            + [time_spec((CHUNK, 32)), time_spec((CHUNK, 8)), slot_spec((OWN_SSM, 1))],
            out_specs=[slot_spec((OWN_SSM, STATE))] * 2,
        ),
        out_shape=[state, state],
        compiler_params=pltpu.CompilerParams(vmem_limit_bytes=VMEM),
        cost_estimate=lasting(8),
        name="local_states",
    )(where, xs, bc, bc, bc, bc, meta, marks, p1)


def decay_of(meta, row, allowed, h):
    spread = meta[0, :, 8 + h : 9 + h] - row[0, 8 + h : 9 + h, :]
    return jnp.exp(jnp.where(allowed, spread, NEG_BIG))


def ssm_kernel(
    where, xs, b0, b1, b2, b3, c0, c1, c2, c3, meta, row, marks, segs, state, first, p0, gating, skip,
    out, gated_out, square_out, work,
):
    later = pl.program_id(1) == 1
    core = core_of(where)
    b_mat, c_mat = joined((b0, b1, b2, b3), core), joined((c0, c1, c2, c3), core)
    inner = dot_cols(c_mat, b_mat)
    allowed = (marks[0, :, 0:1] == segs[0, 0:1, :]) & tri(True)
    xs_f = xs[0].astype(f32)
    step, cum = meta[0, :, 0:8], meta[0, :, 8:16]
    stepped = (xs_f * widen(step)).astype(bf16)
    entering = jnp.where(later, p0[0] * state[0] + first[0], state[0]).astype(bf16)
    entry = widen(jnp.exp(cum) * marks[0, :, 1:2])
    for h in range(OWN_HEADS):
        at = slice(h * SSM_HEAD, (h + 1) * SSM_HEAD)
        mix = (inner * decay_of(meta, row, allowed, h)).astype(bf16)
        work[:, at] = dot(mix, stepped[:, at])
    total = work[...] + dot_cols(c_mat, entering) * entry + skip[0:1, :] * xs_f
    out[0] = total
    gate = gating[0]
    gated = total * gate * sigmoid_of(gate)
    gated_out[0] = gated.astype(bf16)
    square_out[0] = row_sums(gated * gated)


def ssm_forward(where, xs, bc, meta, row, marks, segs, state, first, p0, gating, skip):
    chunks = xs.shape[0]
    return pl.pallas_call(
        ssm_kernel,
        grid_spec=pltpu.PrefetchScalarGridSpec(
            num_scalar_prefetch=1,
            grid=(ROWS, 2),
            in_specs=[time_spec((CHUNK, OWN_SSM))]
            + piece_specs(0)
            + piece_specs(1)
            + [
                time_spec((CHUNK, 32)),
                time_spec((16, CHUNK)),
                time_spec((CHUNK, 8)),
                time_spec((8, CHUNK)),
                slot_spec((OWN_SSM, STATE)),
                slot_spec((OWN_SSM, STATE)),
                slot_spec((OWN_SSM, 1)),
                time_spec((CHUNK, OWN_SSM)),
                pl.BlockSpec((8, OWN_SSM), lambda k, t, where: (0, 0)),
            ],
            out_specs=[
                time_spec((CHUNK, OWN_SSM)),
                time_spec((CHUNK, OWN_SSM)),
                time_spec((8, CHUNK)),
            ],
            scratch_shapes=[pltpu.VMEM((CHUNK, OWN_SSM), f32)],
        ),
        out_shape=[
            jax.ShapeDtypeStruct((chunks, CHUNK, OWN_SSM), f32),
            jax.ShapeDtypeStruct((chunks, CHUNK, OWN_SSM), bf16),
            jax.ShapeDtypeStruct((chunks, 8, CHUNK), f32),
        ],
        compiler_params=pltpu.CompilerParams(vmem_limit_bytes=VMEM),
        cost_estimate=lasting(16),
        name="ssm_forward",
    )(where, xs, bc, bc, bc, bc, bc, bc, bc, bc, meta, row, marks, segs, state, first, p0, gating, skip)


def attention_mask(where, seg_q, seg_k):
    m = pl.program_id(1)
    same = seg_q[...].reshape(HALF, 8)[:, 0:1] == seg_k[0, 0:1, :]
    row = lax.broadcasted_iota(jnp.int32, (HALF, HALF), 0)
    place = lax.rem(row + where[2] * CHUNK, HALF)
    key = lax.broadcasted_iota(jnp.int32, (HALF, HALF), 1)
    return same & ((place >= key) | (m < where[1]))


def slot_keyval(where, own, other):
    mine = pl.program_id(0) // 2 == where[2]
    return jnp.where(mine, own[0, 0], other[0, 0])


def attend_kernel(where, query, kv_own, kv_other, seg_q, seg_k, out, low_out, sum_out, best, total, acc):
    m = pl.program_id(1)
    scale = 1.0 / math.sqrt(ATT_HEAD)

    @pl.when(m == 0)
    def _():
        best[...] = jnp.full_like(best, NEG_BIG)
        total[...] = jnp.zeros_like(total)
        acc[...] = jnp.zeros_like(acc)

    @pl.when(m <= where[1])
    def _():
        q = query[...].reshape(HALF, ATT_HEAD)
        keyval = slot_keyval(where, kv_own, kv_other)
        keys, vals = keyval[:, :ATT_HEAD], keyval[:, ATT_HEAD:]
        scores = jnp.where(attention_mask(where, seg_q, seg_k), dot_cols(q, keys) * scale, NEG_BIG)
        before = best[:, 0:1]
        now = jnp.maximum(before, jnp.max(scores, axis=1, keepdims=True))
        shrink = jnp.exp(before - now)
        weights = jnp.where(scores > 0.5 * NEG_BIG, jnp.exp(scores - now), 0.0)
        total[...] = total[...] * shrink + jnp.sum(weights, axis=1, keepdims=True)
        acc[...] = acc[...] * shrink + dot(weights.astype(bf16), vals)
        best[...] = jnp.broadcast_to(now, best.shape)

    @pl.when(m == pl.num_programs(1) - 1)
    def _():
        context = (acc[...] / total[...]).reshape(2, 1, CHUNK, ATT_HEAD)
        out[...] = context
        low_out[...] = context.astype(bf16)
        sum_out[0] = (best[...] + jnp.log(total[...]))[:, 0:8]


def pair_spec(width):
    return pl.BlockSpec((2, 1, CHUNK, width), lambda k, m, where: (0, k, 0, 0))


def attend(where, query, kv_own, kv_other, seg_q, seg_k):
    slots = kv_own.shape[0]
    keyval_spec = pl.BlockSpec((1, 1, HALF, 2 * ATT_HEAD), lambda k, m, where: (m, k % 2, 0, 0))
    return pl.pallas_call(
        attend_kernel,
        grid_spec=pltpu.PrefetchScalarGridSpec(
            num_scalar_prefetch=1,
            grid=(ROWS, slots),
            in_specs=[
                pair_spec(ATT_HEAD),
                keyval_spec,
                keyval_spec,
                pair_spec(8),
                pl.BlockSpec((1, 8, HALF), lambda k, m, where: (k * slots + m, 0, 0)),
            ],
            out_specs=[
                pair_spec(ATT_HEAD),
                pair_spec(ATT_HEAD),
                pl.BlockSpec((1, HALF, 8), lambda k, m, where: (k, 0, 0)),
            ],
            scratch_shapes=[pltpu.VMEM((HALF, ATT_HEAD), f32)] * 3,
        ),
        out_shape=[
            jax.ShapeDtypeStruct(query.shape, f32),
            jax.ShapeDtypeStruct(query.shape, bf16),
            jax.ShapeDtypeStruct((ROWS, HALF, 8), f32),
        ],
        compiler_params=pltpu.CompilerParams(vmem_limit_bytes=VMEM),
        cost_estimate=lasting(10),
        name="attend",
    )(where, query, kv_own, kv_other, seg_q, seg_k)


def attend_back_kernel(where, query, kv_own, kv_other, seg_q, seg_k, grad, context, sums, query_out, keyval_out):
    m = pl.program_id(1)
    scale = 1.0 / math.sqrt(ATT_HEAD)
    used = m <= where[1]

    @pl.when(m == 0)
    def _():
        query_out[...] = jnp.zeros_like(query_out)

    @pl.when(jnp.logical_not(used))
    def _():
        keyval_out[...] = jnp.zeros_like(keyval_out)

    @pl.when(used)
    def _():
        q = query[...].reshape(HALF, ATT_HEAD)
        g = grad[...].reshape(HALF, ATT_HEAD)
        keyval = slot_keyval(where, kv_own, kv_other)
        keys, vals = keyval[:, :ATT_HEAD], keyval[:, ATT_HEAD:]
        delta = jnp.sum(
            g.astype(f32) * context[...].reshape(HALF, ATT_HEAD), axis=1, keepdims=True
        )
        spread = dot_cols(q, keys) * scale - sums[0, :, 0:1]
        prob = jnp.exp(jnp.where(attention_mask(where, seg_q, seg_k), spread, NEG_BIG))
        slope = (prob * (dot_cols(g, vals) - delta)).astype(bf16)
        part = (dot(slope, keys) * scale).reshape(2, 1, CHUNK, ATT_HEAD)
        query_out[...] = query_out[...] + part
        keyval_out[0, 0, :, :ATT_HEAD] = (dot_rows(slope, q) * scale).astype(bf16)
        keyval_out[0, 0, :, ATT_HEAD:] = dot_rows(prob.astype(bf16), g).astype(bf16)


def attend_back(where, query, kv_own, kv_other, seg_q, seg_k, grad, context, sums):
    slots = kv_own.shape[0]
    keyval_spec = pl.BlockSpec((1, 1, HALF, 2 * ATT_HEAD), lambda k, m, where: (m, k % 2, 0, 0))
    grad_spec = pl.BlockSpec((1, 1, HALF, 2 * ATT_HEAD), lambda k, m, where: (m, k, 0, 0))
    return pl.pallas_call(
        attend_back_kernel,
        grid_spec=pltpu.PrefetchScalarGridSpec(
            num_scalar_prefetch=1,
            grid=(ROWS, slots),
            in_specs=[
                pair_spec(ATT_HEAD),
                keyval_spec,
                keyval_spec,
                pair_spec(8),
                pl.BlockSpec((1, 8, HALF), lambda k, m, where: (k * slots + m, 0, 0)),
                pair_spec(ATT_HEAD),
                pair_spec(ATT_HEAD),
                pl.BlockSpec((1, HALF, 8), lambda k, m, where: (k, 0, 0)),
            ],
            out_specs=[pair_spec(ATT_HEAD), grad_spec],
        ),
        out_shape=[
            jax.ShapeDtypeStruct(query.shape, f32),
            jax.ShapeDtypeStruct((slots, ROWS, HALF, 2 * ATT_HEAD), bf16),
        ],
        compiler_params=pltpu.CompilerParams(vmem_limit_bytes=VMEM),
        cost_estimate=lasting(14),
        name="attend_back",
    )(where, query, kv_own, kv_other, seg_q, seg_k, grad, context, sums)


def gate_back_kernel(
    where, es, scale, gating, ssm_out, c0, c1, c2, c3, meta, marks, p0,
    gy_out, gating_out, later_out, both_out,
):
    gate = gating[0]
    sig = sigmoid_of(gate)
    act = gate * sig
    out = ssm_out[0]
    norm = scale[0, :, 0:1]
    unit = out * act * norm
    grad = norm * (es[0] - unit * scale[0, :, 1:2])
    gy = (grad * act).astype(bf16)
    gy_out[0] = gy
    gating_out[0] = (grad * out * (sig * (1.0 + gate * (1.0 - sig)))).astype(bf16)
    entry = widen(jnp.exp(meta[0, :, 8:16]) * marks[0, :, 1:2])
    across = (gy.astype(f32) * entry).astype(bf16)
    local = dot_rows(across, joined((c0, c1, c2, c3), core_of(where, True)))

    @pl.when(pl.program_id(1) == 0)
    def _():
        later_out[0] = local

    @pl.when(pl.program_id(1) == 1)
    def _():
        both_out[0] = p0[0] * later_out[0] + local


def gate_back(where, es, scale, gating, ssm_out, bc, meta, marks, p0):
    chunks = gating.shape[0]
    wide = time_spec((CHUNK, OWN_SSM), True)
    state = jax.ShapeDtypeStruct((ROWS, OWN_SSM, STATE), f32)
    token = jax.ShapeDtypeStruct((chunks, CHUNK, OWN_SSM), bf16)
    return pl.pallas_call(
        gate_back_kernel,
        grid_spec=pltpu.PrefetchScalarGridSpec(
            num_scalar_prefetch=1,
            grid=(ROWS, 2),
            in_specs=[wide, time_spec((CHUNK, 8), True), wide, wide]
            + piece_specs(1)
            + [
                time_spec((CHUNK, 32), True),
                time_spec((CHUNK, 8), True),
                slot_spec((OWN_SSM, 1)),
            ],
            out_specs=[wide, wide, slot_spec((OWN_SSM, STATE)), slot_spec((OWN_SSM, STATE))],
        ),
        out_shape=[token, token, state, state],
        compiler_params=pltpu.CompilerParams(vmem_limit_bytes=VMEM),
        cost_estimate=lasting(11),
        name="gate_back",
    )(where, es, scale, gating, ssm_out, bc, bc, bc, bc, meta, marks, p0)


def ssm_back_kernel(
    where, xs, gy, b0, b1, b2, b3, c0, c1, c2, c3, meta, row, marks, segs, state, first, flow, later,
    p0, p1, skip, head,
    xs_out, o00, o01, o02, o03, o10, o11, o12, o13, step_out, sums_out, work,
):
    early = pl.program_id(1) == 1
    core = core_of(where, True)
    b_mat, c_mat = joined((b0, b1, b2, b3), core), joined((c0, c1, c2, c3), core)
    inner = dot_cols(b_mat, c_mat)
    allowed = (marks[0, :, 0:1] == segs[0, 0:1, :]) & tri(False)
    xs_f = xs[0].astype(f32)
    gy_low = gy[0]
    gy_f = gy_low.astype(f32)
    step, cum, tail_decay, tail = tails_of(meta, marks)
    step_wide, tail_wide = widen(step), widen(tail)
    entry = widen(jnp.exp(cum) * marks[0, :, 1:2])
    stepped = (xs_f * step_wide).astype(bf16)
    grad_inner = jnp.zeros((CHUNK, CHUNK), f32)
    read = jnp.zeros((CHUNK, 8), f32)
    reads = jnp.zeros((8, CHUNK), f32)
    lane = lax.broadcasted_iota(jnp.int32, (CHUNK, 8), 1)
    sublane = lax.broadcasted_iota(jnp.int32, (8, CHUNK), 0)
    for h in range(OWN_HEADS):
        at = slice(h * SSM_HEAD, (h + 1) * SSM_HEAD)
        spread = row[0, 8 + h : 9 + h, :] - meta[0, :, 8 + h : 9 + h]
        decay = jnp.exp(jnp.where(allowed, spread, NEG_BIG))
        slope = decay * dot_cols(stepped[:, at], gy_low[:, at])
        grad_inner = grad_inner + slope
        flow_low = (slope * inner).astype(bf16)
        read = read + dot(flow_low, (lane == h).astype(bf16))
        reads = reads + dot((sublane == h).astype(bf16), flow_low)
        work[:, at] = dot((inner * decay).astype(bf16), gy_low[:, at])
    reads = jnp.concatenate([reads, jnp.zeros((120, CHUNK), f32)], axis=0).T
    flows = reads[:, :8] - read
    from_mix = work[...]
    entering = jnp.where(early, state[0], p0[0] * state[0] + first[0])
    leaving = jnp.where(early, p1[0] * flow[0] + later[0], flow[0])
    leaving_low = leaving.astype(bf16)
    inner_low = grad_inner.astype(bf16)
    across = (gy_f * entry).astype(bf16)
    weighted = (xs_f * tail_wide).astype(bf16)
    grad_b = dot(inner_low, c_mat) + dot(weighted, leaving_low)
    grad_c = dot_rows(inner_low, b_mat) + dot(across, entering.astype(bf16))
    from_state = dot_cols(b_mat, leaving_low)
    skip_row = skip[0:1, :]
    xs_out[0] = skip_row * gy_f + step_wide * from_mix + tail_wide * from_state
    low_first = where[0] < 2
    lower = jnp.where(low_first, grad_b, grad_c).astype(bf16)
    upper = jnp.where(low_first, grad_c, grad_b).astype(bf16)
    for ref, value, i in (
        (o00, lower, 0), (o10, lower, 1), (o01, lower, 2), (o11, lower, 3),
        (o02, upper, 0), (o12, upper, 1), (o03, upper, 2), (o13, upper, 3),
    ):
        for half in range(2):

            @pl.when(core ^ (i % 2) == half)
            def _():
                ref[0, :, half * PIECE : (half + 1) * PIECE] = value[:, i * PIECE : (i + 1) * PIECE]

    entering_low = entering.astype(bf16)
    entry_sum = narrow(gy_f * (dot_cols(c_mat, entering_low) * entry))
    step_sum = narrow(xs_f * from_mix)
    tail_sum = narrow(xs_f * from_state)
    skip_sum = narrow(gy_f * xs_f)
    tail_flow = tail_sum * tail
    passed = jnp.sum(leaving * entering, axis=1, keepdims=True)
    passed = jnp.broadcast_to(passed, (OWN_SSM, 8))
    own_head = head_map(OWN_SSM, 8, 0).astype(f32)
    grad_pass = jnp.sum(passed * own_head, axis=0, keepdims=True)
    passing = jnp.exp(cum[CHUNK - 1 : CHUNK]) * marks[0, CHUNK - 1 : CHUNK, 1:2]
    end = grad_pass * passing + jnp.sum(tail_flow, axis=0, keepdims=True)
    last = lax.broadcasted_iota(jnp.int32, (CHUNK, 8), 0) == CHUNK - 1
    grad_cum = flows + entry_sum - tail_flow + jnp.where(last, end, 0.0)
    grad_rate = exact(tri(False), grad_cum)
    grad_step = step_sum + tail_sum * tail_decay + grad_rate * head[1:2, 0:8]
    raw = grad_step * meta[0, :, 16:24]
    step_out[0] = raw
    sums = [raw, grad_rate * step, skip_sum]
    sums_out[0] = jnp.concatenate(
        [jnp.sum(v, axis=0, keepdims=True) for v in sums] + [jnp.zeros((5, 8), f32)], axis=0
    )


def ssm_back(where, xs, gy, bc, meta, row, marks, segs, state, first, flow, later, p0, p1, skip, head):
    chunks = xs.shape[0]
    wide = time_spec((CHUNK, OWN_SSM), True)
    kept = slot_spec((OWN_SSM, STATE))
    column = slot_spec((OWN_SSM, 1))

    def owner(slot):
        return pl.BlockSpec((1, CHUNK, 2 * PIECE), lambda k, t, where: (k ^ slot, 0, 0))

    piece = jax.ShapeDtypeStruct((ROWS, CHUNK, 2 * PIECE), bf16)
    return pl.pallas_call(
        ssm_back_kernel,
        grid_spec=pltpu.PrefetchScalarGridSpec(
            num_scalar_prefetch=1,
            grid=(ROWS, 2),
            in_specs=[wide, wide]
            + piece_specs(0)
            + piece_specs(1)
            + [
                time_spec((CHUNK, 32), True),
                time_spec((16, CHUNK), True),
                time_spec((CHUNK, 8), True),
                time_spec((8, CHUNK), True),
                kept,
                kept,
                kept,
                kept,
                column,
                column,
                pl.BlockSpec((8, OWN_SSM), lambda k, t, where: (0, 0)),
                pl.BlockSpec((8, 128), lambda k, t, where: (0, 0)),
            ],
            out_specs=[wide]
            + [owner(m) for r in range(2) for m in range(ROWS)]
            + [time_spec((CHUNK, 8), True), time_spec((8, 8), True)],
            scratch_shapes=[pltpu.VMEM((CHUNK, OWN_SSM), f32)],
        ),
        out_shape=[jax.ShapeDtypeStruct((chunks, CHUNK, OWN_SSM), f32)]
        + [piece] * 8
        + [
            jax.ShapeDtypeStruct((chunks, CHUNK, 8), f32),
            jax.ShapeDtypeStruct((chunks, 8, 8), f32),
        ],
        compiler_params=pltpu.CompilerParams(vmem_limit_bytes=VMEM),
        cost_estimate=lasting(30),
        name="ssm_back",
    )(
        where, xs, gy, bc, bc, bc, bc, bc, bc, bc, bc, meta, row, marks, segs, state, first, flow,
        later, p0, p1, skip, head,
    )


def conv_back_kernel(grad_xs, grad_bc, step, slope, proj, halo, marks, returned, conv, out, sums_out, ext, back):
    ext[0:8, :] = halo[0]
    ext[8:, :] = proj[0].astype(bf16).astype(f32)
    rest = jnp.zeros((CHUNK, LANES_A - OWN_CONV), f32)
    both = grad_bc[0]
    own_bc = jnp.where(pl.program_id(0) < ROWS, both[:, :PIECE], both[:, PIECE:])
    grad = jnp.concatenate([grad_xs[0], own_bc, rest], axis=1) * slope[0]
    sums = []
    back[...] = jnp.zeros_like(back)
    back[CHUNK : CHUNK + 8, :] = returned[0]
    for o in range(CONV):
        masked = grad if o == CONV - 1 else grad * marks[0, :, 3 + o : 4 + o]
        sums.append(jnp.sum(masked * ext[5 + o : 5 + o + CHUNK, :], axis=0, keepdims=True))
        back[5 + o : 5 + o + CHUNK, :] = (
            back[5 + o : 5 + o + CHUNK, :] + masked * conv[o : o + 1, :]
        )
    sums.append(jnp.sum(grad, axis=0, keepdims=True))
    sums_out[0] = jnp.concatenate(sums + [jnp.zeros((3, LANES_A), f32)], axis=0)
    mixed = back[8 : 8 + CHUNK, :]
    out[0] = mixed.astype(bf16)
    out[0, :, STEP_AT : STEP_AT + 8] = step[0].astype(bf16)


def conv_backward(grad_xs, grad_bc, step, slope, proj, halo, marks, returned, conv):
    chunks = proj.shape[0]
    block = lambda *shape: pl.BlockSpec((1,) + shape, lambda q: (q, 0, 0))
    return pl.pallas_call(
        conv_back_kernel,
        grid=(chunks,),
        in_specs=[
            block(CHUNK, OWN_SSM),
            pl.BlockSpec((1, CHUNK, 2 * PIECE), lambda q: (lax.rem(q, ROWS), 0, 0)),
            block(CHUNK, 8),
            block(CHUNK, LANES_A),
            block(CHUNK, LANES_A),
            block(8, LANES_A),
            block(CHUNK, 8),
            block(8, LANES_A),
            pl.BlockSpec((8, LANES_A), lambda q: (0, 0)),
        ],
        out_specs=[block(CHUNK, LANES_A), block(8, LANES_A)],
        out_shape=[
            jax.ShapeDtypeStruct((chunks, CHUNK, LANES_A), bf16),
            jax.ShapeDtypeStruct((chunks, 8, LANES_A), f32),
        ],
        scratch_shapes=[pltpu.VMEM((8 + CHUNK, LANES_A), f32)] * 2,
        compiler_params=pltpu.CompilerParams(vmem_limit_bytes=VMEM),
        cost_estimate=lasting(6),
        name="conv_backward",
    )(grad_xs, grad_bc, step, slope, proj, halo, marks, returned, conv)


LARGE = VMEM


def fetch(pieces, held, arrived):
    starts = starts_of(pieces)
    copies = []
    for i, piece in enumerate(pieces):
        at = pl.ds(starts[i], piece.shape[0])
        copies.append(pltpu.make_async_copy(piece, held.at[at], arrived.at[i]))
        copies[-1].start()
    return copies, starts


def by_pair(copies, starts):
    for i in range(0, 8, 2):
        for j, copy in enumerate(copies):
            if i * CHUNK < starts[j + 1] <= (i + 2) * CHUNK:
                copy.wait()
        yield i, slice(i * CHUNK, (i + 2) * CHUNK)


def times_kernel(count, *refs):
    pieces, (weight, out, held, arrived) = refs[:count], refs[count:]
    for i, at in by_pair(*fetch(pieces, held, arrived)):
        out[i : i + 2] = dot(held[at, :], weight[...]).reshape(2, CHUNK, -1)


def times(pieces, weight):
    width, cols = weight.shape
    count = len(pieces)
    return pl.pallas_call(
        lambda *refs: times_kernel(count, *refs),
        in_specs=[ANY] * count + [IN_VMEM],
        out_specs=IN_VMEM,
        out_shape=jax.ShapeDtypeStruct((8, CHUNK, cols), f32),
        scratch_shapes=[pltpu.VMEM((8 * CHUNK, width), bf16), pltpu.SemaphoreType.DMA((count,))],
        compiler_params=pltpu.CompilerParams(vmem_limit_bytes=LARGE),
        cost_estimate=lasting(5 + cols / 80),
        name="times",
    )(*pieces, weight)


def mixer_back_kernel(count, *refs):
    pieces = refs[:count]
    w_out, w_ctx, ssm_out, gating, es_out, context_out, sum_out, held, arrived = refs[count:]
    for i, at in by_pair(*fetch(pieces, held, arrived)):
        es = dot_cols(held[at, :], w_out[...]).reshape(2, CHUNK, OWN_SSM)
        es_out[i : i + 2] = es
        context = dot_cols(held[at, :], w_ctx[...]).astype(bf16)
        context_out[i : i + 2] = context.reshape(2, CHUNK, ATT_HEAD)
        for j in range(2):
            gate = gating[i + j]
            sum_out[i + j] = row_sums(es[j] * ssm_out[i + j] * gate * sigmoid_of(gate))


def mixer_back(pieces, w_out, w_ctx, ssm_out, gating):
    count, width = len(pieces), w_out.shape[1]
    return pl.pallas_call(
        lambda *refs: mixer_back_kernel(count, *refs),
        in_specs=[ANY] * count + [IN_VMEM] * 4,
        out_specs=[IN_VMEM] * 3,
        out_shape=[
            jax.ShapeDtypeStruct((8, CHUNK, OWN_SSM), f32),
            jax.ShapeDtypeStruct((8, CHUNK, ATT_HEAD), bf16),
            jax.ShapeDtypeStruct((8, 8, CHUNK), f32),
        ],
        scratch_shapes=[pltpu.VMEM((8 * CHUNK, width), bf16), pltpu.SemaphoreType.DMA((count,))],
        compiler_params=pltpu.CompilerParams(vmem_limit_bytes=LARGE),
        cost_estimate=lasting(13),
        name="mixer_back",
    )(*pieces, w_out, w_ctx, ssm_out, gating)


def weight_grad_kernel(*refs):
    left, pieces, out = refs[0], refs[1:-1], refs[-1]
    starts = starts_of(pieces)
    total = dot(left[:, : starts[1]], pieces[0][...])
    for i in range(1, len(pieces)):
        total = total + dot(left[:, starts[i] : starts[i + 1]], pieces[i][...])
    out[...] = total.astype(bf16).reshape(out.shape)


def weight_grad(left, pieces, by_part=0):
    cols, rows = left.shape
    width = pieces[0].shape[1]
    parts = by_part or 4
    part = width // parts
    if by_part:
        out_spec = pl.BlockSpec((1, cols, part), lambda i: (i, 0, 0))
        out_shape = jax.ShapeDtypeStruct((parts, cols, part), bf16)
    else:
        out_spec = pl.BlockSpec((cols, part), lambda i: (0, i))
        out_shape = jax.ShapeDtypeStruct((cols, width), bf16)
    return pl.pallas_call(
        weight_grad_kernel,
        grid=(parts,),
        in_specs=[pl.BlockSpec((cols, rows), lambda i: (0, 0))]
        + [pl.BlockSpec((piece.shape[0], part), lambda i: (0, i)) for piece in pieces],
        out_specs=out_spec,
        out_shape=out_shape,
        compiler_params=pltpu.CompilerParams(vmem_limit_bytes=LARGE),
        cost_estimate=lasting(4 + cols / 100),
        name="weight_grad",
    )(left, *pieces)


def terms_kernel(count, turned, adds, scaled_by, far, *refs):
    lefts, weights = refs[:count], refs[count : 2 * count]
    rest = refs[2 * count :]
    norm = rest[0] if scaled_by else None
    got = rest[int(scaled_by) : int(scaled_by) + adds]
    outs = rest[int(scaled_by) + adds :]
    half = outs[0].shape[0]
    rows = 2 * half if far and adds else half
    for k in range(1 if far else ROWS - 1):
        at = slice(k * rows, (k + 1) * rows)
        total = None
        for i in range(count):
            product = (dot_cols if turned else dot)(lefts[i][at, :], weights[i][...])
            if i == 0 and scaled_by:
                product = product * norm[at, 0:1]
            total = product if total is None else total + product
        if adds:
            total = total + got[k][...].astype(f32)
        if adds and far:
            outs[0][...] = total[:half].astype(bf16)
            outs[1][...] = total[half:].astype(bf16)
        else:
            outs[k][...] = total.astype(outs[k].dtype)


def group_terms(lefts, weights, turned, core, far, got=(), norm=None):
    width = weights[0].shape[0 if turned else 1]
    rows = lefts[0].shape[0] // 8
    block = min(width, 512)
    if far:
        row_spec = lambda cols: pl.BlockSpec((rows, cols), lambda i: (core * ROWS + ROWS - 1, 0))
    else:
        row_spec = lambda cols: pl.BlockSpec((ROWS * rows, cols), lambda i: (core, 0))
    in_specs = [row_spec(left.shape[1]) for left in lefts]
    for weight in weights:
        if turned:
            in_specs.append(pl.BlockSpec((block, weight.shape[1]), lambda i: (i, 0)))
        else:
            in_specs.append(pl.BlockSpec((weight.shape[0], block), lambda i: (0, i)))
    operands = list(lefts) + list(weights)
    if norm is not None:
        in_specs.append(row_spec(8))
        operands.append(norm)
    piece = pl.BlockSpec((rows, block), lambda i: (0, i))
    in_specs += [piece] * len(got)
    if got:
        kinds = [(rows // 2, bf16)] * 2 if far else [(rows, f32)] * 3
    else:
        kinds = [(rows, bf16)] * (1 if far else 3)
    depth = sum(left.shape[1] for left in lefts)
    return pl.pallas_call(
        lambda *refs: terms_kernel(len(lefts), turned, len(got), norm is not None, far, *refs),
        grid=(width // block,),
        in_specs=in_specs,
        out_specs=[pl.BlockSpec((n, block), lambda i: (0, i)) for n, _ in kinds],
        out_shape=[jax.ShapeDtypeStruct((n, width), kind) for n, kind in kinds],
        compiler_params=pltpu.CompilerParams(vmem_limit_bytes=LARGE),
        cost_estimate=lasting(4 + depth / 180),
        name="group_terms",
    )(*operands, *got)


def spread(for_x, for_y, to_x, to_y):
    by_x, by_y = fold(for_x, for_y, to_x, to_y)
    return by_x, hop(by_x, 1), hop(by_y, 2)


def scatter_product(lefts, weights, turned=False, norm=None, give=False, meanwhile=None, beside=None):
    far_got = [twin(part) for part in group_terms(lefts, weights, turned, 1, True, norm=norm)]
    near_got = [twin(part) for part in group_terms(lefts, weights, turned, 1, False, norm=norm)]
    if beside is not None:
        near_got, beside = lax.optimization_barrier((near_got, beside))
    far_a, far_b = group_terms(lefts, weights, turned, 0, True, got=far_got, norm=norm)
    own, for_x, for_y = group_terms(lefts, weights, turned, 0, False, got=near_got, norm=norm)
    to_x, to_y = hop(far_a, 2), hop(far_b, 1)
    done = None
    if meanwhile is not None:
        done = meanwhile(own)
        to_x, to_y, done = lax.optimization_barrier((to_x, to_y, done))
    by_x, by_y = fold(for_x, for_y, to_x, to_y)
    sums = own, hop(by_x, 1), hop(by_y, 2)
    return (sums, done, beside, by_x) if give else sums


def fold_kernel(for_x, for_y, to_x, to_y, by_x, by_y):
    half = to_x.shape[0]
    by_x[:half, :] = (for_x[:half, :] + to_x[...].astype(f32)).astype(bf16)
    by_x[half:, :] = for_x[half:, :].astype(bf16)
    by_y[:half, :] = for_y[:half, :].astype(bf16)
    by_y[half:, :] = (for_y[half:, :] + to_y[...].astype(f32)).astype(bf16)


def fold(for_x, for_y, to_x, to_y):
    rows, width = for_x.shape
    block = min(width, 1024)
    spec = lambda n: pl.BlockSpec((n, block), lambda i: (0, i))
    return pl.pallas_call(
        fold_kernel,
        grid=(width // block,),
        in_specs=[spec(rows), spec(rows), spec(rows // 2), spec(rows // 2)],
        out_specs=[spec(rows), spec(rows)],
        out_shape=[jax.ShapeDtypeStruct((rows, width), bf16)] * 2,
        compiler_params=pltpu.CompilerParams(vmem_limit_bytes=VMEM),
        cost_estimate=lasting(2),
        name="fold",
    )(for_x, for_y, to_x, to_y)


def regroup(values, outer, part):
    count = values.shape[1] // part
    if count == 1:
        return values
    inner = count // outer
    order = [o * inner + i for i in range(inner) for o in range(outer)]
    return jnp.concatenate([values[:, k * part : (k + 1) * part] for k in order], axis=1)


def scaled_unit(values):
    scale = lax.rsqrt(jnp.mean(values * values, axis=1, keepdims=True) + EPSILON)
    return values * scale, scale


def norm_in_kernel(part, x, out):
    unit, _ = scaled_unit(x[...].astype(f32))
    out[...] = regroup(unit, ROWS, part).astype(bf16)


def norm_two_kernel(part, x, own, by_x, by_y, hidden_out, out):
    hidden = x[...].astype(f32) + own[...] + by_x[...].astype(f32) + by_y[...].astype(f32)
    hidden_out[...] = hidden
    unit, _ = scaled_unit(hidden)
    out[...] = regroup(unit, ROWS, part).astype(bf16)


def norm_back_kernel(part, values, own, by_x, by_y, base, *outs):
    unit, scale = scaled_unit(values[...].astype(f32))
    grad = own[...] + by_x[...].astype(f32) + by_y[...].astype(f32)
    grad = regroup(grad, grad.shape[1] // part // ROWS, part)
    mean = jnp.mean(grad * unit, axis=1, keepdims=True)
    total = base[...].astype(f32) + scale * (grad - unit * mean)
    for out in outs:
        out[...] = total.astype(out.dtype)


def on_rows(kernel, part, operands, kinds, name):
    rows, width = operands[0].shape
    step = rows // 2
    spec = pl.BlockSpec((step, width), lambda i: (i, 0))
    return pl.pallas_call(
        lambda *refs: kernel(part, *refs),
        grid=(2,),
        in_specs=[spec] * len(operands),
        out_specs=[spec] * len(kinds),
        out_shape=[jax.ShapeDtypeStruct((rows, width), kind) for kind in kinds],
        compiler_params=pltpu.CompilerParams(vmem_limit_bytes=VMEM),
        cost_estimate=lasting(4),
        name=name,
    )(*operands)


def turn(values, cosine, sine):
    return values * cosine + pltpu.roll(values, ATT_HEAD // 2, 1) * sine


def rope_kernel(where, query, key, value, cosine, sine, query_out, keyval_out):
    query_out[0, 0] = turn(query[0], cosine[0], sine[0]).astype(bf16)
    keyval_out[0, 0, :, :ATT_HEAD] = turn(key[0], cosine[0], sine[0]).astype(bf16)
    keyval_out[0, 0, :, ATT_HEAD:] = value[0].astype(bf16)


def rope_forward(where, proj, cosine, sine):
    def part(i):
        return pl.BlockSpec(
            (1, CHUNK, ATT_HEAD), lambda k, t, where: ((t ^ where[2]) * ROWS + k, 0, 4 + i)
        )

    angle = pl.BlockSpec((1, CHUNK, ATT_HEAD), lambda k, t, where: (t ^ where[2], 0, 0))
    return pl.pallas_call(
        rope_kernel,
        grid_spec=pltpu.PrefetchScalarGridSpec(
            num_scalar_prefetch=1,
            grid=(ROWS, 2),
            in_specs=[part(0), part(1), part(2), angle, angle],
            out_specs=[
                pl.BlockSpec((1, 1, CHUNK, ATT_HEAD), lambda k, t, where: (t ^ where[2], k, 0, 0)),
                pl.BlockSpec((1, 1, CHUNK, 2 * ATT_HEAD), lambda k, t, where: (k, t, 0, 0)),
            ],
        ),
        out_shape=[
            jax.ShapeDtypeStruct((2, ROWS, CHUNK, ATT_HEAD), bf16),
            jax.ShapeDtypeStruct((ROWS, 2, CHUNK, 2 * ATT_HEAD), bf16),
        ],
        compiler_params=pltpu.CompilerParams(vmem_limit_bytes=VMEM),
        cost_estimate=lasting(3),
        name="rope_forward",
    )(where, proj, proj, proj, cosine, sine)


def rope_back_kernel(where, query, keyval, cosine, sine, out):
    core, turned = cosine[0], -sine[0]
    out[0, :, :ATT_HEAD] = turn(query[0, 0], core, turned).astype(bf16)
    mine = pl.program_id(0) // 2 == where[2]
    both = jnp.where(mine, keyval[0, 0], 0.0)
    out[0, :, ATT_HEAD : 2 * ATT_HEAD] = turn(both[:, :ATT_HEAD], core, turned).astype(bf16)
    out[0, :, 2 * ATT_HEAD :] = both[:, ATT_HEAD:].astype(bf16)


def rope_back(where, query, keyval, cosine, sine):
    angle = pl.BlockSpec((1, CHUNK, ATT_HEAD), lambda k, t, where: (t ^ where[2], 0, 0))
    return pl.pallas_call(
        rope_back_kernel,
        grid_spec=pltpu.PrefetchScalarGridSpec(
            num_scalar_prefetch=1,
            grid=(ROWS, 2),
            in_specs=[
                pl.BlockSpec((1, 1, CHUNK, ATT_HEAD), lambda k, t, where: (t ^ where[2], k, 0, 0)),
                pl.BlockSpec((1, 1, CHUNK, 2 * ATT_HEAD), lambda k, t, where: (k % 2, t, 0, 0)),
                angle,
                angle,
            ],
            out_specs=pl.BlockSpec(
                (1, CHUNK, 3 * ATT_HEAD), lambda k, t, where: ((t ^ where[2]) * ROWS + k, 0, 0)
            ),
        ),
        out_shape=jax.ShapeDtypeStruct((2 * ROWS, CHUNK, 3 * ATT_HEAD), bf16),
        compiler_params=pltpu.CompilerParams(vmem_limit_bytes=VMEM),
        cost_estimate=lasting(3),
        name="rope_back",
    )(where, query, keyval, cosine, sine)


def feed_kernel(count, *refs):
    n2, g = refs[:count], refs[count : 2 * count]
    w_gu, w_down, act_out, grad_out, held_n, held_g, arrived_n, arrived_g = refs[2 * count :]
    copies_n, starts = fetch(n2, held_n, arrived_n)
    copies_g, _ = fetch(g, held_g, arrived_g)
    own = w_down.shape[0]
    for (i, at), _ in zip(by_pair(copies_n, starts), by_pair(copies_g, starts)):
        both = dot(held_n[at, :], w_gu[...])
        gate, up = both[:, :own], both[:, own:]
        sig = sigmoid_of(gate)
        silu = gate * sig
        act_out[at, :] = (silu * up).astype(bf16)
        grad = dot_cols(held_g[at, :], w_down[...])
        grad_out[at, :own] = (grad * up * (sig * (1.0 + gate * (1.0 - sig)))).astype(bf16)
        grad_out[at, own:] = (grad * silu).astype(bf16)


def feed(n2, g, w_gu, w_down):
    own, width = w_down.shape
    count, rows = len(n2), 8 * CHUNK
    return pl.pallas_call(
        lambda *refs: feed_kernel(count, *refs),
        in_specs=[ANY] * (2 * count) + [IN_VMEM] * 2,
        out_specs=[IN_VMEM] * 2,
        out_shape=[
            jax.ShapeDtypeStruct((rows, own), bf16),
            jax.ShapeDtypeStruct((rows, 2 * own), bf16),
        ],
        scratch_shapes=[
            pltpu.VMEM((rows, width), bf16),
            pltpu.VMEM((rows, width), bf16),
            pltpu.SemaphoreType.DMA((count,)),
            pltpu.SemaphoreType.DMA((count,)),
        ],
        compiler_params=pltpu.CompilerParams(vmem_limit_bytes=LARGE),
        cost_estimate=lasting(23),
        name="feed",
    )(*n2, *g, w_gu, w_down)


def per_device(
    tokens,
    segments,
    cotangent,
    norm_gain,
    gating_weight,
    input_weight,
    state_weight,
    step_weight,
    conv_weight,
    conv_bias,
    step_bias,
    decay_log,
    skip_gain,
    ssm_gain,
    out_weight,
    query_weight,
    keyval_weight,
    context_weight,
    mlp_gain,
    gate_weight,
    up_weight,
    down_weight,
):
    zs = lax.axis_size("z")
    b = lax.axis_index("b")
    z = lax.axis_index("z")
    c = lax.axis_index("c")
    rank = 2 * b + c
    rows = tokens.shape[1]
    width = tokens.shape[2]
    share = norm_gain.shape[0]
    ssm_width = HEADS * SSM_HEAD
    score_scale = 1.0 / math.sqrt(ATT_HEAD)

    def to_z(values):
        return (
            values.reshape(rows, ROWS, zs, 2 * share).transpose(0, 2, 1, 3).reshape(rows, width)
        )

    def from_z(values):
        return (
            values.reshape(rows, zs, ROWS, 2 * share).transpose(0, 2, 1, 3).reshape(rows, width)
        )

    def swap(values):
        return jnp.where(c == 0, values, values[::-1])

    def to_ranks(values):
        return lax.all_to_all(values, ("b", "c"), split_axis=0, concat_axis=0, tiled=True)

    def to_owner(values):
        mine = lax.psum_scatter(values, "z", scatter_dimension=0, tiled=True)[0]
        return mine.T.reshape(RANKS, share, -1)

    def along_z(values):
        return lax.all_gather(values, "z", axis=0, tiled=True)

    def owner_z(values):
        return lax.psum_scatter(values, "z", scatter_dimension=0, tiled=True)

    x = tokens[0]
    cot = cotangent[0]
    aligned = 2 * share % 128 == 0
    block = 2 * share if aligned else width
    lined = (lambda v: v) if aligned else to_z
    unlined = (lambda v: v) if aligned else from_z
    gain_col = norm_gain.astype(f32)[:, None]
    gain2_col = mlp_gain.astype(f32)[:, None]
    ssm_gain_col = ssm_gain.astype(f32)[:, None]

    (n1_own,) = on_rows(norm_in_kernel, block, [x], [bf16], "norm_in")
    scaled = lambda w, gain: (w.astype(f32) * gain).astype(bf16)
    by_rank = lambda w: w.reshape(w.shape[0], RANKS, -1).transpose(1, 0, 2)
    group_kv = KVHEADS * ATT_HEAD
    kv_heads = keyval_weight.reshape(share, 2, KVHEADS, ATT_HEAD).transpose(2, 0, 1, 3)
    kv_rank = jnp.repeat(kv_heads.reshape(KVHEADS, share, 2 * ATT_HEAD), RANKS // KVHEADS, axis=0)
    pad_cols = 128 - OWN_STATE - 8
    chan = conv_bias.shape[0]
    small = jnp.concatenate(
        [segments[0].astype(bf16), conv_weight.reshape(-1), conv_bias.reshape(-1)]
    )
    small_count = small.shape[0]
    small = jnp.pad(small, (0, share * pad_cols - small_count)).reshape(share, pad_cols)
    w_a = jnp.concatenate(
        [
            by_rank(input_weight),
            by_rank(state_weight),
            by_rank(step_weight),
            jnp.zeros((RANKS, share, 8 - OWN_HEADS), bf16),
        ],
        axis=2,
    )
    riders = jnp.broadcast_to(small[None], (RANKS, share, pad_cols))
    w_b = jnp.concatenate([by_rank(query_weight), kv_rank], axis=2)
    w_c = by_rank(gating_weight)
    cols_a, cols_b, cols_c = w_a.shape[2] + pad_cols, w_b.shape[2], w_c.shape[2]
    own_ab = to_ranks(
        jnp.concatenate([scaled(w_a, gain_col[None]), riders, scaled(w_b, gain_col[None])], axis=2)
    )
    w_ab = along_z(own_ab)
    small = w_ab[..., cols_a - pad_cols : cols_a].reshape(zs, ROWS, 2, -1)[..., :small_count]
    w_ab = w_ab.reshape(width, cols_a + cols_b)
    wa, wb = w_ab[:, :cols_a], w_ab[:, cols_a:]
    def ff_ranks(w):
        return (
            w.reshape(w.shape[0], ROWS, zs, 2, -1)
            .transpose(1, 3, 0, 2, 4)
            .reshape(RANKS, w.shape[0], -1)
        )

    w_cgu = jnp.concatenate(
        [
            scaled(w_c, gain_col[None]),
            scaled(
                jnp.concatenate([ff_ranks(gate_weight), ff_ranks(up_weight)], axis=2),
                gain2_col[None],
            ),
        ],
        axis=2,
    )
    n1, w_cgu = gather_group(lined(n1_own), w_cgu)
    own_cgu = to_ranks(w_cgu)
    own_c, w_gu = own_cgu[..., :cols_c], own_cgu[..., cols_c:]
    own_ff = w_gu.shape[2] // 2

    row_out = out_weight.shape[0]
    row_ctx = context_weight.shape[0]
    w_oc = jnp.concatenate([scaled(out_weight, ssm_gain_col), context_weight], axis=0)[None]
    segs = small[..., :rows].transpose(1, 0, 2, 3).reshape(ROWS, zs * 2 * rows).astype(f32)
    segs_all = jnp.concatenate(
        [lax.dynamic_slice_in_dim(segs, k ^ b, 1, 0) for k in range(ROWS)], axis=0
    )
    conv_all = small[..., rows:].transpose(1, 0, 2, 3).reshape(-1, CONV + 1, chan).astype(f32)
    conv_all = conv_all.transpose(1, 0, 2).reshape(CONV + 1, -1)
    conv_own = jnp.concatenate(
        [
            lax.dynamic_slice_in_dim(conv_all, rank * OWN_SSM, OWN_SSM, 1),
            lax.dynamic_slice_in_dim(conv_all, ssm_width + rank * OWN_STATE, OWN_STATE, 1),
        ],
        axis=1,
    )
    seg_pad = jnp.concatenate([jnp.zeros((ROWS, rows), f32), segs_all], axis=1)
    seg_near = lax.dynamic_slice_in_dim(seg_pad, z * 2 * rows, 3 * rows, 1)
    seg_time = seg_near[:, rows:].reshape(ROWS, 2, rows).transpose(1, 0, 2)
    seg = swap(seg_time).reshape(2 * ROWS, rows)
    seg_before = seg_near[:, : 2 * rows].reshape(ROWS, 2, rows).transpose(1, 0, 2)
    seg_before = swap(seg_before).reshape(2 * ROWS, rows)
    marks = marks_of(seg, seg_before)
    seg_rows = jnp.broadcast_to(seg[:, None, :], (2 * ROWS, 8, rows))
    seg_query = marks.reshape(2, ROWS, rows, 8)
    seg_keys = segs_all.reshape(ROWS * zs, 1, 2 * rows)
    seg_keys = jnp.broadcast_to(seg_keys, (ROWS * zs, 8, 2 * rows))
    where = jnp.stack([b, z, c]).astype(jnp.int32)
    conv_own = jnp.pad(conv_own, ((0, 3), (0, LANES_A - OWN_CONV)))
    own_slice = lambda v: lax.dynamic_slice_in_dim(v.astype(f32), rank * OWN_HEADS, OWN_HEADS, 0)
    rate = -jnp.exp(own_slice(decay_log))
    head = jnp.pad(jnp.stack([own_slice(step_bias), rate]), ((0, 6), (0, 128 - OWN_HEADS)))
    skip_wide = jnp.broadcast_to(jnp.repeat(own_slice(skip_gain), SSM_HEAD)[None], (8, OWN_SSM))

    half_head = ATT_HEAD // 2
    frequency = jnp.exp(jnp.arange(half_head, dtype=f32) * (-2.0 * math.log(ROPE_BASE) / ATT_HEAD))
    core_place = (z * 2 + (jnp.arange(2) ^ c)) * rows
    places = (core_place[:, None] + jnp.arange(rows)[None, :]).astype(f32)
    angles = (places[:, :, None] * frequency).reshape(2, rows, half_head)
    cosine, sine = jnp.cos(angles), jnp.sin(angles)
    cosine = jnp.concatenate([cosine, cosine], axis=-1)
    sine = jnp.concatenate([-sine, sine], axis=-1)

    chunks = 2 * ROWS
    proj = times(n1, after(w_ab, own_cgu))
    g_all, proj = gather_group(after(cot, own_cgu), proj)
    query, keyval = rope_forward(where, proj, cosine, sine)
    own_kv = lax.dynamic_slice_in_dim(keyval, 2 * c, 2, 0).reshape(1, 2, 2 * rows, 2 * ATT_HEAD)
    kv_own = along_z(own_kv)

    def before_chunk(own_last, moved):
        return jnp.stack(
            [jnp.where(c == 0, moved, own_last[1]), jnp.where(c == 0, own_last[0], moved)]
        )

    tails = after(proj[:, rows - 8 :, :cols_a], where)
    tails = tails.reshape(2, ROWS, 8, cols_a).astype(bf16)
    last_core = jnp.where(c == 0, tails[1], tails[0])
    moved = zshift(last_core[:, 8 - CONV + 1 :], 1)
    moved = jnp.pad(moved, ((0, 0), (8 - CONV + 1, 0), (0, 0)))
    halo = before_chunk(tails, moved).reshape(chunks, 8, cols_a).astype(f32)
    xs, bc_own, slope, meta, meta_rows = conv_forward(proj, halo, marks, conv_own, head)
    mine = [bc_own] + [hop(bc_own, m) for m in range(1, ROWS)]
    mine = jnp.stack(mine)
    bc = jnp.concatenate([mine, twin(mine)], axis=0)
    wc = along_z(after(own_c, own_kv)).reshape(width, cols_c)

    passing = jnp.exp(meta[:, rows - 1, 8 : 8 + OWN_HEADS]) * marks[:, rows - 1, 1:2]
    pass_wide = swap(jnp.repeat(passing, SSM_HEAD, axis=1).reshape(2, ROWS, OWN_SSM, 1))
    p0, p1 = pass_wide[0], pass_wide[1]
    pass_both = p0 * p1
    first_local, both_local = local_states(where, xs, bc, meta, marks, p1)
    kv_other = twin(kv_own)
    state = jnp.zeros_like(both_local)
    for s in range(zs - 1):
        message = (pass_both * state + both_local).astype(bf16)
        if s == 1:
            query = after(query, message)
            context, context_low, logsum = attend(
                where, query, kv_own, kv_other, seg_query, seg_keys
            )
            gating = times(n1, after(wc, message))
        if s == zs - 2:
            w_oc = along_z(after(w_oc, message))
        moved = lax.ppermute(message, "z", [(s, s + 1)])
        if s == 0:
            moved, *g_all = lax.optimization_barrier((moved, *g_all))
        if s == 1:
            moved, context_low, gating = lax.optimization_barrier((moved, context_low, gating))
        state = state + moved.astype(f32)

    halves = w_oc.reshape(2, zs // 2, row_out + row_ctx, width)
    kept = lax.dynamic_index_in_dim(halves, c, 0, keepdims=False)
    sent = lax.dynamic_index_in_dim(halves, 1 - c, 0, keepdims=False)
    got = twin(sent)
    both = jnp.where(c == 0, jnp.stack([kept, got], 1), jnp.stack([got, kept], 1))
    w_out = both[:, :, :row_out].reshape(-1, width)
    w_ctx = both[:, :, row_out:].reshape(-1, width)
    w_gu_full = along_z(after(w_gu, state)).reshape(width, 2 * own_ff)
    w_down = along_z(after(down_weight, w_gu, state))

    ssm_out, gated_low, squares = ssm_forward(
        where, xs, bc, meta, meta_rows, marks, seg_rows, state, first_local, p0, gating, skip_wide
    )
    squares = sum_group(squares[:, 0].reshape(2, ROWS, rows))
    scale_ssm = lax.rsqrt(squares * (1.0 / ssm_width) + EPSILON).reshape(chunks, rows, 1)

    flat = lambda v: v.reshape(-1, v.shape[-1])
    norms = jnp.broadcast_to(scale_ssm.reshape(-1, 1), (chunks * rows, 8))
    mixed = scatter_product([flat(gated_low), flat(context_low)], [w_out, w_ctx], norm=norms)
    hidden, n2_own = on_rows(norm_two_kernel, block, [x, *mixed], [f32, bf16], "norm_two")

    n2 = gather_group(lined(n2_own))
    activation, grad_gu = feed(n2, g_all, w_gu_full, w_down)

    e2, grad_down_terms, _, folded = scatter_product(
        [grad_gu],
        [w_gu_full],
        turned=True,
        give=True,
        meanwhile=lambda own: weight_grad(after(activation, own).T, g_all),
    )
    grad_down = owner_z(grad_down_terms)
    grad_gu_terms = weight_grad(after(grad_gu, folded).T, n2, zs)
    *e2, grad_gu_terms = lax.optimization_barrier((*e2, grad_gu_terms))
    grad_gu_w = to_owner(grad_gu_terms)
    grad_hidden, grad_mix_own = on_rows(
        norm_back_kernel, block, [hidden, *map(unlined, e2), cot], [f32, bf16], "norm_back"
    )
    unit_low = (gated_low.astype(f32) * scale_ssm).astype(bf16)
    mixer_left = jnp.concatenate([flat(unit_low), flat(context_low)], axis=-1).T
    late = after(activation, grad_mix_own)
    late_other = [group_terms([late], [w_down], False, 1, far) for far in (True, False)]

    def late_sums(meanwhile):
        other, left = meanwhile
        far_got, near_got = [[twin(part) for part in parts] for parts in other]
        return (
            group_terms([late], [w_down], False, 0, True, got=far_got),
            group_terms([late], [w_down], False, 0, False, got=near_got),
            left,
        )

    grad_mix, ((far_a, far_b), (late_own, for_x, for_y), mixer_left) = gather_group(
        grad_mix_own, (late_other, mixer_left), late_sums
    )
    to_x, to_y = hop(far_a, 2), hop(far_b, 1)
    es, grad_context, es_sum = mixer_back(
        grad_mix, after(w_out, late_own, far_a, mixer_left), w_ctx, ssm_out, gating
    )
    grad_oc_w = weight_grad(after(mixer_left, es_sum), grad_mix)
    es_sum = es_sum[:, 0] * scale_ssm[..., 0]
    es_mean = sum_group(es_sum.reshape(2, ROWS, rows)) * (1.0 / ssm_width)
    scales = jnp.pad(
        jnp.stack([scale_ssm[..., 0], es_mean.reshape(chunks, rows)], axis=-1),
        ((0, 0), (0, 0), (0, 6)),
    )
    scales, to_x, to_y, grad_oc_w = lax.optimization_barrier((scales, to_x, to_y, grad_oc_w))
    gy, grad_gating, later_grad, both_grad = gate_back(
        where, es, scales, gating, ssm_out, bc, meta, marks, p0
    )

    def out_grads(grad_oc_w):
        grad_out_rows = grad_oc_w[:OWN_SSM].reshape(zs // 2, 2, row_out, width)
        grad_ctx_rows = grad_oc_w[OWN_SSM:].reshape(zs // 2, 2, row_ctx, width)
        grad_oc = jnp.concatenate([grad_out_rows, grad_ctx_rows], axis=2)
        oc_kept = lax.dynamic_index_in_dim(grad_oc, c, 1, keepdims=False)
        oc_got = twin(lax.dynamic_index_in_dim(grad_oc, 1 - c, 1, keepdims=False))
        return jnp.where(
            c == 0,
            jnp.concatenate([oc_kept, oc_got], axis=0),
            jnp.concatenate([oc_got, oc_kept], axis=0),
        )

    flowing = jnp.zeros_like(both_grad)
    grad_c_low = flat(grad_gating)
    for s in range(zs - 1, 0, -1):
        message = (pass_both * flowing + both_grad).astype(bf16)
        if s == 1:
            grad_context = after(grad_context, message).reshape(2, ROWS, rows, ATT_HEAD)
            grad_query, grad_kv = attend_back(
                where, query, kv_own, kv_other, seg_query, seg_keys, grad_context, context, logsum
            )
            grad_wc_terms = weight_grad(after(grad_c_low, message).T, n1, zs)
        moved = lax.ppermute(message, "z", [(s, s - 1)])
        if s == zs - 1:
            late_folded, late_x, late_y = spread(for_x, for_y, to_x, to_y)
            moved, late_folded = lax.optimization_barrier((moved, late_folded))
        if s == zs - 2:
            got_gu = to_ranks(after(grad_gu_w, message, grad_down))
            oc_all = out_grads(after(grad_oc_w, message))
            moved, got_gu, oc_all = lax.optimization_barrier((moved, got_gu, oc_all))
        if s == 1:
            moved, grad_query, grad_kv, grad_wc_terms, late_x, late_y = lax.optimization_barrier(
                (moved, grad_query, grad_kv, grad_wc_terms, late_x, late_y)
            )
        flowing = flowing + moved.astype(f32)
    grad_wc = to_owner(grad_wc_terms)

    kv_kept = lax.dynamic_slice_in_dim(grad_kv, 2 * c, 2, 1).astype(f32)
    kv_got = twin(lax.dynamic_slice_in_dim(grad_kv, 2 - 2 * c, 2, 1)).astype(f32)
    kv_terms = (kv_kept + kv_got).astype(bf16)
    kv_grad = owner_z(kv_terms)
    kv_grad = kv_grad[0].astype(f32)
    grad_b_low = rope_back(
        where, grad_query, kv_grad.reshape(2, 2, rows, 2 * ATT_HEAD), cosine, sine
    )
    grad_b_low = flat(grad_b_low)
    grad_wb_terms = weight_grad(grad_b_low.T, n1, zs)
    grad_wb = to_owner(grad_wb_terms)

    got_gu = got_gu.astype(f32)
    grad_xs, *bc_terms, grad_step, head_sums = ssm_back(
        where, xs, gy, bc, meta, meta_rows, marks, seg_rows, state, first_local, flowing, later_grad,
        p0, p1, skip_wide, head,
    )
    got = twin(jnp.stack(bc_terms[ROWS:])).astype(f32)
    bc_sums = [bc_terms[k].astype(f32) + got[k] for k in range(ROWS)]
    grad_bc = bc_sums[0]
    for k in range(1, ROWS):
        grad_bc = grad_bc + hop(bc_sums[k].astype(bf16), k).astype(f32)

    near = CONV - 1
    bc_near = grad_bc[:, :near].reshape(ROWS, near, 2, PIECE).transpose(2, 0, 1, 3)
    grad_near = jnp.concatenate(
        [grad_xs[:, :near], bc_near.reshape(chunks, near, PIECE)], axis=-1
    )
    grad_near = grad_near * slope[:, :near, :OWN_CONV]
    give = jnp.zeros((chunks, near, OWN_CONV), f32)
    for o in range(near):
        masked = grad_near[:, : near - o] * marks[:, : near - o, 3 + o : 4 + o]
        give = give + jnp.pad(masked * conv_own[o, :OWN_CONV], ((0, 0), (o, 0), (0, 0)))
    give = give.reshape(2, ROWS, near, OWN_CONV)
    moved = zshift(jnp.where(c == 0, give[0], give[1]).astype(bf16), -1).astype(f32)
    given = jnp.stack(
        [jnp.where(c == 0, give[1], moved), jnp.where(c == 0, moved, give[0])]
    ).reshape(chunks, near, OWN_CONV)
    given = after(given, grad_wb_terms)
    given = jnp.pad(given, ((0, 0), (8 - near, 0), (0, LANES_A - OWN_CONV)))
    grad_a_low, conv_sums = conv_backward(
        grad_xs, grad_bc, grad_step, slope, proj, halo, marks, given, conv_own
    )
    grad_a_low = flat(grad_a_low)
    conv_sums = jnp.sum(conv_sums, axis=0)[: CONV + 1, :OWN_CONV]
    head_sums = jnp.sum(head_sums, axis=0)[:3, :OWN_HEADS] * jnp.stack(
        [jnp.ones_like(rate), rate, jnp.ones_like(rate)]
    )
    head_sums = jnp.pad(head_sums.reshape(1, -1), ((0, 0), (0, OWN_CONV - 3 * OWN_HEADS)))

    def all_sums(sums):
        total = sums
        for flip in range(1, zs):
            total = total + zhop(sums, flip)
        table = jnp.stack([total, twin(total)])
        return jnp.concatenate([table] + [hop(table, flip) for flip in range(1, ROWS)], axis=0)

    grad_wa_terms = weight_grad(grad_a_low.T, n1, zs)
    grad_a_low = after(grad_a_low, grad_wa_terms)
    sums = jnp.concatenate([conv_sums, head_sums], axis=0)
    e1, table, _, e1_folded = scatter_product(
        [grad_c_low, grad_b_low, grad_a_low],
        [wc, wb, wa],
        turned=True,
        give=True,
        meanwhile=lambda own: all_sums(sums),
    )
    grad_wa = to_owner(grad_wa_terms)
    late_own = after(late_own, e1_folded)
    result = (hidden + late_own + late_x.astype(f32) + late_y.astype(f32)).astype(bf16)
    grad_oc_own = owner_z(after(oc_all, grad_wa_terms))[0].astype(f32)
    got = to_ranks(after(jnp.concatenate([grad_wa, grad_wb, grad_wc], axis=2), e1_folded))

    def unrank(values):
        return values.transpose(1, 0, 2).reshape(share, -1)

    def ff_unrank(values):
        return (
            values.reshape(ROWS, 2, share, zs, own_ff // zs)
            .transpose(2, 0, 3, 1, 4)
            .reshape(share, -1)
        )

    def gain_grad(pairs):
        return sum(jnp.sum(w.astype(f32) * d, axis=1) for w, d in pairs)

    d_gate, d_up = ff_unrank(got_gu[..., :own_ff]), ff_unrank(got_gu[..., own_ff:])
    d_out, d_ctx = grad_oc_own[:row_out], grad_oc_own[row_out:]
    ready = (
        gain_grad(((gate_weight, d_gate), (up_weight, d_up))),
        d_gate * gain2_col,
        d_up * gain2_col,
        grad_down.astype(f32),
        result,
    )
    *e1, got, ready = lax.optimization_barrier((*e1, got, ready))
    got_a, got_bc = got[..., :cols_a], got[..., cols_a:]
    d_mlp_gain, d_gate, d_up, d_down, result = ready
    d_ssm_gain = gain_grad(((out_weight, d_out),))
    (grad_x,) = on_rows(
        norm_back_kernel, block, [x, *map(unlined, e1), grad_hidden], [bf16], "norm_back_in"
    )

    got_bc = got_bc.astype(f32)
    got_b, got_c = got_bc[..., :cols_b], got_bc[..., cols_b:]
    d_query = unrank(got_b[..., :ATT_HEAD])
    d_kv = got_b[..., ATT_HEAD:].reshape(KVHEADS, RANKS // KVHEADS, share, 2, ATT_HEAD).sum(1)
    d_kv = d_kv.transpose(1, 2, 0, 3).reshape(share, 2 * group_kv)
    d_gating = unrank(got_c)
    gain_part = gain_grad(
        ((gating_weight, d_gating), (query_weight, d_query), (keyval_weight, d_kv))
    )
    ready = (gain_part, d_query * gain_col, d_kv * gain_col, d_gating * gain_col)
    gain_part, d_query, d_kv, d_gating = ready
    got_a = got_a.astype(f32)
    d_input = unrank(got_a[..., :OWN_SSM])
    d_state = unrank(got_a[..., OWN_SSM:OWN_CONV])
    d_step = unrank(got_a[..., OWN_CONV : OWN_CONV + OWN_HEADS])
    d_norm_gain = gain_part + gain_grad(
        ((input_weight, d_input), (state_weight, d_state), (step_weight, d_step))
    )

    place = jnp.arange(RANKS)
    chosen = ((place ^ rank)[:, None] == place[None, :]).astype(f32)
    table = jnp.einsum("rs,sof->rof", chosen, table, precision=HIGH)
    conv_ssm = table[:, : CONV + 1, :OWN_SSM].transpose(1, 0, 2).reshape(CONV + 1, -1)
    conv_state = table[:, : CONV + 1, OWN_SSM:].transpose(1, 0, 2).reshape(CONV + 1, -1)
    conv_full = jnp.concatenate([conv_ssm, conv_state], axis=1)
    conv_mine = lax.dynamic_slice_in_dim(conv_full, (rank // 2 * zs * 2 + z * 2 + c) * chan, chan, 1)
    heads = table[:, CONV + 1, : 3 * OWN_HEADS].reshape(RANKS, 3, OWN_HEADS)
    heads = heads.transpose(1, 0, 2).reshape(3, HEADS)

    return (
        result[None],
        grad_x[None],
        d_norm_gain,
        d_gating,
        d_input * gain_col,
        d_state * gain_col,
        d_step * gain_col,
        conv_mine[:CONV],
        conv_mine[CONV],
        heads[0],
        heads[1],
        heads[2],
        d_ssm_gain,
        d_out * ssm_gain_col,
        d_query,
        d_kv,
        d_ctx,
        d_mlp_gain,
        d_gate,
        d_up,
        d_down,
    )


def solution(mesh):
    places = mesh.devices.reshape(ROWS, mesh.shape["seq"] // 2, 2)
    split = Mesh(places, ("b", "z", "c"))
    everywhere = ("b", "z", "c")
    row = P(everywhere, None)
    vector = P(everywhere)
    token = P("b", ("z", "c"), None)
    return jax.shard_map(
        per_device,
        mesh=split,
        in_specs=(
            token,
            P("b", ("z", "c")),
            token,
            vector,
            row,
            row,
            row,
            row,
            P(None, everywhere),
            vector,
            P(),
            P(),
            P(),
            vector,
            row,
            row,
            row,
            row,
            vector,
            row,
            row,
            row,
        ),
        out_specs=(
            token,
            token,
            vector,
            row,
            row,
            row,
            row,
            P(None, everywhere),
            vector,
            P(),
            P(),
            P(),
            vector,
            row,
            row,
            row,
            row,
            vector,
            row,
            row,
            row,
        ),
        check_vma=False,
    )
```

```python
import math

import jax
import jax.numpy as jnp
from jax import lax
from jax.experimental import pallas as pl
from jax.experimental.pallas import tpu as pltpu
from jax.sharding import Mesh
from jax.sharding import PartitionSpec as P

HEADS = 48
SSM_HEAD = 64
STATE = 256
CONV = 4
QHEADS = 8
KVHEADS = 2
ATT_HEAD = 128
EPSILON = 1e-05
ROPE_BASE = 10000.0
NEG_BIG = -1e30
HIGH = lax.Precision.HIGHEST

RANKS = 8
ROWS = 4
OWN_HEADS = HEADS // RANKS
OWN_SSM = OWN_HEADS * SSM_HEAD
OWN_STATE = 2 * STATE // RANKS
OWN_CONV = OWN_SSM + OWN_STATE

bf16 = jnp.bfloat16
f32 = jnp.float32


ANY = pl.BlockSpec(memory_space=pl.ANY)
IN_VMEM = pl.BlockSpec(memory_space=pltpu.VMEM)
CHUNK = 256
LANES_A = 512
STEP_AT = OWN_CONV
PIECE = OWN_STATE
HALF = 2 * CHUNK


def dot(left, right, dims=((1,), (0,))):
    return lax.dot_general(left, right, (dims, ((), ())), preferred_element_type=f32)


def dot_rows(left, right):
    return dot(left, right, ((0,), (0,)))


def dot_cols(left, right):
    return dot(left, right, ((1,), (1,)))


def bdot(left, right, lc, rc):
    return lax.dot_general(
        left, right, (((lc,), (rc,)), ((0,), (0,))), preferred_element_type=f32
    )


def hop(values, flip):
    return lax.ppermute(values, "b", [(i, i ^ flip) for i in range(ROWS)])


def twin(values):
    return lax.ppermute(values, "c", [(0, 1), (1, 0)])


def zhop(values, flip):
    return lax.ppermute(values, "z", [(i, i ^ flip) for i in range(lax.axis_size("z"))])


def zshift(values, step):
    size = lax.axis_size("z")
    return lax.ppermute(
        values, "z", [(i, i + step) for i in range(size) if 0 <= i + step < size]
    )


def after(values, *earlier):
    return lax.optimization_barrier((values,) + earlier)[0]


def gather_group(own, meanwhile=None, then=None):
    half = own.shape[0] // 2
    by_x = hop(own, 1)
    by_y = hop(own, 2)
    if meanwhile is not None:
        by_x, by_y, meanwhile = lax.optimization_barrier((by_x, by_y, meanwhile))
    far = hop(by_x[:half], 2), hop(by_y[half:], 1)
    if then is not None:
        *far, meanwhile = lax.optimization_barrier((*far, then(meanwhile)))
    mine = [own, by_x, by_y, *far]
    pieces = mine + [twin(part) for part in mine]
    return pieces if meanwhile is None else (pieces, meanwhile)


def starts_of(pieces):
    starts = [0]
    for piece in pieces:
        starts.append(starts[-1] + piece.shape[0])
    return starts


def reslot(values, flip, axis):
    order = [k ^ flip for k in range(ROWS)]
    return jnp.concatenate(
        [lax.slice_in_dim(values, k, k + 1, axis=axis) for k in order], axis=axis
    )


def sum_group(values):
    values = values + twin(values)[::-1]
    total = values
    for flip in range(1, ROWS):
        total = total + reslot(hop(values, flip), flip, 1)
    return total


def silu_slope(values):
    sigmoid = jax.nn.sigmoid(values)
    return sigmoid * (1.0 + values * (1.0 - sigmoid))


def rms_scale(values):
    return lax.rsqrt(jnp.mean(values * values, axis=-1, keepdims=True) + EPSILON)


def rotate(values, cosine, sine):
    half = values.shape[-1] // 2
    first = values[..., :half]
    second = values[..., half:]
    return jnp.concatenate([first * cosine - second * sine, second * cosine + first * sine], axis=-1)


def split(values, count):
    terms = []
    for _ in range(count):
        low = values.astype(bf16)
        terms.append(low)
        values = values - low.astype(f32)
    return terms


def exact(ones, values, dims=((1,), (0,)), count=3):
    return sum(dot(ones.astype(bf16), term, dims) for term in split(values, count))


def head_map(rows, cols, along):
    channel = lax.broadcasted_iota(jnp.int32, (rows, cols), along)
    head = lax.broadcasted_iota(jnp.int32, (rows, cols), 1 - along)
    return (channel // SSM_HEAD == head).astype(bf16)


def widen(values):
    rows = values.shape[0]
    first = lax.broadcasted_iota(jnp.int32, (rows, 2 * SSM_HEAD), 1) < SSM_HEAD
    parts = []
    for h in range(0, OWN_HEADS, 2):
        left = jnp.broadcast_to(values[:, h : h + 1], first.shape)
        right = jnp.broadcast_to(values[:, h + 1 : h + 2], first.shape)
        parts.append(jnp.where(first, left, right))
    return jnp.concatenate(parts, axis=1)


def narrow(values):
    ones = head_map(OWN_SSM, 8, 0)
    return sum(dot(term, ones) for term in split(values, 2))


def row_sums(values):
    ones = jnp.ones((8, values.shape[1]), bf16)
    return exact(ones, values, ((1,), (1,)), 2)


def sigmoid_of(values):
    return 1.0 / (1.0 + jnp.exp(-values))


def tri(lower):
    t = lax.broadcasted_iota(jnp.int32, (CHUNK, CHUNK), 0)
    s = lax.broadcasted_iota(jnp.int32, (CHUNK, CHUNK), 1)
    return (t >= s) if lower else (t <= s)


def conv_kernel(proj, halo, marks, conv, head, xs_out, bc_out, slope_out, meta_out, row_out, ext):
    ext[0:8, :] = halo[0]
    ext[8:, :] = proj[0].astype(bf16).astype(f32)
    pre = conv[4:5, :] + conv[3:4, :] * ext[8 : 8 + CHUNK, :]
    for o in range(CONV - 1):
        pre = pre + conv[o : o + 1, :] * ext[5 + o : 5 + o + CHUNK, :] * marks[0, :, 3 + o : 4 + o]
    sig = sigmoid_of(pre)
    act = (pre * sig).astype(bf16)
    xs_out[0] = act[:, :OWN_SSM]
    for r in range(2):

        @pl.when(pl.program_id(1) == r)
        def _():
            bc_out[0, :, r * PIECE : (r + 1) * PIECE] = act[:, OWN_SSM:OWN_CONV]

    slope_out[0] = sig * (1.0 + pre * (1.0 - sig))
    raw = proj[0][:, STEP_AT : STEP_AT + 8] + head[0:1, 0:8]
    real = lax.broadcasted_iota(jnp.int32, (CHUNK, 8), 1) < OWN_HEADS
    step = jnp.maximum(raw, 0.0) + jnp.log(1.0 + jnp.exp(-jnp.abs(raw)))
    step = jnp.where(real, step, 0.0)
    cum = exact(tri(True), step * head[1:2, 0:8])
    meta = jnp.concatenate(
        [step, cum, sigmoid_of(raw), jnp.zeros((CHUNK, 104), f32)], axis=1
    )
    meta_out[0] = meta[:, :32]
    row_out[0] = meta.T[:16]


def marks_kernel(own, before, out):
    lane = lax.broadcasted_iota(jnp.int32, (1, CHUNK), 1)
    for q in range(own.shape[0]):
        seg, prev = own[q : q + 1, :], before[q : q + 1, :]
        rows = [seg, (seg == prev[:, CHUNK - 1 :]).astype(f32), (seg == seg[:, CHUNK - 1 :]).astype(f32)]
        for o in range(CONV - 1):
            by = CONV - 1 - o
            moved = jnp.where(lane < by, pltpu.roll(prev, by, 1), pltpu.roll(seg, by, 1))
            rows.append((moved == seg).astype(f32))
        rows.append(jnp.zeros((128 - len(rows), CHUNK), f32))
        out[q] = jnp.concatenate(rows, axis=0).T[:, :8]


def marks_of(own, before):
    chunks = own.shape[0]
    return pl.pallas_call(
        marks_kernel,
        in_specs=[IN_VMEM] * 2,
        out_specs=IN_VMEM,
        out_shape=jax.ShapeDtypeStruct((chunks, CHUNK, 8), f32),
        compiler_params=pltpu.CompilerParams(vmem_limit_bytes=VMEM),
        cost_estimate=lasting(3),
        name="marks",
    )(own, before)


def conv_forward(proj, halo, marks, conv, head):
    block = lambda *shape: pl.BlockSpec((1,) + shape, lambda k, r: (r * ROWS + k, 0, 0))
    whole = pl.BlockSpec((8, LANES_A), lambda k, r: (0, 0))
    chunks = proj.shape[0]
    return pl.pallas_call(
        conv_kernel,
        grid=(ROWS, 2),
        in_specs=[
            block(CHUNK, LANES_A),
            block(8, LANES_A),
            block(CHUNK, 8),
            whole,
            pl.BlockSpec((8, 128), lambda k, r: (0, 0)),
        ],
        out_specs=[
            block(CHUNK, OWN_SSM),
            pl.BlockSpec((1, CHUNK, 2 * PIECE), lambda k, r: (k, 0, 0)),
            block(CHUNK, LANES_A),
            block(CHUNK, 32),
            block(16, CHUNK),
        ],
        out_shape=[
            jax.ShapeDtypeStruct((chunks, CHUNK, OWN_SSM), bf16),
            jax.ShapeDtypeStruct((ROWS, CHUNK, 2 * PIECE), bf16),
            jax.ShapeDtypeStruct((chunks, CHUNK, LANES_A), f32),
            jax.ShapeDtypeStruct((chunks, CHUNK, 32), f32),
            jax.ShapeDtypeStruct((chunks, 16, CHUNK), f32),
        ],
        scratch_shapes=[pltpu.VMEM((8 + CHUNK, LANES_A), f32)],
        compiler_params=pltpu.CompilerParams(vmem_limit_bytes=VMEM),
        cost_estimate=lasting(8),
        name="conv_forward",
    )(proj, halo, marks, conv, head)


VMEM = 60 * 1024 * 1024


def lasting(microseconds):
    return pl.CostEstimate(
        flops=0, bytes_accessed=int(microseconds * 1.1e6), transcendentals=0
    )


def time_spec(shape, backward=False):
    def at(k, t, where):
        core = (1 - t if backward else t) ^ where[2]
        return (core * ROWS + k,) + (0,) * len(shape)

    return pl.BlockSpec((1,) + tuple(shape), at)


def slot_spec(shape):
    return pl.BlockSpec((1,) + tuple(shape), lambda k, t, where: (k,) + (0,) * len(shape))


def piece_specs(kind):
    def spec(i):
        def at(k, t, where):
            slot = (i // 2 + 2 * kind) ^ (2 * (where[0] // 2))
            return (i % 2 * ROWS + slot, k ^ slot, 0, 0)

        return pl.BlockSpec((1, 1, CHUNK, 2 * PIECE), at)

    return [spec(i) for i in range(4)]


def core_of(where, backward=False):
    t = pl.program_id(1)
    return (1 - t if backward else t) ^ where[2]


def joined(pieces, core):
    parts = []
    for i, piece in enumerate(pieces):
        both = piece[0, 0]
        parts.append(jnp.where(core ^ (i % 2) == 0, both[:, :PIECE], both[:, PIECE:]))
    return jnp.concatenate(parts, axis=1)


def tails_of(meta, marks):
    step, cum = meta[0, :, 0:8], meta[0, :, 8:16]
    last = cum[CHUNK - 1 : CHUNK]
    decay = jnp.exp(last - cum) * marks[0, :, 2:3]
    return step, cum, decay, decay * step


def local_kernel(where, xs, b0, b1, b2, b3, meta, marks, p1, first_out, both_out):
    _, _, _, tail = tails_of(meta, marks)
    weighted = (xs[0].astype(f32) * widen(tail)).astype(bf16)
    local = dot_rows(weighted, joined((b0, b1, b2, b3), core_of(where)))

    @pl.when(pl.program_id(1) == 0)
    def _():
        first_out[0] = local

    @pl.when(pl.program_id(1) == 1)
    def _():
        both_out[0] = p1[0] * first_out[0] + local


def local_states(where, xs, bc, meta, marks, p1):
    state = jax.ShapeDtypeStruct((ROWS, OWN_SSM, STATE), f32)
    return pl.pallas_call(
        local_kernel,
        grid_spec=pltpu.PrefetchScalarGridSpec(
            num_scalar_prefetch=1,
            grid=(ROWS, 2),
            in_specs=[time_spec((CHUNK, OWN_SSM))]
            + piece_specs(0)
            + [time_spec((CHUNK, 32)), time_spec((CHUNK, 8)), slot_spec((OWN_SSM, 1))],
            out_specs=[slot_spec((OWN_SSM, STATE))] * 2,
        ),
        out_shape=[state, state],
        compiler_params=pltpu.CompilerParams(vmem_limit_bytes=VMEM),
        cost_estimate=lasting(8),
        name="local_states",
    )(where, xs, bc, bc, bc, bc, meta, marks, p1)


def decay_of(meta, row, allowed, h):
    spread = meta[0, :, 8 + h : 9 + h] - row[0, 8 + h : 9 + h, :]
    return jnp.exp(jnp.where(allowed, spread, NEG_BIG))


def ssm_kernel(
    where, xs, b0, b1, b2, b3, c0, c1, c2, c3, meta, row, marks, segs, state, first, p0, gating, skip,
    out, gated_out, square_out, work,
):
    later = pl.program_id(1) == 1
    core = core_of(where)
    b_mat, c_mat = joined((b0, b1, b2, b3), core), joined((c0, c1, c2, c3), core)
    inner = dot_cols(c_mat, b_mat)
    allowed = (marks[0, :, 0:1] == segs[0, 0:1, :]) & tri(True)
    xs_f = xs[0].astype(f32)
    step, cum = meta[0, :, 0:8], meta[0, :, 8:16]
    stepped = (xs_f * widen(step)).astype(bf16)
    entering = jnp.where(later, p0[0] * state[0] + first[0], state[0]).astype(bf16)
    entry = widen(jnp.exp(cum) * marks[0, :, 1:2])
    for h in range(OWN_HEADS):
        at = slice(h * SSM_HEAD, (h + 1) * SSM_HEAD)
        mix = (inner * decay_of(meta, row, allowed, h)).astype(bf16)
        work[:, at] = dot(mix, stepped[:, at])
    total = work[...] + dot_cols(c_mat, entering) * entry + skip[0:1, :] * xs_f
    out[0] = total
    gate = gating[0]
    gated = total * gate * sigmoid_of(gate)
    gated_out[0] = gated.astype(bf16)
    square_out[0] = row_sums(gated * gated)


def ssm_forward(where, xs, bc, meta, row, marks, segs, state, first, p0, gating, skip):
    chunks = xs.shape[0]
    return pl.pallas_call(
        ssm_kernel,
        grid_spec=pltpu.PrefetchScalarGridSpec(
            num_scalar_prefetch=1,
            grid=(ROWS, 2),
            in_specs=[time_spec((CHUNK, OWN_SSM))]
            + piece_specs(0)
            + piece_specs(1)
            + [
                time_spec((CHUNK, 32)),
                time_spec((16, CHUNK)),
                time_spec((CHUNK, 8)),
                time_spec((8, CHUNK)),
                slot_spec((OWN_SSM, STATE)),
                slot_spec((OWN_SSM, STATE)),
                slot_spec((OWN_SSM, 1)),
                time_spec((CHUNK, OWN_SSM)),
                pl.BlockSpec((8, OWN_SSM), lambda k, t, where: (0, 0)),
            ],
            out_specs=[
                time_spec((CHUNK, OWN_SSM)),
                time_spec((CHUNK, OWN_SSM)),
                time_spec((8, CHUNK)),
            ],
            scratch_shapes=[pltpu.VMEM((CHUNK, OWN_SSM), f32)],
        ),
        out_shape=[
            jax.ShapeDtypeStruct((chunks, CHUNK, OWN_SSM), f32),
            jax.ShapeDtypeStruct((chunks, CHUNK, OWN_SSM), bf16),
            jax.ShapeDtypeStruct((chunks, 8, CHUNK), f32),
        ],
        compiler_params=pltpu.CompilerParams(vmem_limit_bytes=VMEM),
        cost_estimate=lasting(16),
        name="ssm_forward",
    )(where, xs, bc, bc, bc, bc, bc, bc, bc, bc, meta, row, marks, segs, state, first, p0, gating, skip)


def attention_mask(where, seg_q, seg_k):
    m = pl.program_id(1)
    same = seg_q[...].reshape(HALF, 8)[:, 0:1] == seg_k[0, 0:1, :]
    row = lax.broadcasted_iota(jnp.int32, (HALF, HALF), 0)
    place = lax.rem(row + where[2] * CHUNK, HALF)
    key = lax.broadcasted_iota(jnp.int32, (HALF, HALF), 1)
    return same & ((place >= key) | (m < where[1]))


def slot_keyval(where, own, other):
    mine = pl.program_id(0) // 2 == where[2]
    return jnp.where(mine, own[0, 0], other[0, 0])


def attend_kernel(where, query, kv_own, kv_other, seg_q, seg_k, out, low_out, sum_out, best, total, acc):
    m = pl.program_id(1)
    scale = 1.0 / math.sqrt(ATT_HEAD)

    @pl.when(m == 0)
    def _():
        best[...] = jnp.full_like(best, NEG_BIG)
        total[...] = jnp.zeros_like(total)
        acc[...] = jnp.zeros_like(acc)

    @pl.when(m <= where[1])
    def _():
        q = query[...].reshape(HALF, ATT_HEAD)
        keyval = slot_keyval(where, kv_own, kv_other)
        keys, vals = keyval[:, :ATT_HEAD], keyval[:, ATT_HEAD:]
        scores = jnp.where(attention_mask(where, seg_q, seg_k), dot_cols(q, keys) * scale, NEG_BIG)
        before = best[:, 0:1]
        now = jnp.maximum(before, jnp.max(scores, axis=1, keepdims=True))
        shrink = jnp.exp(before - now)
        weights = jnp.where(scores > 0.5 * NEG_BIG, jnp.exp(scores - now), 0.0)
        total[...] = total[...] * shrink + jnp.sum(weights, axis=1, keepdims=True)
        acc[...] = acc[...] * shrink + dot(weights.astype(bf16), vals)
        best[...] = jnp.broadcast_to(now, best.shape)

    @pl.when(m == pl.num_programs(1) - 1)
    def _():
        context = (acc[...] / total[...]).reshape(2, 1, CHUNK, ATT_HEAD)
        out[...] = context
        low_out[...] = context.astype(bf16)
        sum_out[0] = (best[...] + jnp.log(total[...]))[:, 0:8]


def pair_spec(width):
    return pl.BlockSpec((2, 1, CHUNK, width), lambda k, m, where: (0, k, 0, 0))


def attend(where, query, kv_own, kv_other, seg_q, seg_k):
    slots = kv_own.shape[0]
    keyval_spec = pl.BlockSpec((1, 1, HALF, 2 * ATT_HEAD), lambda k, m, where: (m, k % 2, 0, 0))
    return pl.pallas_call(
        attend_kernel,
        grid_spec=pltpu.PrefetchScalarGridSpec(
            num_scalar_prefetch=1,
            grid=(ROWS, slots),
            in_specs=[
                pair_spec(ATT_HEAD),
                keyval_spec,
                keyval_spec,
                pair_spec(8),
                pl.BlockSpec((1, 8, HALF), lambda k, m, where: (k * slots + m, 0, 0)),
            ],
            out_specs=[
                pair_spec(ATT_HEAD),
                pair_spec(ATT_HEAD),
                pl.BlockSpec((1, HALF, 8), lambda k, m, where: (k, 0, 0)),
            ],
            scratch_shapes=[pltpu.VMEM((HALF, ATT_HEAD), f32)] * 3,
        ),
        out_shape=[
            jax.ShapeDtypeStruct(query.shape, f32),
            jax.ShapeDtypeStruct(query.shape, bf16),
            jax.ShapeDtypeStruct((ROWS, HALF, 8), f32),
        ],
        compiler_params=pltpu.CompilerParams(vmem_limit_bytes=VMEM),
        cost_estimate=lasting(10),
        name="attend",
    )(where, query, kv_own, kv_other, seg_q, seg_k)


def attend_back_kernel(where, query, kv_own, kv_other, seg_q, seg_k, grad, context, sums, query_out, keyval_out):
    m = pl.program_id(1)
    scale = 1.0 / math.sqrt(ATT_HEAD)
    used = m <= where[1]

    @pl.when(m == 0)
    def _():
        query_out[...] = jnp.zeros_like(query_out)

    @pl.when(jnp.logical_not(used))
    def _():
        keyval_out[...] = jnp.zeros_like(keyval_out)

    @pl.when(used)
    def _():
        q = query[...].reshape(HALF, ATT_HEAD)
        g = grad[...].reshape(HALF, ATT_HEAD)
        keyval = slot_keyval(where, kv_own, kv_other)
        keys, vals = keyval[:, :ATT_HEAD], keyval[:, ATT_HEAD:]
        delta = jnp.sum(
            g.astype(f32) * context[...].reshape(HALF, ATT_HEAD), axis=1, keepdims=True
        )
        spread = dot_cols(q, keys) * scale - sums[0, :, 0:1]
        prob = jnp.exp(jnp.where(attention_mask(where, seg_q, seg_k), spread, NEG_BIG))
        slope = (prob * (dot_cols(g, vals) - delta)).astype(bf16)
        part = (dot(slope, keys) * scale).reshape(2, 1, CHUNK, ATT_HEAD)
        query_out[...] = query_out[...] + part
        keyval_out[0, 0, :, :ATT_HEAD] = (dot_rows(slope, q) * scale).astype(bf16)
        keyval_out[0, 0, :, ATT_HEAD:] = dot_rows(prob.astype(bf16), g).astype(bf16)


def attend_back(where, query, kv_own, kv_other, seg_q, seg_k, grad, context, sums):
    slots = kv_own.shape[0]
    keyval_spec = pl.BlockSpec((1, 1, HALF, 2 * ATT_HEAD), lambda k, m, where: (m, k % 2, 0, 0))
    grad_spec = pl.BlockSpec((1, 1, HALF, 2 * ATT_HEAD), lambda k, m, where: (m, k, 0, 0))
    return pl.pallas_call(
        attend_back_kernel,
        grid_spec=pltpu.PrefetchScalarGridSpec(
            num_scalar_prefetch=1,
            grid=(ROWS, slots),
            in_specs=[
                pair_spec(ATT_HEAD),
                keyval_spec,
                keyval_spec,
                pair_spec(8),
                pl.BlockSpec((1, 8, HALF), lambda k, m, where: (k * slots + m, 0, 0)),
                pair_spec(ATT_HEAD),
                pair_spec(ATT_HEAD),
                pl.BlockSpec((1, HALF, 8), lambda k, m, where: (k, 0, 0)),
            ],
            out_specs=[pair_spec(ATT_HEAD), grad_spec],
        ),
        out_shape=[
            jax.ShapeDtypeStruct(query.shape, f32),
            jax.ShapeDtypeStruct((slots, ROWS, HALF, 2 * ATT_HEAD), bf16),
        ],
        compiler_params=pltpu.CompilerParams(vmem_limit_bytes=VMEM),
        cost_estimate=lasting(14),
        name="attend_back",
    )(where, query, kv_own, kv_other, seg_q, seg_k, grad, context, sums)


def gate_back_kernel(
    where, es, scale, gating, ssm_out, c0, c1, c2, c3, meta, marks, p0,
    gy_out, gating_out, later_out, both_out,
):
    gate = gating[0]
    sig = sigmoid_of(gate)
    act = gate * sig
    out = ssm_out[0]
    norm = scale[0, :, 0:1]
    unit = out * act * norm
    grad = norm * (es[0] - unit * scale[0, :, 1:2])
    gy = (grad * act).astype(bf16)
    gy_out[0] = gy
    gating_out[0] = (grad * out * (sig * (1.0 + gate * (1.0 - sig)))).astype(bf16)
    entry = widen(jnp.exp(meta[0, :, 8:16]) * marks[0, :, 1:2])
    across = (gy.astype(f32) * entry).astype(bf16)
    local = dot_rows(across, joined((c0, c1, c2, c3), core_of(where, True)))

    @pl.when(pl.program_id(1) == 0)
    def _():
        later_out[0] = local

    @pl.when(pl.program_id(1) == 1)
    def _():
        both_out[0] = p0[0] * later_out[0] + local


def gate_back(where, es, scale, gating, ssm_out, bc, meta, marks, p0):
    chunks = gating.shape[0]
    wide = time_spec((CHUNK, OWN_SSM), True)
    state = jax.ShapeDtypeStruct((ROWS, OWN_SSM, STATE), f32)
    token = jax.ShapeDtypeStruct((chunks, CHUNK, OWN_SSM), bf16)
    return pl.pallas_call(
        gate_back_kernel,
        grid_spec=pltpu.PrefetchScalarGridSpec(
            num_scalar_prefetch=1,
            grid=(ROWS, 2),
            in_specs=[wide, time_spec((CHUNK, 8), True), wide, wide]
            + piece_specs(1)
            + [
                time_spec((CHUNK, 32), True),
                time_spec((CHUNK, 8), True),
                slot_spec((OWN_SSM, 1)),
            ],
            out_specs=[wide, wide, slot_spec((OWN_SSM, STATE)), slot_spec((OWN_SSM, STATE))],
        ),
        out_shape=[token, token, state, state],
        compiler_params=pltpu.CompilerParams(vmem_limit_bytes=VMEM),
        cost_estimate=lasting(11),
        name="gate_back",
    )(where, es, scale, gating, ssm_out, bc, bc, bc, bc, meta, marks, p0)


def ssm_back_kernel(
    where, xs, gy, b0, b1, b2, b3, c0, c1, c2, c3, meta, row, marks, segs, state, first, flow, later,
    p0, p1, skip, head,
    xs_out, o00, o01, o02, o03, o10, o11, o12, o13, step_out, sums_out, work,
):
    early = pl.program_id(1) == 1
    core = core_of(where, True)
    b_mat, c_mat = joined((b0, b1, b2, b3), core), joined((c0, c1, c2, c3), core)
    inner = dot_cols(b_mat, c_mat)
    allowed = (marks[0, :, 0:1] == segs[0, 0:1, :]) & tri(False)
    xs_f = xs[0].astype(f32)
    gy_low = gy[0]
    gy_f = gy_low.astype(f32)
    step, cum, tail_decay, tail = tails_of(meta, marks)
    step_wide, tail_wide = widen(step), widen(tail)
    entry = widen(jnp.exp(cum) * marks[0, :, 1:2])
    stepped = (xs_f * step_wide).astype(bf16)
    grad_inner = jnp.zeros((CHUNK, CHUNK), f32)
    read = jnp.zeros((CHUNK, 8), f32)
    reads = jnp.zeros((8, CHUNK), f32)
    lane = lax.broadcasted_iota(jnp.int32, (CHUNK, 8), 1)
    sublane = lax.broadcasted_iota(jnp.int32, (8, CHUNK), 0)
    for h in range(OWN_HEADS):
        at = slice(h * SSM_HEAD, (h + 1) * SSM_HEAD)
        spread = row[0, 8 + h : 9 + h, :] - meta[0, :, 8 + h : 9 + h]
        decay = jnp.exp(jnp.where(allowed, spread, NEG_BIG))
        slope = decay * dot_cols(stepped[:, at], gy_low[:, at])
        grad_inner = grad_inner + slope
        flow_low = (slope * inner).astype(bf16)
        read = read + dot(flow_low, (lane == h).astype(bf16))
        reads = reads + dot((sublane == h).astype(bf16), flow_low)
        work[:, at] = dot((inner * decay).astype(bf16), gy_low[:, at])
    reads = jnp.concatenate([reads, jnp.zeros((120, CHUNK), f32)], axis=0).T
    flows = reads[:, :8] - read
    from_mix = work[...]
    entering = jnp.where(early, state[0], p0[0] * state[0] + first[0])
    leaving = jnp.where(early, p1[0] * flow[0] + later[0], flow[0])
    leaving_low = leaving.astype(bf16)
    inner_low = grad_inner.astype(bf16)
    across = (gy_f * entry).astype(bf16)
    weighted = (xs_f * tail_wide).astype(bf16)
    grad_b = dot(inner_low, c_mat) + dot(weighted, leaving_low)
    grad_c = dot_rows(inner_low, b_mat) + dot(across, entering.astype(bf16))
    from_state = dot_cols(b_mat, leaving_low)
    skip_row = skip[0:1, :]
    xs_out[0] = skip_row * gy_f + step_wide * from_mix + tail_wide * from_state
    low_first = where[0] < 2
    lower = jnp.where(low_first, grad_b, grad_c).astype(bf16)
    upper = jnp.where(low_first, grad_c, grad_b).astype(bf16)
    for ref, value, i in (
        (o00, lower, 0), (o10, lower, 1), (o01, lower, 2), (o11, lower, 3),
        (o02, upper, 0), (o12, upper, 1), (o03, upper, 2), (o13, upper, 3),
    ):
        for half in range(2):

            @pl.when(core ^ (i % 2) == half)
            def _():
                ref[0, :, half * PIECE : (half + 1) * PIECE] = value[:, i * PIECE : (i + 1) * PIECE]

    entering_low = entering.astype(bf16)
    entry_sum = narrow(gy_f * (dot_cols(c_mat, entering_low) * entry))
    step_sum = narrow(xs_f * from_mix)
    tail_sum = narrow(xs_f * from_state)
    skip_sum = narrow(gy_f * xs_f)
    tail_flow = tail_sum * tail
    passed = jnp.sum(leaving * entering, axis=1, keepdims=True)
    passed = jnp.broadcast_to(passed, (OWN_SSM, 8))
    own_head = head_map(OWN_SSM, 8, 0).astype(f32)
    grad_pass = jnp.sum(passed * own_head, axis=0, keepdims=True)
    passing = jnp.exp(cum[CHUNK - 1 : CHUNK]) * marks[0, CHUNK - 1 : CHUNK, 1:2]
    end = grad_pass * passing + jnp.sum(tail_flow, axis=0, keepdims=True)
    last = lax.broadcasted_iota(jnp.int32, (CHUNK, 8), 0) == CHUNK - 1
    grad_cum = flows + entry_sum - tail_flow + jnp.where(last, end, 0.0)
    grad_rate = exact(tri(False), grad_cum)
    grad_step = step_sum + tail_sum * tail_decay + grad_rate * head[1:2, 0:8]
    raw = grad_step * meta[0, :, 16:24]
    step_out[0] = raw
    sums = [raw, grad_rate * step, skip_sum]
    sums_out[0] = jnp.concatenate(
        [jnp.sum(v, axis=0, keepdims=True) for v in sums] + [jnp.zeros((5, 8), f32)], axis=0
    )


def ssm_back(where, xs, gy, bc, meta, row, marks, segs, state, first, flow, later, p0, p1, skip, head):
    chunks = xs.shape[0]
    wide = time_spec((CHUNK, OWN_SSM), True)
    kept = slot_spec((OWN_SSM, STATE))
    column = slot_spec((OWN_SSM, 1))

    def owner(slot):
        return pl.BlockSpec((1, CHUNK, 2 * PIECE), lambda k, t, where: (k ^ slot, 0, 0))

    piece = jax.ShapeDtypeStruct((ROWS, CHUNK, 2 * PIECE), bf16)
    return pl.pallas_call(
        ssm_back_kernel,
        grid_spec=pltpu.PrefetchScalarGridSpec(
            num_scalar_prefetch=1,
            grid=(ROWS, 2),
            in_specs=[wide, wide]
            + piece_specs(0)
            + piece_specs(1)
            + [
                time_spec((CHUNK, 32), True),
                time_spec((16, CHUNK), True),
                time_spec((CHUNK, 8), True),
                time_spec((8, CHUNK), True),
                kept,
                kept,
                kept,
                kept,
                column,
                column,
                pl.BlockSpec((8, OWN_SSM), lambda k, t, where: (0, 0)),
                pl.BlockSpec((8, 128), lambda k, t, where: (0, 0)),
            ],
            out_specs=[wide]
            + [owner(m) for r in range(2) for m in range(ROWS)]
            + [time_spec((CHUNK, 8), True), time_spec((8, 8), True)],
            scratch_shapes=[pltpu.VMEM((CHUNK, OWN_SSM), f32)],
        ),
        out_shape=[jax.ShapeDtypeStruct((chunks, CHUNK, OWN_SSM), f32)]
        + [piece] * 8
        + [
            jax.ShapeDtypeStruct((chunks, CHUNK, 8), f32),
            jax.ShapeDtypeStruct((chunks, 8, 8), f32),
        ],
        compiler_params=pltpu.CompilerParams(vmem_limit_bytes=VMEM),
        cost_estimate=lasting(30),
        name="ssm_back",
    )(
        where, xs, gy, bc, bc, bc, bc, bc, bc, bc, bc, meta, row, marks, segs, state, first, flow,
        later, p0, p1, skip, head,
    )


def conv_back_kernel(grad_xs, grad_bc, step, slope, proj, halo, marks, returned, conv, out, sums_out, ext, back):
    ext[0:8, :] = halo[0]
    ext[8:, :] = proj[0].astype(bf16).astype(f32)
    rest = jnp.zeros((CHUNK, LANES_A - OWN_CONV), f32)
    both = grad_bc[0]
    own_bc = jnp.where(pl.program_id(0) < ROWS, both[:, :PIECE], both[:, PIECE:])
    grad = jnp.concatenate([grad_xs[0], own_bc, rest], axis=1) * slope[0]
    sums = []
    back[...] = jnp.zeros_like(back)
    back[CHUNK : CHUNK + 8, :] = returned[0]
    for o in range(CONV):
        masked = grad if o == CONV - 1 else grad * marks[0, :, 3 + o : 4 + o]
        sums.append(jnp.sum(masked * ext[5 + o : 5 + o + CHUNK, :], axis=0, keepdims=True))
        back[5 + o : 5 + o + CHUNK, :] = (
            back[5 + o : 5 + o + CHUNK, :] + masked * conv[o : o + 1, :]
        )
    sums.append(jnp.sum(grad, axis=0, keepdims=True))
    sums_out[0] = jnp.concatenate(sums + [jnp.zeros((3, LANES_A), f32)], axis=0)
    mixed = back[8 : 8 + CHUNK, :]
    out[0] = mixed.astype(bf16)
    out[0, :, STEP_AT : STEP_AT + 8] = step[0].astype(bf16)


def conv_backward(grad_xs, grad_bc, step, slope, proj, halo, marks, returned, conv):
    chunks = proj.shape[0]
    block = lambda *shape: pl.BlockSpec((1,) + shape, lambda q: (q, 0, 0))
    return pl.pallas_call(
        conv_back_kernel,
        grid=(chunks,),
        in_specs=[
            block(CHUNK, OWN_SSM),
            pl.BlockSpec((1, CHUNK, 2 * PIECE), lambda q: (lax.rem(q, ROWS), 0, 0)),
            block(CHUNK, 8),
            block(CHUNK, LANES_A),
            block(CHUNK, LANES_A),
            block(8, LANES_A),
            block(CHUNK, 8),
            block(8, LANES_A),
            pl.BlockSpec((8, LANES_A), lambda q: (0, 0)),
        ],
        out_specs=[block(CHUNK, LANES_A), block(8, LANES_A)],
        out_shape=[
            jax.ShapeDtypeStruct((chunks, CHUNK, LANES_A), bf16),
            jax.ShapeDtypeStruct((chunks, 8, LANES_A), f32),
        ],
        scratch_shapes=[pltpu.VMEM((8 + CHUNK, LANES_A), f32)] * 2,
        compiler_params=pltpu.CompilerParams(vmem_limit_bytes=VMEM),
        cost_estimate=lasting(6),
        name="conv_backward",
    )(grad_xs, grad_bc, step, slope, proj, halo, marks, returned, conv)


LARGE = VMEM


def fetch(pieces, held, arrived):
    starts = starts_of(pieces)
    copies = []
    for i, piece in enumerate(pieces):
        at = pl.ds(starts[i], piece.shape[0])
        copies.append(pltpu.make_async_copy(piece, held.at[at], arrived.at[i]))
        copies[-1].start()
    return copies, starts


def by_pair(copies, starts):
    for i in range(0, 8, 2):
        for j, copy in enumerate(copies):
            if i * CHUNK < starts[j + 1] <= (i + 2) * CHUNK:
                copy.wait()
        yield i, slice(i * CHUNK, (i + 2) * CHUNK)


def times_kernel(count, *refs):
    pieces, (weight, out, held, arrived) = refs[:count], refs[count:]
    for i, at in by_pair(*fetch(pieces, held, arrived)):
        out[i : i + 2] = dot(held[at, :], weight[...]).reshape(2, CHUNK, -1)


def times(pieces, weight):
    width, cols = weight.shape
    count = len(pieces)
    return pl.pallas_call(
        lambda *refs: times_kernel(count, *refs),
        in_specs=[ANY] * count + [IN_VMEM],
        out_specs=IN_VMEM,
        out_shape=jax.ShapeDtypeStruct((8, CHUNK, cols), f32),
        scratch_shapes=[pltpu.VMEM((8 * CHUNK, width), bf16), pltpu.SemaphoreType.DMA((count,))],
        compiler_params=pltpu.CompilerParams(vmem_limit_bytes=LARGE),
        cost_estimate=lasting(5 + cols / 80),
        name="times",
    )(*pieces, weight)


def mixer_back_kernel(count, *refs):
    pieces = refs[:count]
    w_out, w_ctx, ssm_out, gating, es_out, context_out, sum_out, held, arrived = refs[count:]
    for i, at in by_pair(*fetch(pieces, held, arrived)):
        es = dot_cols(held[at, :], w_out[...]).reshape(2, CHUNK, OWN_SSM)
        es_out[i : i + 2] = es
        context = dot_cols(held[at, :], w_ctx[...]).astype(bf16)
        context_out[i : i + 2] = context.reshape(2, CHUNK, ATT_HEAD)
        for j in range(2):
            gate = gating[i + j]
            sum_out[i + j] = row_sums(es[j] * ssm_out[i + j] * gate * sigmoid_of(gate))


def mixer_back(pieces, w_out, w_ctx, ssm_out, gating):
    count, width = len(pieces), w_out.shape[1]
    return pl.pallas_call(
        lambda *refs: mixer_back_kernel(count, *refs),
        in_specs=[ANY] * count + [IN_VMEM] * 4,
        out_specs=[IN_VMEM] * 3,
        out_shape=[
            jax.ShapeDtypeStruct((8, CHUNK, OWN_SSM), f32),
            jax.ShapeDtypeStruct((8, CHUNK, ATT_HEAD), bf16),
            jax.ShapeDtypeStruct((8, 8, CHUNK), f32),
        ],
        scratch_shapes=[pltpu.VMEM((8 * CHUNK, width), bf16), pltpu.SemaphoreType.DMA((count,))],
        compiler_params=pltpu.CompilerParams(vmem_limit_bytes=LARGE),
        cost_estimate=lasting(13),
        name="mixer_back",
    )(*pieces, w_out, w_ctx, ssm_out, gating)


def weight_grad_kernel(*refs):
    left, pieces, out = refs[0], refs[1:-1], refs[-1]
    starts = starts_of(pieces)
    total = dot(left[:, : starts[1]], pieces[0][...])
    for i in range(1, len(pieces)):
        total = total + dot(left[:, starts[i] : starts[i + 1]], pieces[i][...])
    out[...] = total.astype(bf16).reshape(out.shape)


def weight_grad(left, pieces, by_part=0):
    cols, rows = left.shape
    width = pieces[0].shape[1]
    parts = by_part or 4
    part = width // parts
    if by_part:
        out_spec = pl.BlockSpec((1, cols, part), lambda i: (i, 0, 0))
        out_shape = jax.ShapeDtypeStruct((parts, cols, part), bf16)
    else:
        out_spec = pl.BlockSpec((cols, part), lambda i: (0, i))
        out_shape = jax.ShapeDtypeStruct((cols, width), bf16)
    return pl.pallas_call(
        weight_grad_kernel,
        grid=(parts,),
        in_specs=[pl.BlockSpec((cols, rows), lambda i: (0, 0))]
        + [pl.BlockSpec((piece.shape[0], part), lambda i: (0, i)) for piece in pieces],
        out_specs=out_spec,
        out_shape=out_shape,
        compiler_params=pltpu.CompilerParams(vmem_limit_bytes=LARGE),
        cost_estimate=lasting(4 + cols / 100),
        name="weight_grad",
    )(left, *pieces)


def terms_kernel(count, turned, adds, scaled_by, far, *refs):
    lefts, weights = refs[:count], refs[count : 2 * count]
    rest = refs[2 * count :]
    norm = rest[0] if scaled_by else None
    got = rest[int(scaled_by) : int(scaled_by) + adds]
    outs = rest[int(scaled_by) + adds :]
    half = outs[0].shape[0]
    rows = 2 * half if far and adds else half
    for k in range(1 if far else ROWS - 1):
        at = slice(k * rows, (k + 1) * rows)
        total = None
        for i in range(count):
            product = (dot_cols if turned else dot)(lefts[i][at, :], weights[i][...])
            if i == 0 and scaled_by:
                product = product * norm[at, 0:1]
            total = product if total is None else total + product
        if adds:
            total = total + got[k][...].astype(f32)
        if adds and far:
            outs[0][...] = total[:half].astype(bf16)
            outs[1][...] = total[half:].astype(bf16)
        else:
            outs[k][...] = total.astype(outs[k].dtype)


def group_terms(lefts, weights, turned, core, far, got=(), norm=None):
    width = weights[0].shape[0 if turned else 1]
    rows = lefts[0].shape[0] // 8
    block = min(width, 512)
    if far:
        row_spec = lambda cols: pl.BlockSpec((rows, cols), lambda i: (core * ROWS + ROWS - 1, 0))
    else:
        row_spec = lambda cols: pl.BlockSpec((ROWS * rows, cols), lambda i: (core, 0))
    in_specs = [row_spec(left.shape[1]) for left in lefts]
    for weight in weights:
        if turned:
            in_specs.append(pl.BlockSpec((block, weight.shape[1]), lambda i: (i, 0)))
        else:
            in_specs.append(pl.BlockSpec((weight.shape[0], block), lambda i: (0, i)))
    operands = list(lefts) + list(weights)
    if norm is not None:
        in_specs.append(row_spec(8))
        operands.append(norm)
    piece = pl.BlockSpec((rows, block), lambda i: (0, i))
    in_specs += [piece] * len(got)
    if got:
        kinds = [(rows // 2, bf16)] * 2 if far else [(rows, f32)] * 3
    else:
        kinds = [(rows, bf16)] * (1 if far else 3)
    depth = sum(left.shape[1] for left in lefts)
    return pl.pallas_call(
        lambda *refs: terms_kernel(len(lefts), turned, len(got), norm is not None, far, *refs),
        grid=(width // block,),
        in_specs=in_specs,
        out_specs=[pl.BlockSpec((n, block), lambda i: (0, i)) for n, _ in kinds],
        out_shape=[jax.ShapeDtypeStruct((n, width), kind) for n, kind in kinds],
        compiler_params=pltpu.CompilerParams(vmem_limit_bytes=LARGE),
        cost_estimate=lasting(4 + depth / 180),
        name="group_terms",
    )(*operands, *got)


def spread(for_x, for_y, to_x, to_y):
    by_x, by_y = fold(for_x, for_y, to_x, to_y)
    return by_x, hop(by_x, 1), hop(by_y, 2)


def scatter_product(lefts, weights, turned=False, norm=None, give=False, meanwhile=None, beside=None):
    far_got = [twin(part) for part in group_terms(lefts, weights, turned, 1, True, norm=norm)]
    near_got = [twin(part) for part in group_terms(lefts, weights, turned, 1, False, norm=norm)]
    if beside is not None:
        near_got, beside = lax.optimization_barrier((near_got, beside))
    far_a, far_b = group_terms(lefts, weights, turned, 0, True, got=far_got, norm=norm)
    own, for_x, for_y = group_terms(lefts, weights, turned, 0, False, got=near_got, norm=norm)
    to_x, to_y = hop(far_a, 2), hop(far_b, 1)
    done = None
    if meanwhile is not None:
        done = meanwhile(own)
        to_x, to_y, done = lax.optimization_barrier((to_x, to_y, done))
    by_x, by_y = fold(for_x, for_y, to_x, to_y)
    sums = own, hop(by_x, 1), hop(by_y, 2)
    return (sums, done, beside, by_x) if give else sums


def fold_kernel(for_x, for_y, to_x, to_y, by_x, by_y):
    half = to_x.shape[0]
    by_x[:half, :] = (for_x[:half, :] + to_x[...].astype(f32)).astype(bf16)
    by_x[half:, :] = for_x[half:, :].astype(bf16)
    by_y[:half, :] = for_y[:half, :].astype(bf16)
    by_y[half:, :] = (for_y[half:, :] + to_y[...].astype(f32)).astype(bf16)


def fold(for_x, for_y, to_x, to_y):
    rows, width = for_x.shape
    block = min(width, 1024)
    spec = lambda n: pl.BlockSpec((n, block), lambda i: (0, i))
    return pl.pallas_call(
        fold_kernel,
        grid=(width // block,),
        in_specs=[spec(rows), spec(rows), spec(rows // 2), spec(rows // 2)],
        out_specs=[spec(rows), spec(rows)],
        out_shape=[jax.ShapeDtypeStruct((rows, width), bf16)] * 2,
        compiler_params=pltpu.CompilerParams(vmem_limit_bytes=VMEM),
        cost_estimate=lasting(2),
        name="fold",
    )(for_x, for_y, to_x, to_y)


def regroup(values, outer, part):
    count = values.shape[1] // part
    if count == 1:
        return values
    inner = count // outer
    order = [o * inner + i for i in range(inner) for o in range(outer)]
    return jnp.concatenate([values[:, k * part : (k + 1) * part] for k in order], axis=1)


def scaled_unit(values):
    scale = lax.rsqrt(jnp.mean(values * values, axis=1, keepdims=True) + EPSILON)
    return values * scale, scale


def norm_in_kernel(part, x, out):
    unit, _ = scaled_unit(x[...].astype(f32))
    out[...] = regroup(unit, ROWS, part).astype(bf16)


def norm_two_kernel(part, x, own, by_x, by_y, hidden_out, out):
    hidden = x[...].astype(f32) + own[...] + by_x[...].astype(f32) + by_y[...].astype(f32)
    hidden_out[...] = hidden
    unit, _ = scaled_unit(hidden)
    out[...] = regroup(unit, ROWS, part).astype(bf16)


def norm_back_kernel(part, values, own, by_x, by_y, base, *outs):
    unit, scale = scaled_unit(values[...].astype(f32))
    grad = own[...] + by_x[...].astype(f32) + by_y[...].astype(f32)
    grad = regroup(grad, grad.shape[1] // part // ROWS, part)
    mean = jnp.mean(grad * unit, axis=1, keepdims=True)
    total = base[...].astype(f32) + scale * (grad - unit * mean)
    for out in outs:
        out[...] = total.astype(out.dtype)


def on_rows(kernel, part, operands, kinds, name):
    rows, width = operands[0].shape
    step = rows // 2
    spec = pl.BlockSpec((step, width), lambda i: (i, 0))
    return pl.pallas_call(
        lambda *refs: kernel(part, *refs),
        grid=(2,),
        in_specs=[spec] * len(operands),
        out_specs=[spec] * len(kinds),
        out_shape=[jax.ShapeDtypeStruct((rows, width), kind) for kind in kinds],
        compiler_params=pltpu.CompilerParams(vmem_limit_bytes=VMEM),
        cost_estimate=lasting(4),
        name=name,
    )(*operands)


def turn(values, cosine, sine):
    return values * cosine + pltpu.roll(values, ATT_HEAD // 2, 1) * sine


def rope_kernel(where, query, key, value, cosine, sine, query_out, keyval_out):
    query_out[0, 0] = turn(query[0], cosine[0], sine[0]).astype(bf16)
    keyval_out[0, 0, :, :ATT_HEAD] = turn(key[0], cosine[0], sine[0]).astype(bf16)
    keyval_out[0, 0, :, ATT_HEAD:] = value[0].astype(bf16)


def rope_forward(where, proj, cosine, sine):
    def part(i):
        return pl.BlockSpec(
            (1, CHUNK, ATT_HEAD), lambda k, t, where: ((t ^ where[2]) * ROWS + k, 0, 4 + i)
        )

    angle = pl.BlockSpec((1, CHUNK, ATT_HEAD), lambda k, t, where: (t ^ where[2], 0, 0))
    return pl.pallas_call(
        rope_kernel,
        grid_spec=pltpu.PrefetchScalarGridSpec(
            num_scalar_prefetch=1,
            grid=(ROWS, 2),
            in_specs=[part(0), part(1), part(2), angle, angle],
            out_specs=[
                pl.BlockSpec((1, 1, CHUNK, ATT_HEAD), lambda k, t, where: (t ^ where[2], k, 0, 0)),
                pl.BlockSpec((1, 1, CHUNK, 2 * ATT_HEAD), lambda k, t, where: (k, t, 0, 0)),
            ],
        ),
        out_shape=[
            jax.ShapeDtypeStruct((2, ROWS, CHUNK, ATT_HEAD), bf16),
            jax.ShapeDtypeStruct((ROWS, 2, CHUNK, 2 * ATT_HEAD), bf16),
        ],
        compiler_params=pltpu.CompilerParams(vmem_limit_bytes=VMEM),
        cost_estimate=lasting(3),
        name="rope_forward",
    )(where, proj, proj, proj, cosine, sine)


def rope_back_kernel(where, query, keyval, cosine, sine, out):
    core, turned = cosine[0], -sine[0]
    out[0, :, :ATT_HEAD] = turn(query[0, 0], core, turned).astype(bf16)
    mine = pl.program_id(0) // 2 == where[2]
    both = jnp.where(mine, keyval[0, 0], 0.0)
    out[0, :, ATT_HEAD : 2 * ATT_HEAD] = turn(both[:, :ATT_HEAD], core, turned).astype(bf16)
    out[0, :, 2 * ATT_HEAD :] = both[:, ATT_HEAD:].astype(bf16)


def rope_back(where, query, keyval, cosine, sine):
    angle = pl.BlockSpec((1, CHUNK, ATT_HEAD), lambda k, t, where: (t ^ where[2], 0, 0))
    return pl.pallas_call(
        rope_back_kernel,
        grid_spec=pltpu.PrefetchScalarGridSpec(
            num_scalar_prefetch=1,
            grid=(ROWS, 2),
            in_specs=[
                pl.BlockSpec((1, 1, CHUNK, ATT_HEAD), lambda k, t, where: (t ^ where[2], k, 0, 0)),
                pl.BlockSpec((1, 1, CHUNK, 2 * ATT_HEAD), lambda k, t, where: (k % 2, t, 0, 0)),
                angle,
                angle,
            ],
            out_specs=pl.BlockSpec(
                (1, CHUNK, 3 * ATT_HEAD), lambda k, t, where: ((t ^ where[2]) * ROWS + k, 0, 0)
            ),
        ),
        out_shape=jax.ShapeDtypeStruct((2 * ROWS, CHUNK, 3 * ATT_HEAD), bf16),
        compiler_params=pltpu.CompilerParams(vmem_limit_bytes=VMEM),
        cost_estimate=lasting(3),
        name="rope_back",
    )(where, query, keyval, cosine, sine)


def feed_kernel(count, *refs):
    n2, g = refs[:count], refs[count : 2 * count]
    w_gu, w_down, act_out, grad_out, held_n, held_g, arrived_n, arrived_g = refs[2 * count :]
    copies_n, starts = fetch(n2, held_n, arrived_n)
    copies_g, _ = fetch(g, held_g, arrived_g)
    own = w_down.shape[0]
    for (i, at), _ in zip(by_pair(copies_n, starts), by_pair(copies_g, starts)):
        both = dot(held_n[at, :], w_gu[...])
        gate, up = both[:, :own], both[:, own:]
        sig = sigmoid_of(gate)
        silu = gate * sig
        act_out[at, :] = (silu * up).astype(bf16)
        grad = dot_cols(held_g[at, :], w_down[...])
        grad_out[at, :own] = (grad * up * (sig * (1.0 + gate * (1.0 - sig)))).astype(bf16)
        grad_out[at, own:] = (grad * silu).astype(bf16)


def feed(n2, g, w_gu, w_down):
    own, width = w_down.shape
    count, rows = len(n2), 8 * CHUNK
    return pl.pallas_call(
        lambda *refs: feed_kernel(count, *refs),
        in_specs=[ANY] * (2 * count) + [IN_VMEM] * 2,
        out_specs=[IN_VMEM] * 2,
        out_shape=[
            jax.ShapeDtypeStruct((rows, own), bf16),
            jax.ShapeDtypeStruct((rows, 2 * own), bf16),
        ],
        scratch_shapes=[
            pltpu.VMEM((rows, width), bf16),
            pltpu.VMEM((rows, width), bf16),
            pltpu.SemaphoreType.DMA((count,)),
            pltpu.SemaphoreType.DMA((count,)),
        ],
        compiler_params=pltpu.CompilerParams(vmem_limit_bytes=LARGE),
        cost_estimate=lasting(23),
        name="feed",
    )(*n2, *g, w_gu, w_down)


def per_device(
    tokens,
    segments,
    cotangent,
    norm_gain,
    gating_weight,
    input_weight,
    state_weight,
    step_weight,
    conv_weight,
    conv_bias,
    step_bias,
    decay_log,
    skip_gain,
    ssm_gain,
    out_weight,
    query_weight,
    keyval_weight,
    context_weight,
    mlp_gain,
    gate_weight,
    up_weight,
    down_weight,
):
    zs = lax.axis_size("z")
    b = lax.axis_index("b")
    z = lax.axis_index("z")
    c = lax.axis_index("c")
    rank = 2 * b + c
    rows = tokens.shape[1]
    width = tokens.shape[2]
    share = norm_gain.shape[0]
    ssm_width = HEADS * SSM_HEAD
    score_scale = 1.0 / math.sqrt(ATT_HEAD)

    def to_z(values):
        return (
            values.reshape(rows, ROWS, zs, 2 * share).transpose(0, 2, 1, 3).reshape(rows, width)
        )

    def from_z(values):
        return (
            values.reshape(rows, zs, ROWS, 2 * share).transpose(0, 2, 1, 3).reshape(rows, width)
        )

    def swap(values):
        return jnp.where(c == 0, values, values[::-1])

    def to_ranks(values):
        return lax.all_to_all(values, ("b", "c"), split_axis=0, concat_axis=0, tiled=True)

    def to_owner(values):
        mine = lax.psum_scatter(values, "z", scatter_dimension=0, tiled=True)[0]
        return mine.T.reshape(RANKS, share, -1)

    def along_z(values):
        return lax.all_gather(values, "z", axis=0, tiled=True)

    def owner_z(values):
        return lax.psum_scatter(values, "z", scatter_dimension=0, tiled=True)

    x = tokens[0]
    cot = cotangent[0]
    aligned = 2 * share % 128 == 0
    block = 2 * share if aligned else width
    lined = (lambda v: v) if aligned else to_z
    unlined = (lambda v: v) if aligned else from_z
    gain_col = norm_gain.astype(f32)[:, None]
    gain2_col = mlp_gain.astype(f32)[:, None]
    ssm_gain_col = ssm_gain.astype(f32)[:, None]

    (n1_own,) = on_rows(norm_in_kernel, block, [x], [bf16], "norm_in")
    scaled = lambda w, gain: (w.astype(f32) * gain).astype(bf16)
    by_rank = lambda w: w.reshape(w.shape[0], RANKS, -1).transpose(1, 0, 2)
    group_kv = KVHEADS * ATT_HEAD
    kv_heads = keyval_weight.reshape(share, 2, KVHEADS, ATT_HEAD).transpose(2, 0, 1, 3)
    kv_rank = jnp.repeat(kv_heads.reshape(KVHEADS, share, 2 * ATT_HEAD), RANKS // KVHEADS, axis=0)
    pad_cols = 128 - OWN_STATE - 8
    chan = conv_bias.shape[0]
    small = jnp.concatenate(
        [segments[0].astype(bf16), conv_weight.reshape(-1), conv_bias.reshape(-1)]
    )
    small_count = small.shape[0]
    small = jnp.pad(small, (0, share * pad_cols - small_count)).reshape(share, pad_cols)
    w_a = jnp.concatenate(
        [
            by_rank(input_weight),
            by_rank(state_weight),
            by_rank(step_weight),
            jnp.zeros((RANKS, share, 8 - OWN_HEADS), bf16),
        ],
        axis=2,
    )
    riders = jnp.broadcast_to(small[None], (RANKS, share, pad_cols))
    w_b = jnp.concatenate([by_rank(query_weight), kv_rank], axis=2)
    w_c = by_rank(gating_weight)
    cols_a, cols_b, cols_c = w_a.shape[2] + pad_cols, w_b.shape[2], w_c.shape[2]
    own_ab = to_ranks(
        jnp.concatenate([scaled(w_a, gain_col[None]), riders, scaled(w_b, gain_col[None])], axis=2)
    )
    w_ab = along_z(own_ab)
    small = w_ab[..., cols_a - pad_cols : cols_a].reshape(zs, ROWS, 2, -1)[..., :small_count]
    w_ab = w_ab.reshape(width, cols_a + cols_b)
    wa, wb = w_ab[:, :cols_a], w_ab[:, cols_a:]
    def ff_ranks(w):
        return (
            w.reshape(w.shape[0], ROWS, zs, 2, -1)
            .transpose(1, 3, 0, 2, 4)
            .reshape(RANKS, w.shape[0], -1)
        )

    w_cgu = jnp.concatenate(
        [
            scaled(w_c, gain_col[None]),
            scaled(
                jnp.concatenate([ff_ranks(gate_weight), ff_ranks(up_weight)], axis=2),
                gain2_col[None],
            ),
        ],
        axis=2,
    )
    n1, w_cgu = gather_group(lined(n1_own), w_cgu)
    own_cgu = to_ranks(w_cgu)
    own_c, w_gu = own_cgu[..., :cols_c], own_cgu[..., cols_c:]
    own_ff = w_gu.shape[2] // 2

    row_out = out_weight.shape[0]
    row_ctx = context_weight.shape[0]
    w_oc = jnp.concatenate([scaled(out_weight, ssm_gain_col), context_weight], axis=0)[None]
    segs = small[..., :rows].transpose(1, 0, 2, 3).reshape(ROWS, zs * 2 * rows).astype(f32)
    segs_all = jnp.concatenate(
        [lax.dynamic_slice_in_dim(segs, k ^ b, 1, 0) for k in range(ROWS)], axis=0
    )
    conv_all = small[..., rows:].transpose(1, 0, 2, 3).reshape(-1, CONV + 1, chan).astype(f32)
    conv_all = conv_all.transpose(1, 0, 2).reshape(CONV + 1, -1)
    conv_own = jnp.concatenate(
        [
            lax.dynamic_slice_in_dim(conv_all, rank * OWN_SSM, OWN_SSM, 1),
            lax.dynamic_slice_in_dim(conv_all, ssm_width + rank * OWN_STATE, OWN_STATE, 1),
        ],
        axis=1,
    )
    seg_pad = jnp.concatenate([jnp.zeros((ROWS, rows), f32), segs_all], axis=1)
    seg_near = lax.dynamic_slice_in_dim(seg_pad, z * 2 * rows, 3 * rows, 1)
    seg_time = seg_near[:, rows:].reshape(ROWS, 2, rows).transpose(1, 0, 2)
    seg = swap(seg_time).reshape(2 * ROWS, rows)
    seg_before = seg_near[:, : 2 * rows].reshape(ROWS, 2, rows).transpose(1, 0, 2)
    seg_before = swap(seg_before).reshape(2 * ROWS, rows)
    marks = marks_of(seg, seg_before)
    seg_rows = jnp.broadcast_to(seg[:, None, :], (2 * ROWS, 8, rows))
    seg_query = marks.reshape(2, ROWS, rows, 8)
    seg_keys = segs_all.reshape(ROWS * zs, 1, 2 * rows)
    seg_keys = jnp.broadcast_to(seg_keys, (ROWS * zs, 8, 2 * rows))
    where = jnp.stack([b, z, c]).astype(jnp.int32)
    conv_own = jnp.pad(conv_own, ((0, 3), (0, LANES_A - OWN_CONV)))
    own_slice = lambda v: lax.dynamic_slice_in_dim(v.astype(f32), rank * OWN_HEADS, OWN_HEADS, 0)
    rate = -jnp.exp(own_slice(decay_log))
    head = jnp.pad(jnp.stack([own_slice(step_bias), rate]), ((0, 6), (0, 128 - OWN_HEADS)))
    skip_wide = jnp.broadcast_to(jnp.repeat(own_slice(skip_gain), SSM_HEAD)[None], (8, OWN_SSM))

    half_head = ATT_HEAD // 2
    frequency = jnp.exp(jnp.arange(half_head, dtype=f32) * (-2.0 * math.log(ROPE_BASE) / ATT_HEAD))
    core_place = (z * 2 + (jnp.arange(2) ^ c)) * rows
    places = (core_place[:, None] + jnp.arange(rows)[None, :]).astype(f32)
    angles = (places[:, :, None] * frequency).reshape(2, rows, half_head)
    cosine, sine = jnp.cos(angles), jnp.sin(angles)
    cosine = jnp.concatenate([cosine, cosine], axis=-1)
    sine = jnp.concatenate([-sine, sine], axis=-1)

    chunks = 2 * ROWS
    proj = times(n1, after(w_ab, own_cgu))
    g_all, proj = gather_group(after(cot, own_cgu), proj)
    query, keyval = rope_forward(where, proj, cosine, sine)
    own_kv = lax.dynamic_slice_in_dim(keyval, 2 * c, 2, 0).reshape(1, 2, 2 * rows, 2 * ATT_HEAD)
    kv_own = along_z(own_kv)

    def before_chunk(own_last, moved):
        return jnp.stack(
            [jnp.where(c == 0, moved, own_last[1]), jnp.where(c == 0, own_last[0], moved)]
        )

    tails = after(proj[:, rows - 8 :, :cols_a], where)
    tails = tails.reshape(2, ROWS, 8, cols_a).astype(bf16)
    last_core = jnp.where(c == 0, tails[1], tails[0])
    moved = zshift(last_core[:, 8 - CONV + 1 :], 1)
    moved = jnp.pad(moved, ((0, 0), (8 - CONV + 1, 0), (0, 0)))
    halo = before_chunk(tails, moved).reshape(chunks, 8, cols_a).astype(f32)
    xs, bc_own, slope, meta, meta_rows = conv_forward(proj, halo, marks, conv_own, head)
    mine = [bc_own] + [hop(bc_own, m) for m in range(1, ROWS)]
    mine = jnp.stack(mine)
    bc = jnp.concatenate([mine, twin(mine)], axis=0)
    wc = along_z(after(own_c, own_kv)).reshape(width, cols_c)

    passing = jnp.exp(meta[:, rows - 1, 8 : 8 + OWN_HEADS]) * marks[:, rows - 1, 1:2]
    pass_wide = swap(jnp.repeat(passing, SSM_HEAD, axis=1).reshape(2, ROWS, OWN_SSM, 1))
    p0, p1 = pass_wide[0], pass_wide[1]
    pass_both = p0 * p1
    first_local, both_local = local_states(where, xs, bc, meta, marks, p1)
    kv_other = twin(kv_own)
    state = jnp.zeros_like(both_local)
    for s in range(zs - 1):
        message = (pass_both * state + both_local).astype(bf16)
        if s == 1:
            query = after(query, message)
            context, context_low, logsum = attend(
                where, query, kv_own, kv_other, seg_query, seg_keys
            )
            gating = times(n1, after(wc, message))
        if s == zs - 2:
            w_oc = along_z(after(w_oc, message))
        moved = lax.ppermute(message, "z", [(s, s + 1)])
        if s == 0:
            moved, *g_all = lax.optimization_barrier((moved, *g_all))
        if s == 1:
            moved, context_low, gating = lax.optimization_barrier((moved, context_low, gating))
        state = state + moved.astype(f32)

    halves = w_oc.reshape(2, zs // 2, row_out + row_ctx, width)
    kept = lax.dynamic_index_in_dim(halves, c, 0, keepdims=False)
    sent = lax.dynamic_index_in_dim(halves, 1 - c, 0, keepdims=False)
    got = twin(sent)
    both = jnp.where(c == 0, jnp.stack([kept, got], 1), jnp.stack([got, kept], 1))
    w_out = both[:, :, :row_out].reshape(-1, width)
    w_ctx = both[:, :, row_out:].reshape(-1, width)
    w_gu_full = along_z(after(w_gu, state)).reshape(width, 2 * own_ff)
    w_down = along_z(after(down_weight, w_gu, state))

    ssm_out, gated_low, squares = ssm_forward(
        where, xs, bc, meta, meta_rows, marks, seg_rows, state, first_local, p0, gating, skip_wide
    )
    squares = sum_group(squares[:, 0].reshape(2, ROWS, rows))
    scale_ssm = lax.rsqrt(squares * (1.0 / ssm_width) + EPSILON).reshape(chunks, rows, 1)

    flat = lambda v: v.reshape(-1, v.shape[-1])
    norms = jnp.broadcast_to(scale_ssm.reshape(-1, 1), (chunks * rows, 8))
    mixed = scatter_product([flat(gated_low), flat(context_low)], [w_out, w_ctx], norm=norms)
    hidden, n2_own = on_rows(norm_two_kernel, block, [x, *mixed], [f32, bf16], "norm_two")

    n2 = gather_group(lined(n2_own))
    activation, grad_gu = feed(n2, g_all, w_gu_full, w_down)

    e2, grad_down_terms, _, folded = scatter_product(
        [grad_gu],
        [w_gu_full],
        turned=True,
        give=True,
        meanwhile=lambda own: weight_grad(after(activation, own).T, g_all),
    )
    grad_down = owner_z(grad_down_terms)
    grad_gu_terms = weight_grad(after(grad_gu, folded).T, n2, zs)
    *e2, grad_gu_terms = lax.optimization_barrier((*e2, grad_gu_terms))
    grad_gu_w = to_owner(grad_gu_terms)
    grad_hidden, grad_mix_own = on_rows(
        norm_back_kernel, block, [hidden, *map(unlined, e2), cot], [f32, bf16], "norm_back"
    )
    unit_low = (gated_low.astype(f32) * scale_ssm).astype(bf16)
    mixer_left = jnp.concatenate([flat(unit_low), flat(context_low)], axis=-1).T
    late = after(activation, grad_mix_own)
    late_other = [group_terms([late], [w_down], False, 1, far) for far in (True, False)]

    def late_sums(meanwhile):
        other, left = meanwhile
        far_got, near_got = [[twin(part) for part in parts] for parts in other]
        return (
            group_terms([late], [w_down], False, 0, True, got=far_got),
            group_terms([late], [w_down], False, 0, False, got=near_got),
            left,
        )

    grad_mix, ((far_a, far_b), (late_own, for_x, for_y), mixer_left) = gather_group(
        grad_mix_own, (late_other, mixer_left), late_sums
    )
    to_x, to_y = hop(far_a, 2), hop(far_b, 1)
    es, grad_context, es_sum = mixer_back(
        grad_mix, after(w_out, late_own, far_a, mixer_left), w_ctx, ssm_out, gating
    )
    grad_oc_w = weight_grad(after(mixer_left, es_sum), grad_mix)
    es_sum = es_sum[:, 0] * scale_ssm[..., 0]
    es_mean = sum_group(es_sum.reshape(2, ROWS, rows)) * (1.0 / ssm_width)
    scales = jnp.pad(
        jnp.stack([scale_ssm[..., 0], es_mean.reshape(chunks, rows)], axis=-1),
        ((0, 0), (0, 0), (0, 6)),
    )
    scales, to_x, to_y, grad_oc_w = lax.optimization_barrier((scales, to_x, to_y, grad_oc_w))
    gy, grad_gating, later_grad, both_grad = gate_back(
        where, es, scales, gating, ssm_out, bc, meta, marks, p0
    )

    def out_grads(grad_oc_w):
        grad_out_rows = grad_oc_w[:OWN_SSM].reshape(zs // 2, 2, row_out, width)
        grad_ctx_rows = grad_oc_w[OWN_SSM:].reshape(zs // 2, 2, row_ctx, width)
        grad_oc = jnp.concatenate([grad_out_rows, grad_ctx_rows], axis=2)
        oc_kept = lax.dynamic_index_in_dim(grad_oc, c, 1, keepdims=False)
        oc_got = twin(lax.dynamic_index_in_dim(grad_oc, 1 - c, 1, keepdims=False))
        return jnp.where(
            c == 0,
            jnp.concatenate([oc_kept, oc_got], axis=0),
            jnp.concatenate([oc_got, oc_kept], axis=0),
        )

    flowing = jnp.zeros_like(both_grad)
    grad_c_low = flat(grad_gating)
    for s in range(zs - 1, 0, -1):
        message = (pass_both * flowing + both_grad).astype(bf16)
        if s == 1:
            grad_context = after(grad_context, message).reshape(2, ROWS, rows, ATT_HEAD)
            grad_query, grad_kv = attend_back(
                where, query, kv_own, kv_other, seg_query, seg_keys, grad_context, context, logsum
            )
        moved = lax.ppermute(message, "z", [(s, s - 1)])
        if s == zs - 1:
            late_folded, late_x, late_y = spread(for_x, for_y, to_x, to_y)
            moved, late_folded = lax.optimization_barrier((moved, late_folded))
        if s == zs - 2:
            oc_all = out_grads(after(grad_oc_w, message))
            grad_wc_terms = weight_grad(after(grad_c_low, message).T, n1, zs)
            moved, grad_gu_w, grad_down, oc_all, grad_wc_terms = lax.optimization_barrier(
                (moved, grad_gu_w, grad_down, oc_all, grad_wc_terms)
            )
        if s == 1:
            moved, grad_query, grad_kv, late_x, late_y = lax.optimization_barrier(
                (moved, grad_query, grad_kv, late_x, late_y)
            )
        flowing = flowing + moved.astype(f32)
    grad_wc = to_owner(grad_wc_terms)

    kv_kept = lax.dynamic_slice_in_dim(grad_kv, 2 * c, 2, 1).astype(f32)
    kv_got = twin(lax.dynamic_slice_in_dim(grad_kv, 2 - 2 * c, 2, 1)).astype(f32)
    kv_terms = (kv_kept + kv_got).astype(bf16)
    kv_grad = owner_z(kv_terms)
    kv_grad = kv_grad[0].astype(f32)
    grad_b_low = rope_back(
        where, grad_query, kv_grad.reshape(2, 2, rows, 2 * ATT_HEAD), cosine, sine
    )
    grad_b_low = flat(grad_b_low)
    grad_wb_terms = weight_grad(grad_b_low.T, n1, zs)
    grad_wb = to_owner(grad_wb_terms)

    grad_xs, *bc_terms, grad_step, head_sums = ssm_back(
        where, xs, gy, bc, meta, meta_rows, marks, seg_rows, state, first_local, flowing, later_grad,
        p0, p1, skip_wide, head,
    )
    got = twin(jnp.stack(bc_terms[ROWS:])).astype(f32)
    bc_sums = [bc_terms[k].astype(f32) + got[k] for k in range(ROWS)]
    grad_bc = bc_sums[0]
    for k in range(1, ROWS):
        grad_bc = grad_bc + hop(bc_sums[k].astype(bf16), k).astype(f32)

    near = CONV - 1
    bc_near = grad_bc[:, :near].reshape(ROWS, near, 2, PIECE).transpose(2, 0, 1, 3)
    grad_near = jnp.concatenate(
        [grad_xs[:, :near], bc_near.reshape(chunks, near, PIECE)], axis=-1
    )
    grad_near = grad_near * slope[:, :near, :OWN_CONV]
    give = jnp.zeros((chunks, near, OWN_CONV), f32)
    for o in range(near):
        masked = grad_near[:, : near - o] * marks[:, : near - o, 3 + o : 4 + o]
        give = give + jnp.pad(masked * conv_own[o, :OWN_CONV], ((0, 0), (o, 0), (0, 0)))
    give = give.reshape(2, ROWS, near, OWN_CONV)
    moved = zshift(jnp.where(c == 0, give[0], give[1]).astype(bf16), -1).astype(f32)
    given = jnp.stack(
        [jnp.where(c == 0, give[1], moved), jnp.where(c == 0, moved, give[0])]
    ).reshape(chunks, near, OWN_CONV)
    got_gu = to_ranks(after(grad_gu_w, grad_xs))
    given, got_gu = lax.optimization_barrier((after(given, grad_wb_terms), got_gu))
    given = jnp.pad(given, ((0, 0), (8 - near, 0), (0, LANES_A - OWN_CONV)))
    grad_a_low, conv_sums = conv_backward(
        grad_xs, grad_bc, grad_step, slope, proj, halo, marks, given, conv_own
    )
    grad_a_low = flat(grad_a_low)
    conv_sums = jnp.sum(conv_sums, axis=0)[: CONV + 1, :OWN_CONV]
    head_sums = jnp.sum(head_sums, axis=0)[:3, :OWN_HEADS] * jnp.stack(
        [jnp.ones_like(rate), rate, jnp.ones_like(rate)]
    )
    head_sums = jnp.pad(head_sums.reshape(1, -1), ((0, 0), (0, OWN_CONV - 3 * OWN_HEADS)))

    def all_sums(sums):
        total = sums
        for flip in range(1, zs):
            total = total + zhop(sums, flip)
        table = jnp.stack([total, twin(total)])
        return jnp.concatenate([table] + [hop(table, flip) for flip in range(1, ROWS)], axis=0)

    grad_wa_terms = weight_grad(grad_a_low.T, n1, zs)
    grad_a_low = after(grad_a_low, grad_wa_terms)
    sums = jnp.concatenate([conv_sums, head_sums], axis=0)
    e1, table, _, e1_folded = scatter_product(
        [grad_c_low, grad_b_low, grad_a_low],
        [wc, wb, wa],
        turned=True,
        give=True,
        meanwhile=lambda own: all_sums(sums),
    )
    grad_wa = to_owner(grad_wa_terms)
    late_own = after(late_own, e1_folded)
    result = (hidden + late_own + late_x.astype(f32) + late_y.astype(f32)).astype(bf16)
    grad_oc_own = owner_z(after(oc_all, grad_wa_terms))[0].astype(f32)
    got = to_ranks(after(jnp.concatenate([grad_wa, grad_wb, grad_wc], axis=2), e1_folded))

    def unrank(values):
        return values.transpose(1, 0, 2).reshape(share, -1)

    def ff_unrank(values):
        return (
            values.reshape(ROWS, 2, share, zs, own_ff // zs)
            .transpose(2, 0, 3, 1, 4)
            .reshape(share, -1)
        )

    def gain_grad(pairs):
        return sum(jnp.sum(w.astype(f32) * d, axis=1) for w, d in pairs)

    got_gu = got_gu.astype(f32)
    d_gate, d_up = ff_unrank(got_gu[..., :own_ff]), ff_unrank(got_gu[..., own_ff:])
    d_out, d_ctx = grad_oc_own[:row_out], grad_oc_own[row_out:]
    ready = (
        gain_grad(((gate_weight, d_gate), (up_weight, d_up))),
        d_gate * gain2_col,
        d_up * gain2_col,
        grad_down.astype(f32),
        result,
    )
    *e1, got, ready = lax.optimization_barrier((*e1, got, ready))
    got_a, got_bc = got[..., :cols_a], got[..., cols_a:]
    d_mlp_gain, d_gate, d_up, d_down, result = ready
    d_ssm_gain = gain_grad(((out_weight, d_out),))
    (grad_x,) = on_rows(
        norm_back_kernel, block, [x, *map(unlined, e1), grad_hidden], [bf16], "norm_back_in"
    )

    got_bc = got_bc.astype(f32)
    got_b, got_c = got_bc[..., :cols_b], got_bc[..., cols_b:]
    d_query = unrank(got_b[..., :ATT_HEAD])
    d_kv = got_b[..., ATT_HEAD:].reshape(KVHEADS, RANKS // KVHEADS, share, 2, ATT_HEAD).sum(1)
    d_kv = d_kv.transpose(1, 2, 0, 3).reshape(share, 2 * group_kv)
    d_gating = unrank(got_c)
    gain_part = gain_grad(
        ((gating_weight, d_gating), (query_weight, d_query), (keyval_weight, d_kv))
    )
    ready = (gain_part, d_query * gain_col, d_kv * gain_col, d_gating * gain_col)
    gain_part, d_query, d_kv, d_gating = ready
    got_a = got_a.astype(f32)
    d_input = unrank(got_a[..., :OWN_SSM])
    d_state = unrank(got_a[..., OWN_SSM:OWN_CONV])
    d_step = unrank(got_a[..., OWN_CONV : OWN_CONV + OWN_HEADS])
    d_norm_gain = gain_part + gain_grad(
        ((input_weight, d_input), (state_weight, d_state), (step_weight, d_step))
    )

    place = jnp.arange(RANKS)
    chosen = ((place ^ rank)[:, None] == place[None, :]).astype(f32)
    table = jnp.einsum("rs,sof->rof", chosen, table, precision=HIGH)
    conv_ssm = table[:, : CONV + 1, :OWN_SSM].transpose(1, 0, 2).reshape(CONV + 1, -1)
    conv_state = table[:, : CONV + 1, OWN_SSM:].transpose(1, 0, 2).reshape(CONV + 1, -1)
    conv_full = jnp.concatenate([conv_ssm, conv_state], axis=1)
    conv_mine = lax.dynamic_slice_in_dim(conv_full, (rank // 2 * zs * 2 + z * 2 + c) * chan, chan, 1)
    heads = table[:, CONV + 1, : 3 * OWN_HEADS].reshape(RANKS, 3, OWN_HEADS)
    heads = heads.transpose(1, 0, 2).reshape(3, HEADS)

    return (
        result[None],
        grad_x[None],
        d_norm_gain,
        d_gating,
        d_input * gain_col,
        d_state * gain_col,
        d_step * gain_col,
        conv_mine[:CONV],
        conv_mine[CONV],
        heads[0],
        heads[1],
        heads[2],
        d_ssm_gain,
        d_out * ssm_gain_col,
        d_query,
        d_kv,
        d_ctx,
        d_mlp_gain,
        d_gate,
        d_up,
        d_down,
    )


def solution(mesh):
    places = mesh.devices.reshape(ROWS, mesh.shape["seq"] // 2, 2)
    split = Mesh(places, ("b", "z", "c"))
    everywhere = ("b", "z", "c")
    row = P(everywhere, None)
    vector = P(everywhere)
    token = P("b", ("z", "c"), None)
    return jax.shard_map(
        per_device,
        mesh=split,
        in_specs=(
            token,
            P("b", ("z", "c")),
            token,
            vector,
            row,
            row,
            row,
            row,
            P(None, everywhere),
            vector,
            P(),
            P(),
            P(),
            vector,
            row,
            row,
            row,
            row,
            vector,
            row,
            row,
            row,
        ),
        out_specs=(
            token,
            token,
            vector,
            row,
            row,
            row,
            row,
            P(None, everywhere),
            vector,
            P(),
            P(),
            P(),
            vector,
            row,
            row,
            row,
            row,
            vector,
            row,
            row,
            row,
        ),
        check_vma=False,
    )
```
